32 devices in a mesh: group: 4 (over x, core), dp: 2 (over y), mp: 4 (over z).
Axes of the slice: x: 2, y: 2, z: 4, core: 2. Of those that a mesh axis runs over, the one named last changes fastest.
Arguments:
- image_tokens: bfloat16 [4, 4, 1024, 1536], P('group', 'dp', None, 'mp'), may hold values from -6 to 6
- text_tokens: bfloat16 [4, 4, 154, 1536], P('group', 'dp', None, 'mp'), may hold values from -6 to 6
- image_modulation: float32 [4, 4, 6, 1536], P('group', 'dp', None, 'mp'), may hold values from -3 to 3
- text_modulation: float32 [4, 4, 6, 1536], P('group', 'dp', None, 'mp'), may hold values from -3 to 3
- image_cotan: bfloat16 [4, 4, 1024, 1536], P('group', 'dp', None, 'mp'), may hold values from -6 to 6
- text_cotan: bfloat16 [4, 4, 154, 1536], P('group', 'dp', None, 'mp'), may hold values from -6 to 6
- group_counts: int32 [4], P('group'), may hold values from 2 to 4, as said below
- global_qkv: float32 [2, 1536, 3, 1536], P(None, ('dp', 'group'), None, 'mp'), may hold values from -1 to 1, as said below
- global_output: float32 [2, 1536, 1536], P(None, ('mp', 'dp', 'group')), may hold values from -1 to 1, as said below
- global_expand: float32 [2, 1536, 6144], P(None, ('dp', 'group'), 'mp'), may hold values from -1 to 1, as said below
- global_reduce: float32 [2, 6144, 1536], P(None, ('mp', 'dp', 'group')), may hold values from -1 to 1, as said below
- global_textqkv: float32 [2, 1536, 3, 1536], P(None, ('dp', 'group'), None, 'mp'), may hold values from -1 to 1, as said below
- global_textout: float32 [2, 1536, 1536], P(None, ('mp', 'dp', 'group')), may hold values from -1 to 1, as said below
- global_textexpand: float32 [2, 1536, 6144], P(None, ('dp', 'group'), 'mp'), may hold values from -1 to 1, as said below
- global_textreduce: float32 [2, 6144, 1536], P(None, ('mp', 'dp', 'group')), may hold values from -1 to 1, as said below
- moments_qkv: float32 [4, 2, 1536, 3, 1536], P('group', None, 'dp', None, 'mp'), may hold values from -1 to 1, as said below
- moments_output: float32 [4, 2, 1536, 1536], P('group', None, ('mp', 'dp')), may hold values from -1 to 1, as said below
- moments_expand: float32 [4, 2, 1536, 6144], P('group', None, 'dp', 'mp'), may hold values from -1 to 1, as said below
- moments_reduce: float32 [4, 2, 6144, 1536], P('group', None, ('mp', 'dp')), may hold values from -1 to 1, as said below
- moments_textqkv: float32 [4, 2, 1536, 3, 1536], P('group', None, 'dp', None, 'mp'), may hold values from -1 to 1, as said below
- moments_textout: float32 [4, 2, 1536, 1536], P('group', None, ('mp', 'dp')), may hold values from -1 to 1, as said below
- moments_textexpand: float32 [4, 2, 1536, 6144], P('group', None, 'dp', 'mp'), may hold values from -1 to 1, as said below
- moments_textreduce: float32 [4, 2, 6144, 1536], P('group', None, ('mp', 'dp')), may hold values from -1 to 1, as said below
Outputs:
- image_result: bfloat16 [4, 4, 1024, 1536], P('group', 'dp', None, 'mp')
- text_result: bfloat16 [4, 4, 154, 1536], P('group', 'dp', None, 'mp')
- image_grad: bfloat16 [4, 4, 1024, 1536], P('group', 'dp', None, 'mp')
- text_grad: bfloat16 [4, 4, 154, 1536], P('group', 'dp', None, 'mp')
- image_modgrad: float32 [4, 4, 6, 1536], P('group', 'dp', None, 'mp')
- text_modgrad: float32 [4, 4, 6, 1536], P('group', 'dp', None, 'mp')
- fresh_qkv: float32 [4, 2, 1536, 3, 1536], P('group', None, 'dp', None, 'mp')
- fresh_output: float32 [4, 2, 1536, 1536], P('group', None, ('mp', 'dp'))
- fresh_expand: float32 [4, 2, 1536, 6144], P('group', None, 'dp', 'mp')
- fresh_reduce: float32 [4, 2, 6144, 1536], P('group', None, ('mp', 'dp'))
- fresh_textqkv: float32 [4, 2, 1536, 3, 1536], P('group', None, 'dp', None, 'mp')
- fresh_textout: float32 [4, 2, 1536, 1536], P('group', None, ('mp', 'dp'))
- fresh_textexpand: float32 [4, 2, 1536, 6144], P('group', None, 'dp', 'mp')
- fresh_textreduce: float32 [4, 2, 6144, 1536], P('group', None, ('mp', 'dp'))
- outer_qkv: float32 [3, 1536, 3, 1536], P(None, ('dp', 'group'), None, 'mp')
- outer_output: float32 [3, 1536, 1536], P(None, ('mp', 'dp', 'group'))
- outer_expand: float32 [3, 1536, 6144], P(None, ('dp', 'group'), 'mp')
- outer_reduce: float32 [3, 6144, 1536], P(None, ('mp', 'dp', 'group'))
- outer_textqkv: float32 [3, 1536, 3, 1536], P(None, ('dp', 'group'), None, 'mp')
- outer_textout: float32 [3, 1536, 1536], P(None, ('mp', 'dp', 'group'))
- outer_textexpand: float32 [3, 1536, 6144], P(None, ('dp', 'group'), 'mp')
- outer_textreduce: float32 [3, 6144, 1536], P(None, ('mp', 'dp', 'group'))
The draws below stay inside these ranges and needn't reach their ends.
Inputs may be any that keep to these rules, and one draw needn't show every extreme that they name: `group_counts`: live slots of each group; in every draw one group has all 4 live and another exactly 2. `global_qkv`: index 0 is the master weight, index 1 the outer momentum. `global_output`: as global_qkv. `global_expand`: as global_qkv. `global_reduce`: as global_qkv. `global_textqkv`: as global_qkv. `global_textout`: as global_qkv. `global_textexpand`: as global_qkv. `global_textreduce`: as global_qkv. `moments_qkv`: index 1 (second moments) is positive. `moments_output`: index 1 (second moments) is positive. `moments_expand`: index 1 (second moments) is positive. `moments_reduce`: index 1 (second moments) is positive. `moments_textqkv`: index 1 (second moments) is positive. `moments_textout`: index 1 (second moments) is positive. `moments_textexpand`: index 1 (second moments) is positive. `moments_textreduce`: index 1 (second moments) is positive.
All inputs are finite; a program needn't handle non-finite values.
Results may differ from the reference program's by a relative error of at most 0.025.
The reference program's roundings to bfloat16 on the way count: a program that leaves them out, or rounds other values in their place, can miss the bound.
Values may be sent and summed in bfloat16 or wider, within the bound.
No kernel may reach another device: no remote copies, remote signals or barrier semaphores. Data moves between devices by JAX's collectives and lax.ppermute only.
A program may use at most 576 MiB of HBM per device.

```python
import math
import jax
import jax.numpy as jnp
from jax import lax

D = 1536
HEADS = 24
HEAD_DIM = 64
FF = 6144
LI = 1024
LT = 154
MB = 2
STEP = 3
GROUPS = 4
SLOTS = 4
N_DP = 2


def draw_master_pair(key, shape, fan_in, label):
    master_key, momentum_key = jax.random.split(jax.random.fold_in(key, label))
    spread = fan_in ** (-0.5)
    master = jnp.clip(jax.random.normal(master_key, shape, jnp.float32), -4.0, 4.0) * spread
    momentum = jax.random.uniform(momentum_key, shape, jnp.float32, -0.005, 0.005)
    return jnp.stack([master, momentum])


def draw_moment_pair(key, shape, label):
    first_key, second_key = jax.random.split(jax.random.fold_in(key, label))
    full_shape = (GROUPS,) + shape
    first = jnp.clip(jax.random.normal(first_key, full_shape, jnp.float32) * 0.2, -0.8, 0.8)
    second = jnp.exp(jax.random.uniform(second_key, full_shape, jnp.float32, math.log(0.02), 0.0))
    return jnp.stack([first, second], 1)


def draw_group_counts(key, part):
    count_key, order_key = jax.random.split(jax.random.fold_in(key, 17))
    drawn = jax.random.randint(count_key, (GROUPS,), SLOTS // 2, SLOTS + 1)
    ranks = jax.random.permutation(order_key, GROUPS)
    counts = jnp.where(ranks == 0, SLOTS, jnp.where(ranks == 1, SLOTS // 2, drawn))
    return counts.astype(jnp.int32)


def draw_global_qkv(key, part):
    return draw_master_pair(key, (D, 3, D), D // 2, 101)


def draw_global_output(key, part):
    return draw_master_pair(key, (D, D), D // 8, 102)


def draw_global_expand(key, part):
    return draw_master_pair(key, (D, FF), D, 103)


def draw_global_reduce(key, part):
    return draw_master_pair(key, (FF, D), FF, 104)


def draw_global_textqkv(key, part):
    return draw_master_pair(key, (D, 3, D), D // 2, 105)


def draw_global_textout(key, part):
    return draw_master_pair(key, (D, D), D // 8, 106)


def draw_global_textexpand(key, part):
    return draw_master_pair(key, (D, FF), D, 107)


def draw_global_textreduce(key, part):
    return draw_master_pair(key, (FF, D), FF, 108)


def draw_moments_qkv(key, part):
    return draw_moment_pair(key, (D, 3, D), 201)


def draw_moments_output(key, part):
    return draw_moment_pair(key, (D, D), 202)


def draw_moments_expand(key, part):
    return draw_moment_pair(key, (D, FF), 203)


def draw_moments_reduce(key, part):
    return draw_moment_pair(key, (FF, D), 204)


def draw_moments_textqkv(key, part):
    return draw_moment_pair(key, (D, 3, D), 205)


def draw_moments_textout(key, part):
    return draw_moment_pair(key, (D, D), 206)


def draw_moments_textexpand(key, part):
    return draw_moment_pair(key, (D, FF), 207)


def draw_moments_textreduce(key, part):
    return draw_moment_pair(key, (FF, D), 208)


def level_of(own_key, dims, cuts, low, top_value):
    def one(dim, blocks):
        heights = jax.random.uniform(jax.random.fold_in(jax.random.fold_in(own_key, 6), dim), (blocks,), jnp.float32, low / len(cuts), top_value / len(cuts))
        return jnp.repeat(jnp.exp(heights), dims[dim] // blocks).reshape((-1,) + (1,) * (len(dims) - dim - 1))

    loudness = one(*cuts[0])
    for cut in cuts[1:]:
        loudness = loudness * one(*cut)
    return loudness


def noise(stream_key, dims, deviation, most, pieces=(), held_as=jnp.bfloat16):
    values = jax.random.normal(stream_key, dims, jnp.float32) * deviation
    if len(pieces) > 0:
        values = level_of(stream_key, dims, pieces, -0.22, 0.18) * values
    return jnp.clip(values, min=-most, max=most).astype(held_as)


def setup_inputs(seed: int = 0) -> dict:
    keys = jax.random.split(jax.random.key(seed), 24)
    return {
        "image_tokens": noise(keys[0], (GROUPS, SLOTS, LI, D), 1.0, 6.0, ((0, 4), (1, 2), (3, 4))),
        "text_tokens": noise(keys[1], (GROUPS, SLOTS, LT, D), 1.0, 6.0, ((0, 4), (1, 2), (3, 4))),
        "image_modulation": noise(keys[2], (GROUPS, SLOTS, 6, D), 0.7, 3.0, ((0, 4), (1, 2), (3, 4)), jnp.float32),
        "text_modulation": noise(keys[3], (GROUPS, SLOTS, 6, D), 0.7, 3.0, ((0, 4), (1, 2), (3, 4)), jnp.float32),
        "image_cotan": noise(keys[4], (GROUPS, SLOTS, LI, D), 1.0, 6.0, ((0, 4), (1, 2), (3, 4))),
        "text_cotan": noise(keys[5], (GROUPS, SLOTS, LT, D), 1.0, 6.0, ((0, 4), (1, 2), (3, 4))),
        "group_counts": draw_group_counts(jax.random.fold_in(keys[23], 71), 0),
        "global_qkv": draw_global_qkv(jax.random.fold_in(keys[23], 71), 0),
        "global_output": draw_global_output(jax.random.fold_in(keys[23], 71), 0),
        "global_expand": draw_global_expand(jax.random.fold_in(keys[23], 71), 0),
        "global_reduce": draw_global_reduce(jax.random.fold_in(keys[23], 71), 0),
        "global_textqkv": draw_global_textqkv(jax.random.fold_in(keys[23], 71), 0),
        "global_textout": draw_global_textout(jax.random.fold_in(keys[23], 71), 0),
        "global_textexpand": draw_global_textexpand(jax.random.fold_in(keys[23], 71), 0),
        "global_textreduce": draw_global_textreduce(jax.random.fold_in(keys[23], 71), 0),
        "moments_qkv": draw_moments_qkv(jax.random.fold_in(keys[23], 71), 0),
        "moments_output": draw_moments_output(jax.random.fold_in(keys[23], 71), 0),
        "moments_expand": draw_moments_expand(jax.random.fold_in(keys[23], 71), 0),
        "moments_reduce": draw_moments_reduce(jax.random.fold_in(keys[23], 71), 0),
        "moments_textqkv": draw_moments_textqkv(jax.random.fold_in(keys[23], 71), 0),
        "moments_textout": draw_moments_textout(jax.random.fold_in(keys[23], 71), 0),
        "moments_textexpand": draw_moments_textexpand(jax.random.fold_in(keys[23], 71), 0),
        "moments_textreduce": draw_moments_textreduce(jax.random.fold_in(keys[23], 71), 0),
    }


EPS_NORM = 1e-06
BETA_ONE = 0.9
BETA_TWO = 0.95
ADAM_EPS = 1e-08
LEARN_RATE = 0.02
DECAY_RATE = 0.1
OUTER_RATE = 0.7
OUTER_MOMENT = 0.9

@jax.custom_vjp
def low(v):
    return lax.optimization_barrier(v.astype(jnp.bfloat16)).astype(jnp.float32)

@jax.custom_vjp
def low_back(v):
    return v

def low_keep(v):
    return (low(v), None)

def low_pass(kept, grad):
    return (grad,)

def back_keep(v):
    return (v, None)

def back_low(kept, grad):
    return (low(grad),)
low.defvjp(low_keep, low_pass)
low_back.defvjp(back_keep, back_low)

def normalize(rows):
    centre = rows - lax.optimization_barrier(jnp.mean(rows, -1, keepdims=True))
    return centre * lax.rsqrt(lax.optimization_barrier(jnp.mean(centre * centre, -1, keepdims=True)) + EPS_NORM)

def layer(image, text, image_mod, text_mod, qkv_weight, out_weight, expand_weight, reduce_weight, tqkv_weight, tout_weight, texpand_weight, treduce_weight):
    high = lax.Precision.HIGHEST
    image_len = image.shape[0]
    length = image_len + text.shape[0]
    h_image = low(normalize(image) * (1.0 + image_mod[1]) + image_mod[0])
    h_text = low(normalize(text) * (1.0 + text_mod[1]) + text_mod[0])
    projected = jnp.concatenate([jnp.einsum('td,dcf->ctf', h_image, qkv_weight, precision=high), jnp.einsum('td,dcf->ctf', h_text, tqkv_weight, precision=high)], 1)
    projected = low_back(low(projected))
    per_head = projected.reshape(3, length, HEADS, HEAD_DIM)
    scores = low_back(jnp.einsum('qhe,khe->hqk', per_head[0], per_head[1], precision=high) * HEAD_DIM ** (-0.5))
    probability = low(jax.nn.softmax(scores, -1))
    mixed = jnp.einsum('hqk,khe->qhe', probability, per_head[2], precision=high).reshape(length, D)
    mixed = low_back(low(mixed))
    att_image = low_back(jnp.dot(mixed[:image_len], out_weight, precision=high, preferred_element_type=jnp.float32))
    att_text = low_back(jnp.dot(mixed[image_len:], tout_weight, precision=high, preferred_element_type=jnp.float32))
    after_image = image + image_mod[2] * att_image
    after_text = text + text_mod[2] * att_text
    two_image = low(normalize(after_image) * (1.0 + image_mod[4]) + image_mod[3])
    two_text = low(normalize(after_text) * (1.0 + text_mod[4]) + text_mod[3])
    inner_image = low_back(jnp.dot(two_image, expand_weight, precision=high, preferred_element_type=jnp.float32))
    inner_text = low_back(jnp.dot(two_text, texpand_weight, precision=high, preferred_element_type=jnp.float32))
    act_image = low(jax.nn.gelu(inner_image, approximate=True))
    act_text = low(jax.nn.gelu(inner_text, approximate=True))
    branch_image = low_back(jnp.dot(act_image, reduce_weight, precision=high, preferred_element_type=jnp.float32))
    branch_text = low_back(jnp.dot(act_text, treduce_weight, precision=high, preferred_element_type=jnp.float32))
    return (after_image + image_mod[5] * branch_image, after_text + text_mod[5] * branch_text)

def reference(image_tokens, text_tokens, image_modulation, text_modulation, image_cotan, text_cotan, group_counts, global_qkv, global_output, global_expand, global_reduce, global_textqkv, global_textout, global_textexpand, global_textreduce, moments_qkv, moments_output, moments_expand, moments_reduce, moments_textqkv, moments_textout, moments_textexpand, moments_textreduce):
    states = (global_qkv, global_output, global_expand, global_reduce, global_textqkv, global_textout, global_textexpand, global_textreduce)
    moments = (moments_qkv, moments_output, moments_expand, moments_reduce, moments_textqkv, moments_textout, moments_textexpand, moments_textreduce)
    weights = tuple((low(state[0]) for state in states))
    slot_index = jnp.arange(SLOTS, dtype=jnp.int32)
    order = slot_index % MB * N_DP + slot_index // MB
    correct_one = 1.0 - BETA_ONE ** STEP
    correct_two = 1.0 - BETA_TWO ** STEP
    results = [[], [], [], [], [], []]
    fresh_all = [[] for state in states]
    update_sum = [jnp.zeros_like(state[0]) for state in states]

    def one_slot(carry, inputs):
        image, text, image_mod, text_mod, image_cot, text_cot, flag = inputs
        outputs, pullback = jax.vjp(layer, image.astype(jnp.float32), text.astype(jnp.float32), image_mod, text_mod, *weights)
        grads = pullback((image_cot.astype(jnp.float32) * flag, text_cot.astype(jnp.float32) * flag))
        new_carry = tuple((held + more for held, more in zip(carry, grads[4:])))
        return (new_carry, (outputs[0].astype(jnp.bfloat16), outputs[1].astype(jnp.bfloat16), grads[0].astype(jnp.bfloat16), grads[1].astype(jnp.bfloat16), grads[2], grads[3]))
    for group in range(GROUPS):
        live = (order < group_counts[group]).astype(jnp.float32)
        zeros = tuple((jnp.zeros_like(weight) for weight in weights))
        totals, slot_outs = lax.scan(one_slot, zeros, (image_tokens[group], text_tokens[group], image_modulation[group], text_modulation[group], image_cotan[group], text_cotan[group], live))
        for place in range(6):
            results[place].append(slot_outs[place])
        count = group_counts[group].astype(jnp.float32)
        for place in range(8):
            gradient = totals[place] / count
            first = BETA_ONE * moments[place][group, 0] + (1.0 - BETA_ONE) * gradient
            second = BETA_TWO * moments[place][group, 1] + (1.0 - BETA_TWO) * gradient * gradient
            update = LEARN_RATE * (first / correct_one / (jnp.sqrt(second / correct_two) + ADAM_EPS) + DECAY_RATE * states[place][0])
            update_sum[place] = update_sum[place] + update
            fresh_all[place].append(jnp.stack([first, second]))
    outer_all = []
    for place in range(8):
        delta = update_sum[place] / GROUPS
        momentum = OUTER_MOMENT * states[place][1] + delta
        weight = states[place][0] - OUTER_RATE * (delta + OUTER_MOMENT * momentum)
        outer_all.append(jnp.stack([weight, delta, momentum]))
    stacked = [jnp.stack(items) for items in results]
    fresh = [jnp.stack(items) for items in fresh_all]
    return (stacked[0], stacked[1], stacked[2], stacked[3], stacked[4], stacked[5], fresh[0], fresh[1], fresh[2], fresh[3], fresh[4], fresh[5], fresh[6], fresh[7], outer_all[0], outer_all[1], outer_all[2], outer_all[3], outer_all[4], outer_all[5], outer_all[6], outer_all[7])
```

```python
import jax
import jax.numpy as jnp
from jax import lax
from jax.experimental import pallas as pl
from jax.experimental.pallas import tpu as pltpu
from jax.sharding import PartitionSpec as P

BF = jnp.bfloat16
F32 = jnp.float32
EPS_NORM = 1e-06
STEP = 3
BETA_ONE = 0.9
BETA_TWO = 0.95
ADAM_EPS = 1e-08
LEARN_RATE = 0.02
DECAY_RATE = 0.1
OUTER_RATE = 0.7
OUTER_MOMENT = 0.9
BLOCK = 256
VMEM_BYTES = 60 * 1024 * 1024
NT = (((1,), (1,)), ((), ()))
NN = (((1,), (0,)), ((), ()))
TN = (((0,), (0,)), ((), ()))


def mm(a, b, dims=NN):
    return lax.dot_general(a, b, dims, preferred_element_type=F32)


def call(kernel, grid, in_specs, out_specs, out_shape, flops, nbytes, scratch=(), prefetch=1):
    return pl.pallas_call(
        kernel,
        grid_spec=pltpu.PrefetchScalarGridSpec(
            num_scalar_prefetch=prefetch,
            grid=grid,
            in_specs=in_specs,
            out_specs=out_specs,
            scratch_shapes=list(scratch),
        ),
        out_shape=out_shape,
        compiler_params=pltpu.CompilerParams(
            vmem_limit_bytes=VMEM_BYTES, dimension_semantics=("arbitrary",) * len(grid)
        ),
        cost_estimate=pl.CostEstimate(flops=int(flops), bytes_accessed=int(nbytes), transcendentals=0),
    )


def rows_spec(width):
    return pl.BlockSpec((BLOCK, width), lambda i, *_: (i, 0))


def whole(shape):
    return pl.BlockSpec(shape, lambda *_: (0,) * len(shape), pipeline_mode=pl.Buffered(1))


def struct(shape, dtype):
    return jax.ShapeDtypeStruct(shape, dtype)


def ln_qkv(ids, xm, xo, mod, wi, wt, image_len, image_row, text_row):
    rows, half = xm.shape
    width, local = 2 * half, half // 2
    cols = 3 * local
    image_blocks = image_len // BLOCK

    def kernel(ids_ref, xm_ref, xo_ref, mod_ref, wi_ref, wt_ref, h_ref, qkv_ref, n_ref, inv_ref):
        i = pl.program_id(0)
        base = jnp.where(i < image_blocks, image_row, text_row)
        shift = mod_ref[pl.ds(base, 1), :]
        scale = 1.0 + mod_ref[pl.ds(base + 1, 1), :]
        first = ids_ref[1] == 0
        here = pl.ds(pl.multiple_of(ids_ref[0] * half, 128), half)
        there = pl.ds(pl.multiple_of((1 - ids_ref[0]) * half, 128), half)

        def chunk(r, carry):
            at = pl.ds(pl.multiple_of(r * 32, 32), 32)
            a = xm_ref[at, :].astype(F32)
            b = xo_ref[at, :].astype(F32)
            mean = (jnp.sum(a, 1, keepdims=True) + jnp.sum(b, 1, keepdims=True)) / width
            a, b = a - mean, b - mean
            var = (jnp.sum(a * a, 1, keepdims=True) + jnp.sum(b * b, 1, keepdims=True)) / width
            inv = lax.rsqrt(var + EPS_NORM)
            a, b = a * inv, b * inv
            n_ref[at, :] = jnp.where(first, a[:, :local], a[:, local:])
            inv_ref[at, :] = jnp.broadcast_to(inv, (32, 128))
            h_ref[at, here] = (a * scale[:, :half] + shift[:, :half]).astype(BF)
            h_ref[at, there] = (b * scale[:, half:] + shift[:, half:]).astype(BF)
            return carry

        lax.fori_loop(0, BLOCK // 32, chunk, 0, unroll=BLOCK // 32)

        def project(w_ref):
            for j in range(3):
                qkv_ref[j] = mm(h_ref[...], w_ref[j]).astype(BF)

        @pl.when(i < image_blocks)
        def _():
            project(wi_ref)

        @pl.when(i >= image_blocks)
        def _():
            project(wt_ref)

    return call(
        kernel,
        (pl.cdiv(rows, BLOCK),),
        [rows_spec(half), rows_spec(half), whole(mod.shape), whole(wi.shape), whole(wt.shape)],
        [
            rows_spec(width),
            pl.BlockSpec((3, BLOCK, local), lambda i, *_: (0, i, 0)),
            rows_spec(local),
            rows_spec(128),
        ],
        [
            struct((rows, width), BF),
            struct((3, rows, local), BF),
            struct((rows, local), F32),
            struct((rows, 128), F32),
        ],
        2 * rows * width * cols,
        rows * width * 6 + 4 * width * cols,
    )(ids, xm, xo, mod, wi, wt)


def pair_mask(array, head, dim):
    lane = lax.broadcasted_iota(jnp.int32, array.shape, 1)
    return jnp.where(lane // dim == head, array, jnp.zeros_like(array))


def q_chunks(rows, image_len):
    return [(s, BLOCK) for s in range(0, image_len, BLOCK)] + [(image_len, rows - image_len)]


def attend(qkv, length, image_len, dim=64):
    _, rows, local = qkv.shape
    pairs = local // 128
    lanes = pl.cdiv(rows, BLOCK) * BLOCK
    tail = length // 8 * 8
    scale = dim**-0.5

    def kernel(qkv_ref, out_ref, lse_ref, s_ref):
        for start, size in q_chunks(rows, image_len):
            total = None
            for head in range(128 // dim):
                q = pair_mask(qkv_ref[0, start : start + size, :], head, dim) * jnp.asarray(scale, BF)
                s_ref[:, :size] = mm(qkv_ref[1], q, NT)
                if tail < rows:
                    last = s_ref[tail:, :size]
                    row = lax.broadcasted_iota(jnp.int32, last.shape, 0) + tail
                    s_ref[tail:, :size] = jnp.where(row < length, last, -1e30)
                s = s_ref[:, :size]
                top = jnp.max(s, 0, keepdims=True)
                e = jnp.exp(s - top)
                norm = jnp.sum(e, 0, keepdims=True)
                lse_ref[0, head : head + 1, start : start + size] = top + jnp.log(norm)
                p = (e * (1.0 / norm)).astype(BF)
                mix = mm(p, pair_mask(qkv_ref[2], head, dim), TN)
                total = mix if total is None else total + mix
            out_ref[start : start + size, :] = total.astype(BF)

    return pl.pallas_call(
        kernel,
        grid=(pairs,),
        in_specs=[pl.BlockSpec((3, rows, 128), lambda j: (0, 0, j))],
        out_specs=[
            pl.BlockSpec((rows, 128), lambda j: (0, j)),
            pl.BlockSpec((1, 8, lanes), lambda j: (j, 0, 0)),
        ],
        out_shape=[struct((rows, local), BF), struct((pairs, 8, lanes), F32)],
        scratch_shapes=[pltpu.VMEM((rows, BLOCK), F32)],
        compiler_params=pltpu.CompilerParams(vmem_limit_bytes=VMEM_BYTES),
        cost_estimate=pl.CostEstimate(
            flops=16 * rows * rows * local, bytes_accessed=rows * local * 8, transcendentals=0
        ),
    )(qkv)


def attend_back(qkv, grad, lse, length, image_len, dim=64):
    _, rows, local = qkv.shape
    pairs = local // 128
    lanes = lse.shape[2]
    tail = length // 8 * 8
    scale = dim**-0.5

    def kernel(qkv_ref, grad_ref, lse_ref, out_ref, s_ref, gk_ref, gv_ref):
        gk_ref[...] = jnp.zeros_like(gk_ref)
        gv_ref[...] = jnp.zeros_like(gv_ref)
        for start, size in q_chunks(rows, image_len):
            total = None
            for head in range(128 // dim):
                q = pair_mask(qkv_ref[0, start : start + size, :], head, dim) * jnp.asarray(scale, BF)
                gm = pair_mask(grad_ref[start : start + size, :], head, dim)
                s_ref[:, :size] = mm(qkv_ref[1], q, NT)
                if tail < rows:
                    last = s_ref[tail:, :size]
                    row = lax.broadcasted_iota(jnp.int32, last.shape, 0) + tail
                    s_ref[tail:, :size] = jnp.where(row < length, last, -1e30)
                p = jnp.exp(s_ref[:, :size] - lse_ref[0, head : head + 1, start : start + size])
                gv_ref[...] += mm(p.astype(BF), gm)
                gp = mm(qkv_ref[2], gm, NT)
                delta = jnp.sum(p * gp, 0, keepdims=True)
                gs = (p * (gp - delta)).astype(BF)
                gk_ref[...] += mm(gs, q)
                gq = mm(gs, pair_mask(qkv_ref[1], head, dim), TN)
                total = gq if total is None else total + gq
            out_ref[0, start : start + size, :] = (total * scale).astype(BF)
        out_ref[1] = gk_ref[...].astype(BF)
        out_ref[2] = gv_ref[...].astype(BF)

    return pl.pallas_call(
        kernel,
        grid=(pairs,),
        in_specs=[
            pl.BlockSpec((3, rows, 128), lambda j: (0, 0, j)),
            pl.BlockSpec((rows, 128), lambda j: (0, j)),
            pl.BlockSpec((1, 8, lanes), lambda j: (j, 0, 0)),
        ],
        out_specs=pl.BlockSpec((3, rows, 128), lambda j: (0, 0, j)),
        out_shape=struct((3, rows, local), BF),
        scratch_shapes=[
            pltpu.VMEM((rows, BLOCK), F32),
            pltpu.VMEM((rows, 128), F32),
            pltpu.VMEM((rows, 128), F32),
        ],
        compiler_params=pltpu.CompilerParams(vmem_limit_bytes=VMEM_BYTES),
        cost_estimate=pl.CostEstimate(
            flops=40 * rows * rows * local, bytes_accessed=rows * local * 14, transcendentals=0
        ),
    )(qkv, grad, lse)


def out_project(ids, mixed, wi, wt, image_len):
    rows, local = mixed.shape
    width = wi.shape[1]
    half = width // 2
    image_blocks = image_len // BLOCK

    def kernel(ids_ref, a_ref, wi_ref, wt_ref, keep_ref, send_ref):
        i = pl.program_id(0)
        here = pl.ds(pl.multiple_of(ids_ref[0] * half, 128), half)
        there = pl.ds(pl.multiple_of((1 - ids_ref[0]) * half, 128), half)

        def project(w_ref):
            keep_ref[...] = mm(a_ref[...], w_ref[:, here]).astype(BF)
            send_ref[...] = mm(a_ref[...], w_ref[:, there]).astype(BF)

        @pl.when(i < image_blocks)
        def _():
            project(wi_ref)

        @pl.when(i >= image_blocks)
        def _():
            project(wt_ref)

    return call(
        kernel,
        (pl.cdiv(rows, BLOCK),),
        [rows_spec(local), whole(wi.shape), whole(wt.shape)],
        [rows_spec(half), rows_spec(half)],
        [struct((rows, half), BF), struct((rows, half), BF)],
        2 * rows * width * local,
        rows * width * 3 + 4 * width * local,
    )(ids, mixed, wi, wt)


def input_partial(ids, gqkv, wi, wt, image_len):
    _, rows, local = gqkv.shape
    width = wi.shape[1]
    half = width // 2
    image_blocks = image_len // BLOCK

    def kernel(ids_ref, a_ref, wi_ref, wt_ref, keep_ref, send_ref):
        i = pl.program_id(0)
        here = pl.ds(pl.multiple_of(ids_ref[0] * half, 128), half)
        there = pl.ds(pl.multiple_of((1 - ids_ref[0]) * half, 128), half)

        def project(w_ref):
            for out_ref, lo in ((keep_ref, here), (send_ref, there)):
                total = None
                for j in range(3):
                    part = mm(a_ref[j], w_ref[j, lo, :], NT)
                    total = part if total is None else total + part
                out_ref[...] = total.astype(BF)

        @pl.when(i < image_blocks)
        def _():
            project(wi_ref)

        @pl.when(i >= image_blocks)
        def _():
            project(wt_ref)

    return call(
        kernel,
        (pl.cdiv(rows, BLOCK),),
        [pl.BlockSpec((3, BLOCK, local), lambda i, *_: (0, i, 0)), whole(wi.shape), whole(wt.shape)],
        [rows_spec(half), rows_spec(half)],
        [struct((rows, half), BF), struct((rows, half), BF)],
        2 * rows * width * local * 3,
        rows * width * 5 + 12 * width * local,
    )(ids, gqkv, wi, wt)


def after_norm(xa, xb, aa, ab, gate, half, width):
    a = xa.astype(F32) + gate[:, :half] * aa.astype(F32)
    b = xb.astype(F32) + gate[:, half:] * ab.astype(F32)
    mean = (jnp.sum(a, 1, keepdims=True) + jnp.sum(b, 1, keepdims=True)) / width
    ca, cb = a - mean, b - mean
    var = (jnp.sum(ca * ca, 1, keepdims=True) + jnp.sum(cb * cb, 1, keepdims=True)) / width
    inv = lax.rsqrt(var + EPS_NORM)
    return a, ca * inv, cb * inv, inv


def mid_prepare(ids, live, xm, xo, am, ao, cm, co, mod, image_len, image_row, text_row):
    rows, half = xm.shape
    width, local = 2 * half, half // 2
    image_blocks = image_len // BLOCK
    step = 32

    def kernel(ids_ref, live_ref, xm_ref, xo_ref, am_ref, ao_ref, cm_ref, co_ref, mod_ref, h_ref, g_ref, own_ref):
        i = pl.program_id(0)
        base = jnp.where(i < image_blocks, image_row, text_row)
        gate_a = mod_ref[pl.ds(base + 2, 1), :]
        shift = mod_ref[pl.ds(base + 3, 1), :]
        scale = 1.0 + mod_ref[pl.ds(base + 4, 1), :]
        gate_m = mod_ref[pl.ds(base + 5, 1), :] * live_ref[0]
        first = ids_ref[1] == 0
        here = pl.ds(pl.multiple_of(ids_ref[0] * half, 128), half)
        there = pl.ds(pl.multiple_of((1 - ids_ref[0]) * half, 128), half)

        def chunk(r, carry):
            at = pl.ds(pl.multiple_of(r * step, step), step)
            a, na, nb, _ = after_norm(xm_ref[at, :], xo_ref[at, :], am_ref[at, :], ao_ref[at, :], gate_a, half, width)
            own_ref[at, :] = jnp.where(first, a[:, :local], a[:, local:])
            h_ref[at, here] = (na * scale[:, :half] + shift[:, :half]).astype(BF)
            h_ref[at, there] = (nb * scale[:, half:] + shift[:, half:]).astype(BF)
            g_ref[at, here] = (cm_ref[at, :].astype(F32) * gate_m[:, :half]).astype(BF)
            g_ref[at, there] = (co_ref[at, :].astype(F32) * gate_m[:, half:]).astype(BF)
            return carry

        lax.fori_loop(0, BLOCK // step, chunk, 0, unroll=BLOCK // step)

    return call(
        kernel,
        (pl.cdiv(rows, BLOCK),),
        [rows_spec(half)] * 6 + [whole(mod.shape)],
        [rows_spec(width), rows_spec(width), rows_spec(local)],
        [struct((rows, width), BF), struct((rows, width), BF), struct((rows, local), F32)],
        rows * width * 20,
        rows * width * 11,
        prefetch=2,
    )(ids, live, xm, xo, am, ao, cm, co, mod)


def gelu_pair(v):
    k, c3 = 0.7978845608028654, 0.044715
    v2 = v * v
    t = jnp.tanh(k * v * (1.0 + c3 * v2))
    up = 0.5 * (1.0 + t)
    return v * up, up + 0.5 * v * (1.0 - t * t) * (k * (1.0 + 3.0 * c3 * v2))


def mlp(ids, h, g, w1i, w1t, w2i, w2t, image_len, tile=256):
    rows, width = h.shape
    half = width // 2
    hidden = w1i.shape[1]
    steps = hidden // tile
    piece = 512

    def kernel(
        ids_ref, h_ref, g_ref, w1i_ref, w1t_ref, w2i_ref, w2t_ref,
        act_ref, gin_ref, bk_ref, bs_ref, gk_ref, gs_ref, b_acc, g_acc,
    ):
        i = pl.program_id(0)
        here = pl.ds(pl.multiple_of(ids_ref[0] * half, 128), half)
        there = pl.ds(pl.multiple_of((1 - ids_ref[0]) * half, 128), half)

        def work(at, w1_ref, w2_ref):
            inner = mm(h_ref[at, :], w1_ref[...])
            ag = mm(g_ref[at, :], w2_ref[...], NT)
            act, slope = gelu_pair(inner)
            act = act.astype(BF)
            gin = (ag * slope).astype(BF)
            act_ref[at, :] = act
            gin_ref[at, :] = gin
            parts = ((b_acc, mm(act, w2_ref[...])), (g_acc, mm(gin, w1_ref[...], NT)))

            @pl.when(i == 0)
            def _():
                for ref, value in parts:
                    ref[at, :] = value

            @pl.when(i > 0)
            def _():
                for ref, value in parts:
                    ref[at, :] += value

        def image_piece(r, carry):
            work(pl.ds(pl.multiple_of(r * piece, piece), piece), w1i_ref, w2i_ref)
            return carry

        lax.fori_loop(0, image_len // piece, image_piece, 0)
        work(slice(image_len, rows), w1t_ref, w2t_ref)

        @pl.when(i == steps - 1)
        def _():
            bk_ref[...] = b_acc[:, here].astype(BF)
            bs_ref[...] = b_acc[:, there].astype(BF)
            gk_ref[...] = g_acc[:, here].astype(BF)
            gs_ref[...] = g_acc[:, there].astype(BF)

    w1_spec = pl.BlockSpec((width, tile), lambda i, *_: (0, i))
    w2_spec = pl.BlockSpec((tile, width), lambda i, *_: (i, 0))
    out_tile = pl.BlockSpec((rows, tile), lambda i, *_: (0, i))
    return call(
        kernel,
        (steps,),
        [whole((rows, width)), whole((rows, width)), w1_spec, w1_spec, w2_spec, w2_spec],
        [out_tile, out_tile] + [whole((rows, half))] * 4,
        [struct((rows, hidden), BF)] * 2 + [struct((rows, half), BF)] * 4,
        8 * rows * width * hidden,
        rows * width * 12 + 8 * width * hidden,
        scratch=[pltpu.VMEM((rows, width), F32), pltpu.VMEM((rows, width), F32)],
    )(ids, h, g, w1i, w1t, w2i, w2t)


def back_prepare(ids, live, xm, xo, am, ao, cm, co, gm, go, mod, wi, wt, image_len, image_row, text_row):
    rows, half = xm.shape
    width, local = 2 * half, half // 2
    image_blocks = image_len // BLOCK
    step = 32

    def kernel(
        ids_ref, live_ref, xm_ref, xo_ref, am_ref, ao_ref, cm_ref, co_ref, gm_ref, go_ref, mod_ref, wi_ref, wt_ref,
        ga_ref, gmix_ref, own_ref, sums_ref,
    ):
        i = pl.program_id(0)
        base = jnp.where(i < image_blocks, image_row, text_row)
        gate_a = mod_ref[pl.ds(base + 2, 1), :]
        scale = 1.0 + mod_ref[pl.ds(base + 4, 1), :]
        first = ids_ref[1] == 0
        live_now = live_ref[0]
        here = pl.ds(pl.multiple_of(ids_ref[0] * half, 128), half)
        there = pl.ds(pl.multiple_of((1 - ids_ref[0]) * half, 128), half)

        @pl.when((i == 0) | (i == image_blocks))
        def _():
            sums_ref[...] = jnp.zeros_like(sums_ref)

        def own(v):
            return jnp.where(first, v[:, :local], v[:, local:])

        def chunk(r, carry):
            at = pl.ds(pl.multiple_of(r * step, step), step)
            _, na, nb, inv = after_norm(xm_ref[at, :], xo_ref[at, :], am_ref[at, :], ao_ref[at, :], gate_a, half, width)
            ga = gm_ref[at, :].astype(F32)
            gb = go_ref[at, :].astype(F32)
            qa, qb = ga * scale[:, :half], gb * scale[:, half:]
            mean = (jnp.sum(qa, 1, keepdims=True) + jnp.sum(qb, 1, keepdims=True)) / width
            cross = (jnp.sum(qa * na, 1, keepdims=True) + jnp.sum(qb * nb, 1, keepdims=True)) / width
            fa = cm_ref[at, :].astype(F32) * live_now + inv * (qa - mean - na * cross)
            fb = co_ref[at, :].astype(F32) * live_now + inv * (qb - mean - nb * cross)
            ga_ref[at, here] = (gate_a[:, :half] * fa).astype(BF)
            ga_ref[at, there] = (gate_a[:, half:] * fb).astype(BF)
            fo, go_own = own(fa), own(ga)
            own_ref[at, :] = fo
            row = i * BLOCK + r * step + lax.broadcasted_iota(jnp.int32, (step, local), 0)
            inside = row < rows
            for k, value in enumerate((go_own, go_own * own(na), fo * own(am_ref[at, :].astype(F32)))):
                value = jnp.where(inside, value, 0.0)
                sums_ref[0, k * 8 : (k + 1) * 8, :] += jnp.sum(value.reshape(step // 8, 8, local), 0)
            return carry

        lax.fori_loop(0, BLOCK // step, chunk, 0, unroll=BLOCK // step)

        def project(w_ref):
            gmix_ref[...] = mm(ga_ref[...], w_ref[...], NT).astype(BF)

        @pl.when(i < image_blocks)
        def _():
            project(wi_ref)

        @pl.when(i >= image_blocks)
        def _():
            project(wt_ref)

    return call(
        kernel,
        (pl.cdiv(rows, BLOCK),),
        [rows_spec(half)] * 8 + [whole(mod.shape), whole(wi.shape), whole(wt.shape)],
        [
            rows_spec(width),
            rows_spec(local),
            rows_spec(local),
            pl.BlockSpec((1, 24, local), lambda i, *_: (jnp.where(i < image_blocks, 0, 1), 0, 0)),
        ],
        [
            struct((rows, width), BF),
            struct((rows, local), BF),
            struct((rows, local), F32),
            struct((2, 24, local), F32),
        ],
        2 * rows * width * local,
        rows * width * 12,
        prefetch=2,
    )(ids, live, xm, xo, am, ao, cm, co, gm, go, mod, wi, wt)


def adam(ids, inv_count, moment, grad):
    _, lead, _, piece, cols = moment.shape
    correct_one = 1.0 - BETA_ONE**STEP
    correct_two = 1.0 - BETA_TWO**STEP

    def kernel(ids_ref, inv_ref, m_ref, g_ref, fresh_ref, keep_ref, send_ref):
        t = pl.program_id(1)
        g = g_ref[0, 0].astype(F32) * inv_ref[0]
        first = BETA_ONE * m_ref[0, 0, 0] + (1.0 - BETA_ONE) * g
        second = BETA_TWO * m_ref[1, 0, 0] + (1.0 - BETA_TWO) * g * g
        fresh_ref[0, 0, 0] = first
        fresh_ref[1, 0, 0] = second
        update = ((first / correct_one) / (jnp.sqrt(second / correct_two) + ADAM_EPS)).astype(BF)

        @pl.when(t < 2)
        def _():
            send_ref[0, 0] = update

        @pl.when(t >= 2)
        def _():
            keep_ref[0, 0] = update

    def block(t, ids_ref):
        return (t % 2) * 2 + jnp.where(t < 2, 1 - ids_ref[0], ids_ref[0])

    pairs = pl.BlockSpec((2, 1, 1, piece, cols), lambda l, t, ids_ref, _: (0, l, block(t, ids_ref), 0, 0))
    side = struct((2, lead, piece, cols), BF)
    return call(
        kernel,
        (lead, 4),
        [
            pairs,
            pl.BlockSpec((1, 1, piece, cols), lambda l, t, ids_ref, _: (l, block(t, ids_ref), 0, 0)),
        ],
        [
            pairs,
            pl.BlockSpec((1, 1, piece, cols), lambda l, t, *_: (jnp.maximum(t - 2, 0), l, 0, 0)),
            pl.BlockSpec((1, 1, piece, cols), lambda l, t, *_: (jnp.minimum(t, 1), l, 0, 0)),
        ],
        [struct(moment.shape, F32), side, side],
        lead * piece * cols * 80,
        lead * piece * cols * 80,
        prefetch=2,
    )(ids, inv_count, moment, grad)


def outer_step(ids, state, keep, got, far, groups):
    _, lead, piece, cols = state.shape

    def kernel(ids_ref, s_ref, k_ref, g_ref, f_ref, out_ref):
        near = (k_ref[0, 0].astype(F32) + g_ref[0, 0].astype(F32)).astype(BF).astype(F32)
        total = near + f_ref[0].astype(F32)
        master = s_ref[0, 0]
        delta = LEARN_RATE * (total * (1.0 / groups) + DECAY_RATE * master)
        momentum = OUTER_MOMENT * s_ref[1, 0] + delta
        out_ref[0, 0] = master - OUTER_RATE * (delta + OUTER_MOMENT * momentum)
        out_ref[1, 0] = delta
        out_ref[2, 0] = momentum

    side = pl.BlockSpec((1, 1, piece, cols), lambda l, ids_ref: (ids_ref[2], l, 0, 0))
    return call(
        kernel,
        (lead,),
        [
            pl.BlockSpec((2, 1, piece, cols), lambda l, *_: (0, l, 0, 0)),
            side,
            side,
            pl.BlockSpec((1, piece, cols), lambda l, *_: (l, 0, 0)),
        ],
        pl.BlockSpec((3, 1, piece, cols), lambda l, *_: (0, l, 0, 0)),
        struct((3, lead, piece, cols), F32),
        lead * piece * cols * 10,
        lead * piece * cols * 26,
    )(ids, state, keep, got, far)


def solution(mesh):
    n_group, n_dp, n_mp = mesh.shape["group"], mesh.shape["dp"], mesh.shape["mp"]
    core_perm = [(g, g ^ 1) for g in range(n_group)]
    x_perm = [(g, g ^ 2) for g in range(n_group)]
    z_perm = [(m, m ^ 1) for m in range(n_mp)]
    y_perm = [(d, d ^ 1) for d in range(n_dp)]
    turn_perm = [
        (g * n_mp + m, ((g // 2) * 2 + m // 2) * n_mp + (g % 2) * 2 + m % 2)
        for g in range(n_group)
        for m in range(n_mp)
    ]

    def core_swap(a):
        return lax.ppermute(a, "group", core_perm)

    def x_swap(a):
        return lax.ppermute(a, "group", x_perm)

    def z_swap(a):
        return lax.ppermute(a, "mp", z_perm)

    def y_swap(a):
        return lax.ppermute(a, "dp", y_perm)

    def turn(a):
        return lax.ppermute(a, ("group", "mp"), turn_perm)

    def after(value, *others):
        return lax.optimization_barrier((value,) + others)[0]

    def by(flag, a, b, axis):
        return jnp.where(flag == 0, jnp.concatenate([a, b], axis), jnp.concatenate([b, a], axis))

    def body(
        image_tokens, text_tokens, image_modulation, text_modulation, image_cotan, text_cotan,
        group_counts, *tensors,
    ):
        states, moments = tensors[:8], tensors[8:]
        g, d, m = lax.axis_index("group"), lax.axis_index("dp"), lax.axis_index("mp")
        c, xc, zl = g % 2, g // 2, m % 2
        ids = jnp.stack([c, zl, xc]).astype(jnp.int32)

        slots = image_tokens.shape[1]
        image_len, text_len = image_tokens.shape[2], text_tokens.shape[2]
        text_rows = -(-text_len // 32) * 32
        local = image_tokens.shape[3]
        width = local * n_mp
        rows_all = image_len + text_rows
        length = image_len + text_len

        def join(image, text):
            return jnp.concatenate([image, jnp.pad(text, ((0, text_rows - text_len), (0, 0)))], 0)

        mod_rows = jnp.concatenate(
            [
                image_modulation[0].reshape(-1, local),
                text_modulation[0].reshape(-1, local),
                jnp.broadcast_to(group_counts[0].astype(F32), (1, local)),
            ],
            0,
        )
        mod_rows = jnp.pad(mod_rows, ((0, -mod_rows.shape[0] % 8), (0, 0)))

        def lead_form(a):
            return a.transpose(0, 2, 1, 3) if a.ndim == 4 else a[:, None]

        def weight_pair(index):
            piece = lead_form(states[index][:1])[0].astype(BF)
            return by(c, piece, core_swap(piece), 1)

        x_own, c_own, pairs = [None] * slots, [None] * slots, [None] * 8
        jobs = [("m", 0), ("x", 0), ("w", 0), ("w", 4)]
        jobs += [("x", s) for s in range(1, slots)]
        jobs += [("w", 1), ("w", 5), ("w", 2), ("w", 6), ("c", 0), ("w", 3), ("w", 7)]
        jobs += [("c", s) for s in range(1, slots)]
        done = []
        for kind, i in jobs:
            if kind == "m":
                value = mod_rows
            elif kind == "w":
                value = weight_pair(i)
            elif kind == "x":
                value = join(image_tokens[0, i], text_tokens[0, i])
            else:
                value = join(image_cotan[0, i], text_cotan[0, i])
            if len(done) >= 2:
                value = after(value, done[-2])
            value = turn(value)
            done.append(value)
            if kind == "m":
                mod_own = value
            elif kind == "w":
                pairs[i] = value
            elif kind == "x":
                x_own[i] = value
            else:
                c_own[i] = value
        count = mod_own[slots * 12, 0]

        def gather_rows(own):
            pair = by(zl, own, z_swap(own), 1)
            return pair, core_swap(pair)

        mod_full = jnp.concatenate(gather_rows(mod_own), 1)

        def gather_weight(pair, stream):
            px = x_swap(pair)
            if n_dp == 2:
                py = y_swap(pair)
                pd = x_swap(py) if stream == 0 else y_swap(px)
                return by(d, by(xc, pair, px, 1), by(xc, py, pd, 1), 1)
            return lax.all_gather(by(xc, pair, px, 1), "dp", axis=1, tiled=True)

        full = [gather_weight(pairs[i], i // 4) for i in range(8)]
        full = [w if w.shape[0] > 1 else w[0] for w in full]

        def reduce_half(keep, send):
            return (keep.astype(F32) + core_swap(send).astype(F32)).astype(BF)

        def reduce_full(keep, send):
            mine = reduce_half(keep, send)
            mine = (mine.astype(F32) + z_swap(mine).astype(F32)).astype(BF)
            return mine, core_swap(mine)

        def reduce_own(keep, send):
            mine = reduce_half(keep, send)
            away = lax.dynamic_slice_in_dim(mine, (1 - zl) * local, local, 1)
            here = lax.dynamic_slice_in_dim(mine, zl * local, local, 1)
            return (here.astype(F32) + z_swap(away).astype(F32)).astype(BF).astype(F32)

        def column_sums(a):
            return jnp.stack([jnp.sum(a[:image_len], 0), jnp.sum(a[image_len:], 0)])

        def per_row(index, s):
            return jnp.concatenate(
                [
                    jnp.broadcast_to(mod_own[s * 6 + index], (image_len, local)),
                    jnp.broadcast_to(mod_own[(slots + s) * 6 + index], (text_rows, local)),
                ],
                0,
            )

        results, grads_x, modgrads, saved = [], [], [], []
        xs = [gather_rows(a) for a in x_own]
        cs = [gather_rows(a) for a in c_own]
        for s in range(slots):
            places = (image_len, s * 6, (slots + s) * 6)
            live = (s * n_dp + d < count).astype(F32)
            live_ref = live.reshape(1)
            h1, qkv, n1o, inv1 = ln_qkv(ids, *xs[s], mod_full, full[0], full[4], *places)
            mixed, lse = attend(qkv, length, image_len)
            att = reduce_full(*out_project(ids, mixed, full[1], full[5], image_len))
            h2, gbranch, after_own = mid_prepare(ids, live_ref, *xs[s], *att, *cs[s], mod_full, *places)
            act, ginner, bk, bs, gk, gs = mlp(ids, h2, gbranch, full[2], full[6], full[3], full[7], image_len)
            gh2 = reduce_full(gk, gs)
            gatt, gmixed, gafter_own, sums = back_prepare(
                ids, live_ref, *xs[s], *att, *cs[s], *gh2, mod_full, full[1], full[5], *places
            )
            gqkv = attend_back(qkv, gmixed, lse, length, image_len)
            branch = reduce_own(bk, bs)
            gh1 = reduce_own(*input_partial(ids, gqkv, full[0], full[4], image_len))
            q = gh1 * (1.0 + per_row(1, s))
            total = jnp.stack([jnp.sum(q, 1), jnp.sum(q * n1o, 1)])
            total = total + z_swap(total)
            total = (total + core_swap(total)) / width
            gx = gafter_own + inv1[:, :1] * (q - total[0][:, None] - n1o * total[1][:, None])
            res = after_own + per_row(5, s) * branch
            results.append(turn(res.astype(BF)))
            grads_x.append(turn(gx.astype(BF)))
            sums = jnp.sum(sums.reshape(2, 3, 8, local), 2)
            modgrads.append(
                jnp.stack(
                    [
                        column_sums(gh1), column_sums(gh1 * n1o), sums[:, 2], sums[:, 0], sums[:, 1],
                        column_sums(c_own[s].astype(F32) * live * branch),
                    ]
                )
            )
            saved.append(((h1, gqkv), (mixed, gatt), (h2, ginner), (act, gbranch)))
        mod_back = turn(jnp.stack(modgrads).reshape(slots * 12, local)).reshape(slots, 6, 2, local)

        fresh, outer = [None] * 8, [None] * 8
        inv_count = (1.0 / group_counts[0].astype(F32)).reshape(1)
        for k in (3, 2, 1, 0):
            for stream in range(2):
                idx = k + 4 * stream
                lo, hi = (0, image_len) if stream == 0 else (image_len, rows_all)

                def weight_grad(start, size):
                    total = 0.0
                    for s in range(slots):
                        left, right = saved[s][k]
                        left = lax.dynamic_slice_in_dim(left[lo:hi], start, size, 1)
                        if k == 0:
                            part = jnp.einsum("td,ctf->cdf", left, right[:, lo:hi], preferred_element_type=F32)
                        else:
                            part = mm(left, right[lo:hi], TN)[None]
                        total = total + part
                    return total

                rows = saved[0][k][0].shape[1]
                if n_dp == 2:
                    part = rows // 2
                    got = y_swap(weight_grad((1 - d) * part, part).astype(BF))
                    shard = (weight_grad(d * part, part) + got.astype(F32)).astype(BF)
                else:
                    shard = lax.psum_scatter(
                        weight_grad(0, rows).astype(BF), "dp", scatter_dimension=1, tiled=True
                    )
                grad = turn(shard)
                moment = lead_form(moments[idx][0])
                lead, rows, cols = moment.shape[1:]
                piece = rows // n_group
                new, keep, send = adam(
                    ids, inv_count, moment.reshape(2, lead, n_group, piece, cols),
                    grad.reshape(lead, n_group, piece, cols),
                )
                got = core_swap(send)
                pick = lambda a: lax.dynamic_index_in_dim(a, 1 - xc, 0, False)
                far = x_swap((pick(keep).astype(F32) + pick(got).astype(F32)).astype(BF))
                out = outer_step(ids, lead_form(states[idx]), keep, got, far, n_group)
                new = new.reshape(2, lead, rows, cols)
                if moments[idx].ndim == 5:
                    fresh[idx] = new.transpose(0, 2, 1, 3)[None]
                    outer[idx] = out.transpose(0, 2, 1, 3)
                else:
                    fresh[idx] = new[:, 0][None]
                    outer[idx] = out[:, 0]

        res = jnp.stack(results)
        gx = jnp.stack(grads_x)
        return (
            res[None, :, :image_len],
            res[None, :, image_len:length],
            gx[None, :, :image_len],
            gx[None, :, image_len:length],
            mod_back[None, :, :, 0],
            mod_back[None, :, :, 1],
            *fresh,
            *outer,
        )

    tokens = P("group", "dp", None, "mp")
    weight_specs = (
        P(None, ("dp", "group"), None, "mp"),
        P(None, ("mp", "dp", "group"), None),
        P(None, ("dp", "group"), "mp"),
        P(None, ("mp", "dp", "group"), None),
    ) * 2
    moment_specs = (
        P("group", None, "dp", None, "mp"),
        P("group", None, ("mp", "dp"), None),
        P("group", None, "dp", "mp"),
        P("group", None, ("mp", "dp"), None),
    ) * 2
    return jax.shard_map(
        body,
        mesh=mesh,
        in_specs=(tokens,) * 6 + (P("group"),) + weight_specs + moment_specs,
        out_specs=(tokens,) * 6 + moment_specs + weight_specs,
        check_vma=False,
    )
```

```python
import jax
import jax.numpy as jnp
from jax import lax
from jax.experimental import pallas as pl
from jax.experimental.pallas import tpu as pltpu
from jax.sharding import PartitionSpec as P

BF = jnp.bfloat16
F32 = jnp.float32
EPS_NORM = 1e-06
STEP = 3
BETA_ONE = 0.9
BETA_TWO = 0.95
ADAM_EPS = 1e-08
LEARN_RATE = 0.02
DECAY_RATE = 0.1
OUTER_RATE = 0.7
OUTER_MOMENT = 0.9
BLOCK = 256
VMEM_BYTES = 60 * 1024 * 1024
COST_SHARE = 4
NT = (((1,), (1,)), ((), ()))
NN = (((1,), (0,)), ((), ()))
TN = (((0,), (0,)), ((), ()))


def mm(a, b, dims=NN):
    return lax.dot_general(a, b, dims, preferred_element_type=F32)


def cost(flops, nbytes):
    return pl.CostEstimate(
        flops=int(flops) // COST_SHARE, bytes_accessed=int(nbytes) // COST_SHARE, transcendentals=0
    )


def call(kernel, grid, in_specs, out_specs, out_shape, flops, nbytes, scratch=(), prefetch=1):
    return pl.pallas_call(
        kernel,
        grid_spec=pltpu.PrefetchScalarGridSpec(
            num_scalar_prefetch=prefetch,
            grid=grid,
            in_specs=in_specs,
            out_specs=out_specs,
            scratch_shapes=list(scratch),
        ),
        out_shape=out_shape,
        compiler_params=pltpu.CompilerParams(
            vmem_limit_bytes=VMEM_BYTES, dimension_semantics=("arbitrary",) * len(grid)
        ),
        cost_estimate=cost(flops, nbytes),
    )


def rows_spec(width):
    return pl.BlockSpec((BLOCK, width), lambda i, *_: (i, 0))


def whole(shape):
    return pl.BlockSpec(shape, lambda *_: (0,) * len(shape), pipeline_mode=pl.Buffered(1))


def struct(shape, dtype):
    return jax.ShapeDtypeStruct(shape, dtype)


def cast_states(states):
    cols = states[0].shape[-1]
    sizes = [s.shape[1] * s.shape[2] for s in states]

    def kernel(*refs):
        out_ref, at = refs[-1], 0
        for ref, state in zip(refs, states):
            for lead in range(state.shape[1]):
                rows = state.shape[2]
                out_ref[at : at + rows, :] = ref[0, lead].astype(BF)
                at += rows

    return call(
        kernel,
        (1,),
        [pl.BlockSpec((1,) + s.shape[1:], lambda *_: (0, 0, 0, 0), pipeline_mode=pl.Buffered(1)) for s in states],
        whole((sum(sizes), cols)),
        struct((sum(sizes), cols), BF),
        sum(sizes) * cols,
        sum(sizes) * cols * 6,
        prefetch=0,
    )(*states)


def pair_pieces(ids, mine, other, shapes):
    cols = mine.shape[1]

    def kernel(ids_ref, m_ref, o_ref, *out_refs):
        def lay(first_ref, second_ref):
            at = 0
            for out_ref, group in zip(out_refs, shapes):
                for k, (lead, rows) in enumerate(group):
                    for j in range(lead):
                        out_ref[k * lead + j, :rows, :] = first_ref[at : at + rows, :]
                        out_ref[k * lead + j, rows:, :] = second_ref[at : at + rows, :]
                        at += rows

        @pl.when(ids_ref[0] == 0)
        def _():
            lay(m_ref, o_ref)

        @pl.when(ids_ref[0] == 1)
        def _():
            lay(o_ref, m_ref)

    outs = [(len(group) * group[0][0], 2 * group[0][1], cols) for group in shapes]
    return call(
        kernel,
        (1,),
        [whole(mine.shape), whole(mine.shape)],
        [whole(s) for s in outs],
        [struct(s, BF) for s in outs],
        mine.size,
        mine.size * 8,
    )(ids, mine, other)


def lay_quads(ids, parts):
    lead, rows, cols = parts[0].shape

    def kernel(ids_ref, *refs):
        copies = []
        for k in range(4):
            at = pl.multiple_of(ids_ref[5 + k] * rows, 16)
            copies.append(pltpu.make_async_copy(refs[k], refs[4].at[:, pl.ds(at, rows), :], refs[5].at[k]))
            copies[-1].start()
        for copy in copies:
            copy.wait()

    return pl.pallas_call(
        kernel,
        in_specs=[pl.BlockSpec(memory_space=pltpu.SMEM)] + [pl.BlockSpec(memory_space=pl.ANY)] * 4,
        out_specs=pl.BlockSpec(memory_space=pl.ANY),
        out_shape=struct((lead, 4 * rows, cols), BF),
        scratch_shapes=[pltpu.SemaphoreType.DMA((4,))],
        compiler_params=pltpu.CompilerParams(vmem_limit_bytes=1024 * 1024),
        cost_estimate=cost(0, lead * rows * cols * 16),
    )(ids, *parts)


def ln_qkv(ids, xm, xo, mod, wi, wt, image_len, image_row, text_row):
    rows, half = xm.shape
    width, local = 2 * half, half // 2
    cols = 3 * local
    image_blocks = image_len // BLOCK

    def kernel(ids_ref, xm_ref, xo_ref, mod_ref, wi_ref, wt_ref, h_ref, qkv_ref, n_ref, inv_ref):
        i = pl.program_id(0)
        base = jnp.where(i < image_blocks, image_row, text_row)
        shift = mod_ref[pl.ds(base, 1), :]
        scale = 1.0 + mod_ref[pl.ds(base + 1, 1), :]
        first = ids_ref[1] == 0
        here = pl.ds(pl.multiple_of(ids_ref[0] * half, 128), half)
        there = pl.ds(pl.multiple_of((1 - ids_ref[0]) * half, 128), half)

        def chunk(r, carry):
            at = pl.ds(pl.multiple_of(r * 32, 32), 32)
            a = xm_ref[at, :].astype(F32)
            b = xo_ref[at, :].astype(F32)
            mean = (jnp.sum(a, 1, keepdims=True) + jnp.sum(b, 1, keepdims=True)) / width
            a, b = a - mean, b - mean
            var = (jnp.sum(a * a, 1, keepdims=True) + jnp.sum(b * b, 1, keepdims=True)) / width
            inv = lax.rsqrt(var + EPS_NORM)
            a, b = a * inv, b * inv
            n_ref[at, :] = jnp.where(first, a[:, :local], a[:, local:])
            inv_ref[at, :] = jnp.broadcast_to(inv, (32, 128))
            h_ref[at, here] = (a * scale[:, :half] + shift[:, :half]).astype(BF)
            h_ref[at, there] = (b * scale[:, half:] + shift[:, half:]).astype(BF)
            return carry

        lax.fori_loop(0, BLOCK // 32, chunk, 0, unroll=BLOCK // 32)

        def project(w_ref):
            for j in range(3):
                qkv_ref[j] = mm(h_ref[...], w_ref[j]).astype(BF)

        @pl.when(i < image_blocks)
        def _():
            project(wi_ref)

        @pl.when(i >= image_blocks)
        def _():
            project(wt_ref)

    return call(
        kernel,
        (pl.cdiv(rows, BLOCK),),
        [rows_spec(half), rows_spec(half), whole(mod.shape), whole(wi.shape), whole(wt.shape)],
        [
            rows_spec(width),
            pl.BlockSpec((3, BLOCK, local), lambda i, *_: (0, i, 0)),
            rows_spec(local),
            rows_spec(128),
        ],
        [
            struct((rows, width), BF),
            struct((3, rows, local), BF),
            struct((rows, local), F32),
            struct((rows, 128), F32),
        ],
        2 * rows * width * cols,
        rows * width * 6 + 4 * width * cols,
    )(ids, xm, xo, mod, wi, wt)


def pair_mask(array, head, dim):
    lane = lax.broadcasted_iota(jnp.int32, array.shape, 1)
    return jnp.where(lane // dim == head, array, jnp.zeros_like(array))


def q_chunks(rows, image_len):
    return [(s, BLOCK) for s in range(0, image_len, BLOCK)] + [(image_len, rows - image_len)]


def attend(qkv, length, image_len, dim=64):
    _, rows, local = qkv.shape
    pairs = local // 128
    lanes = pl.cdiv(rows, BLOCK) * BLOCK
    tail = length // 8 * 8
    scale = dim**-0.5

    def kernel(qkv_ref, out_ref, lse_ref, s_ref):
        for start, size in q_chunks(rows, image_len):
            total = None
            for head in range(128 // dim):
                q = pair_mask(qkv_ref[0, start : start + size, :], head, dim) * jnp.asarray(scale, BF)
                s_ref[:, :size] = mm(qkv_ref[1], q, NT)
                if tail < rows:
                    last = s_ref[tail:, :size]
                    row = lax.broadcasted_iota(jnp.int32, last.shape, 0) + tail
                    s_ref[tail:, :size] = jnp.where(row < length, last, -1e30)
                s = s_ref[:, :size]
                top = jnp.max(s, 0, keepdims=True)
                e = jnp.exp(s - top)
                norm = jnp.sum(e, 0, keepdims=True)
                lse_ref[0, head : head + 1, start : start + size] = top + jnp.log(norm)
                p = (e * (1.0 / norm)).astype(BF)
                mix = mm(p, pair_mask(qkv_ref[2], head, dim), TN)
                total = mix if total is None else total + mix
            out_ref[start : start + size, :] = total.astype(BF)

    return pl.pallas_call(
        kernel,
        grid=(pairs,),
        in_specs=[pl.BlockSpec((3, rows, 128), lambda j: (0, 0, j))],
        out_specs=[
            pl.BlockSpec((rows, 128), lambda j: (0, j)),
            pl.BlockSpec((1, 8, lanes), lambda j: (j, 0, 0)),
        ],
        out_shape=[struct((rows, local), BF), struct((pairs, 8, lanes), F32)],
        scratch_shapes=[pltpu.VMEM((rows, BLOCK), F32)],
        compiler_params=pltpu.CompilerParams(vmem_limit_bytes=VMEM_BYTES),
        cost_estimate=cost(16 * rows * rows * local, rows * local * 8),
    )(qkv)


def attend_back(qkv, grad, lse, length, image_len, dim=64):
    _, rows, local = qkv.shape
    pairs = local // 128
    lanes = lse.shape[2]
    tail = length // 8 * 8
    scale = dim**-0.5

    def kernel(qkv_ref, grad_ref, lse_ref, out_ref, s_ref, gk_ref, gv_ref):
        gk_ref[...] = jnp.zeros_like(gk_ref)
        gv_ref[...] = jnp.zeros_like(gv_ref)
        for start, size in q_chunks(rows, image_len):
            total = None
            for head in range(128 // dim):
                q = pair_mask(qkv_ref[0, start : start + size, :], head, dim) * jnp.asarray(scale, BF)
                gm = pair_mask(grad_ref[start : start + size, :], head, dim)
                s_ref[:, :size] = mm(qkv_ref[1], q, NT)
                if tail < rows:
                    last = s_ref[tail:, :size]
                    row = lax.broadcasted_iota(jnp.int32, last.shape, 0) + tail
                    s_ref[tail:, :size] = jnp.where(row < length, last, -1e30)
                p = jnp.exp(s_ref[:, :size] - lse_ref[0, head : head + 1, start : start + size])
                gv_ref[...] += mm(p.astype(BF), gm)
                gp = mm(qkv_ref[2], gm, NT)
                delta = jnp.sum(p * gp, 0, keepdims=True)
                gs = (p * (gp - delta)).astype(BF)
                gk_ref[...] += mm(gs, q)
                gq = mm(gs, pair_mask(qkv_ref[1], head, dim), TN)
                total = gq if total is None else total + gq
            out_ref[0, start : start + size, :] = (total * scale).astype(BF)
        out_ref[1] = gk_ref[...].astype(BF)
        out_ref[2] = gv_ref[...].astype(BF)

    return pl.pallas_call(
        kernel,
        grid=(pairs,),
        in_specs=[
            pl.BlockSpec((3, rows, 128), lambda j: (0, 0, j)),
            pl.BlockSpec((rows, 128), lambda j: (0, j)),
            pl.BlockSpec((1, 8, lanes), lambda j: (j, 0, 0)),
        ],
        out_specs=pl.BlockSpec((3, rows, 128), lambda j: (0, 0, j)),
        out_shape=struct((3, rows, local), BF),
        scratch_shapes=[
            pltpu.VMEM((rows, BLOCK), F32),
            pltpu.VMEM((rows, 128), F32),
            pltpu.VMEM((rows, 128), F32),
        ],
        compiler_params=pltpu.CompilerParams(vmem_limit_bytes=VMEM_BYTES),
        cost_estimate=cost(40 * rows * rows * local, rows * local * 14),
    )(qkv, grad, lse)


def out_project(ids, mixed, wi, wt, image_len):
    rows, local = mixed.shape
    width = wi.shape[1]
    half = width // 2
    image_blocks = image_len // BLOCK

    def kernel(ids_ref, a_ref, wi_ref, wt_ref, keep_ref, send_ref):
        i = pl.program_id(0)
        here = pl.ds(pl.multiple_of(ids_ref[0] * half, 128), half)
        there = pl.ds(pl.multiple_of((1 - ids_ref[0]) * half, 128), half)

        def project(w_ref):
            keep_ref[...] = mm(a_ref[...], w_ref[:, here]).astype(BF)
            send_ref[...] = mm(a_ref[...], w_ref[:, there]).astype(BF)

        @pl.when(i < image_blocks)
        def _():
            project(wi_ref)

        @pl.when(i >= image_blocks)
        def _():
            project(wt_ref)

    return call(
        kernel,
        (pl.cdiv(rows, BLOCK),),
        [rows_spec(local), whole(wi.shape), whole(wt.shape)],
        [rows_spec(half), rows_spec(half)],
        [struct((rows, half), BF), struct((rows, half), BF)],
        2 * rows * width * local,
        rows * width * 3 + 4 * width * local,
    )(ids, mixed, wi, wt)


def input_partial(ids, gqkv, wi, wt, image_len):
    _, rows, local = gqkv.shape
    width = wi.shape[1]
    half = width // 2
    image_blocks = image_len // BLOCK

    def kernel(ids_ref, a_ref, wi_ref, wt_ref, keep_ref, send_ref):
        i = pl.program_id(0)
        here = pl.ds(pl.multiple_of(ids_ref[0] * half, 128), half)
        there = pl.ds(pl.multiple_of((1 - ids_ref[0]) * half, 128), half)

        def project(w_ref):
            for out_ref, lo in ((keep_ref, here), (send_ref, there)):
                total = None
                for j in range(3):
                    part = mm(a_ref[j], w_ref[j, lo, :], NT)
                    total = part if total is None else total + part
                out_ref[...] = total.astype(BF)

        @pl.when(i < image_blocks)
        def _():
            project(wi_ref)

        @pl.when(i >= image_blocks)
        def _():
            project(wt_ref)

    return call(
        kernel,
        (pl.cdiv(rows, BLOCK),),
        [pl.BlockSpec((3, BLOCK, local), lambda i, *_: (0, i, 0)), whole(wi.shape), whole(wt.shape)],
        [rows_spec(half), rows_spec(half)],
        [struct((rows, half), BF), struct((rows, half), BF)],
        2 * rows * width * local * 3,
        rows * width * 5 + 12 * width * local,
    )(ids, gqkv, wi, wt)


def after_norm(xa, xb, aa, ab, gate, half, width):
    a = xa.astype(F32) + gate[:, :half] * aa.astype(F32)
    b = xb.astype(F32) + gate[:, half:] * ab.astype(F32)
    mean = (jnp.sum(a, 1, keepdims=True) + jnp.sum(b, 1, keepdims=True)) / width
    ca, cb = a - mean, b - mean
    var = (jnp.sum(ca * ca, 1, keepdims=True) + jnp.sum(cb * cb, 1, keepdims=True)) / width
    inv = lax.rsqrt(var + EPS_NORM)
    return a, ca * inv, cb * inv, inv


def mid_prepare(ids, live, xm, xo, am, ao, cm, co, mod, image_len, image_row, text_row):
    rows, half = xm.shape
    width, local = 2 * half, half // 2
    image_blocks = image_len // BLOCK
    step = 32

    def kernel(ids_ref, live_ref, xm_ref, xo_ref, am_ref, ao_ref, cm_ref, co_ref, mod_ref, h_ref, g_ref, own_ref):
        i = pl.program_id(0)
        base = jnp.where(i < image_blocks, image_row, text_row)
        gate_a = mod_ref[pl.ds(base + 2, 1), :]
        shift = mod_ref[pl.ds(base + 3, 1), :]
        scale = 1.0 + mod_ref[pl.ds(base + 4, 1), :]
        gate_m = mod_ref[pl.ds(base + 5, 1), :] * live_ref[0]
        first = ids_ref[1] == 0
        here = pl.ds(pl.multiple_of(ids_ref[0] * half, 128), half)
        there = pl.ds(pl.multiple_of((1 - ids_ref[0]) * half, 128), half)

        def chunk(r, carry):
            at = pl.ds(pl.multiple_of(r * step, step), step)
            a, na, nb, _ = after_norm(xm_ref[at, :], xo_ref[at, :], am_ref[at, :], ao_ref[at, :], gate_a, half, width)
            own_ref[at, :] = jnp.where(first, a[:, :local], a[:, local:])
            h_ref[at, here] = (na * scale[:, :half] + shift[:, :half]).astype(BF)
            h_ref[at, there] = (nb * scale[:, half:] + shift[:, half:]).astype(BF)
            g_ref[at, here] = (cm_ref[at, :].astype(F32) * gate_m[:, :half]).astype(BF)
            g_ref[at, there] = (co_ref[at, :].astype(F32) * gate_m[:, half:]).astype(BF)
            return carry

        lax.fori_loop(0, BLOCK // step, chunk, 0, unroll=BLOCK // step)

    return call(
        kernel,
        (pl.cdiv(rows, BLOCK),),
        [rows_spec(half)] * 6 + [whole(mod.shape)],
        [rows_spec(width), rows_spec(width), rows_spec(local)],
        [struct((rows, width), BF), struct((rows, width), BF), struct((rows, local), F32)],
        rows * width * 20,
        rows * width * 11,
        prefetch=2,
    )(ids, live, xm, xo, am, ao, cm, co, mod)


def gelu_pair(v):
    k, c3 = 0.7978845608028654, 0.044715
    v2 = v * v
    t = jnp.tanh(k * v * (1.0 + c3 * v2))
    up = 0.5 * (1.0 + t)
    return v * up, up + 0.5 * v * (1.0 - t * t) * (k * (1.0 + 3.0 * c3 * v2))


def mlp(ids, h, g, w1i, w1t, w2i, w2t, image_len, tile=512):
    rows, width = h.shape
    half = width // 2
    hidden = w1i.shape[1]
    steps = hidden // tile
    piece = 512

    def kernel(
        ids_ref, h_ref, g_ref, w1i_ref, w1t_ref, w2i_ref, w2t_ref,
        act_ref, gin_ref, bk_ref, bs_ref, gk_ref, gs_ref, b_acc, g_acc,
    ):
        i = pl.program_id(0)
        here = pl.ds(pl.multiple_of(ids_ref[0] * half, 128), half)
        there = pl.ds(pl.multiple_of((1 - ids_ref[0]) * half, 128), half)

        def work(at, w1_ref, w2_ref):
            inner = mm(h_ref[at, :], w1_ref[...])
            ag = mm(g_ref[at, :], w2_ref[...], NT)
            act, slope = gelu_pair(inner)
            act = act.astype(BF)
            gin = (ag * slope).astype(BF)
            act_ref[at, :] = act
            gin_ref[at, :] = gin
            parts = ((b_acc, mm(act, w2_ref[...])), (g_acc, mm(gin, w1_ref[...], NT)))

            @pl.when(i == 0)
            def _():
                for ref, value in parts:
                    ref[at, :] = value

            @pl.when(i > 0)
            def _():
                for ref, value in parts:
                    ref[at, :] += value

        def image_piece(r, carry):
            work(pl.ds(pl.multiple_of(r * piece, piece), piece), w1i_ref, w2i_ref)
            return carry

        lax.fori_loop(0, image_len // piece, image_piece, 0)
        work(slice(image_len, rows), w1t_ref, w2t_ref)

        @pl.when(i == steps - 1)
        def _():
            bk_ref[...] = b_acc[:, here].astype(BF)
            bs_ref[...] = b_acc[:, there].astype(BF)
            gk_ref[...] = g_acc[:, here].astype(BF)
            gs_ref[...] = g_acc[:, there].astype(BF)

    w1_spec = pl.BlockSpec((width, tile), lambda i, *_: (0, i))
    w2_spec = pl.BlockSpec((tile, width), lambda i, *_: (i, 0))
    out_tile = pl.BlockSpec((rows, tile), lambda i, *_: (0, i))
    return call(
        kernel,
        (steps,),
        [whole((rows, width)), whole((rows, width)), w1_spec, w1_spec, w2_spec, w2_spec],
        [out_tile, out_tile] + [whole((rows, half))] * 4,
        [struct((rows, hidden), BF)] * 2 + [struct((rows, half), BF)] * 4,
        8 * rows * width * hidden,
        rows * width * 12 + 8 * width * hidden,
        scratch=[pltpu.VMEM((rows, width), F32), pltpu.VMEM((rows, width), F32)],
    )(ids, h, g, w1i, w1t, w2i, w2t)


def back_prepare(ids, live, xm, xo, am, ao, cm, co, gm, go, mod, wi, wt, image_len, image_row, text_row):
    rows, half = xm.shape
    width, local = 2 * half, half // 2
    image_blocks = image_len // BLOCK
    step = 32

    def kernel(
        ids_ref, live_ref, xm_ref, xo_ref, am_ref, ao_ref, cm_ref, co_ref, gm_ref, go_ref, mod_ref, wi_ref, wt_ref,
        ga_ref, gmix_ref, own_ref, sums_ref,
    ):
        i = pl.program_id(0)
        base = jnp.where(i < image_blocks, image_row, text_row)
        gate_a = mod_ref[pl.ds(base + 2, 1), :]
        scale = 1.0 + mod_ref[pl.ds(base + 4, 1), :]
        first = ids_ref[1] == 0
        live_now = live_ref[0]
        here = pl.ds(pl.multiple_of(ids_ref[0] * half, 128), half)
        there = pl.ds(pl.multiple_of((1 - ids_ref[0]) * half, 128), half)

        @pl.when((i == 0) | (i == image_blocks))
        def _():
            sums_ref[...] = jnp.zeros_like(sums_ref)

        def own(v):
            return jnp.where(first, v[:, :local], v[:, local:])

        def chunk(r, carry):
            at = pl.ds(pl.multiple_of(r * step, step), step)
            _, na, nb, inv = after_norm(xm_ref[at, :], xo_ref[at, :], am_ref[at, :], ao_ref[at, :], gate_a, half, width)
            ga = gm_ref[at, :].astype(F32)
            gb = go_ref[at, :].astype(F32)
            qa, qb = ga * scale[:, :half], gb * scale[:, half:]
            mean = (jnp.sum(qa, 1, keepdims=True) + jnp.sum(qb, 1, keepdims=True)) / width
            cross = (jnp.sum(qa * na, 1, keepdims=True) + jnp.sum(qb * nb, 1, keepdims=True)) / width
            fa = cm_ref[at, :].astype(F32) * live_now + inv * (qa - mean - na * cross)
            fb = co_ref[at, :].astype(F32) * live_now + inv * (qb - mean - nb * cross)
            ga_ref[at, here] = (gate_a[:, :half] * fa).astype(BF)
            ga_ref[at, there] = (gate_a[:, half:] * fb).astype(BF)
            fo, go_own = own(fa), own(ga)
            own_ref[at, :] = fo
            row = i * BLOCK + r * step + lax.broadcasted_iota(jnp.int32, (step, local), 0)
            inside = row < rows
            for k, value in enumerate((go_own, go_own * own(na), fo * own(am_ref[at, :].astype(F32)))):
                value = jnp.where(inside, value, 0.0)
                sums_ref[0, k * 8 : (k + 1) * 8, :] += jnp.sum(value.reshape(step // 8, 8, local), 0)
            return carry

        lax.fori_loop(0, BLOCK // step, chunk, 0, unroll=BLOCK // step)

        def project(w_ref):
            gmix_ref[...] = mm(ga_ref[...], w_ref[...], NT).astype(BF)

        @pl.when(i < image_blocks)
        def _():
            project(wi_ref)

        @pl.when(i >= image_blocks)
        def _():
            project(wt_ref)

    return call(
        kernel,
        (pl.cdiv(rows, BLOCK),),
        [rows_spec(half)] * 8 + [whole(mod.shape), whole(wi.shape), whole(wt.shape)],
        [
            rows_spec(width),
            rows_spec(local),
            rows_spec(local),
            pl.BlockSpec((1, 24, local), lambda i, *_: (jnp.where(i < image_blocks, 0, 1), 0, 0)),
        ],
        [
            struct((rows, width), BF),
            struct((rows, local), BF),
            struct((rows, local), F32),
            struct((2, 24, local), F32),
        ],
        2 * rows * width * local,
        rows * width * 12,
        prefetch=2,
    )(ids, live, xm, xo, am, ao, cm, co, gm, go, mod, wi, wt)


def grad_specs(right, tile, height, row_block):
    if right.ndim == 3:
        return (
            pl.BlockSpec((1, height, right.shape[2]), lambda j, *_: (j, row_block, 0)),
            right.shape[0],
            right.shape[2],
        )
    return pl.BlockSpec((height, tile), lambda j, *_: (row_block, j)), right.shape[1] // tile, tile


def grad_out(right, tile, part):
    if right.ndim == 3:
        lead, _, cols = right.shape
        return pl.BlockSpec((1, part, cols), lambda j, *_: (j, 0, 0)), struct((lead, part, cols), BF)
    return (
        pl.BlockSpec((1, part, tile), lambda j, *_: (0, 0, j)),
        struct((1, part, right.shape[1]), BF),
    )


def weight_grad(ids, which, lefts, rights, height, add=None, tile=512):
    part = lefts[0].shape[1] // 2
    n = len(lefts)
    right_spec, steps, _ = grad_specs(rights[0], tile, height, 0)
    narrow = part % 128 != 0
    left_spec = pl.BlockSpec(
        (height, 2 * part if narrow else part),
        lambda j, ids_ref: (0, 0 if narrow else ids_ref[which]),
        pipeline_mode=pl.Buffered(1),
    )
    out_spec, out_shape = grad_out(rights[0], tile, part)
    flat = rights[0].ndim == 2

    def kernel(ids_ref, *refs):
        total = None
        for left_ref, right_ref in zip(refs[:n], refs[n : 2 * n]):
            value = mm(left_ref[...], right_ref[...] if flat else right_ref[0], TN)
            total = value if total is None else total + value
        if narrow:
            total = jnp.where(ids_ref[which] == 0, total[:part], total[part:])
        if add is not None:
            total = total + refs[2 * n][0].astype(F32)
        refs[-1][0] = total.astype(BF)

    more = [] if add is None else [add]
    return call(
        kernel,
        (steps,),
        [left_spec] * n + [right_spec] * n + [out_spec] * len(more),
        out_spec,
        out_shape,
        2 * n * height * part * out_shape.shape[0] * out_shape.shape[2],
        n * height * (part + out_shape.shape[0] * out_shape.shape[2]) * 2,
    )(ids, *lefts, *rights, *more)


def adam(ids, inv_count, moment, grad):
    _, lead, _, piece, cols = moment.shape
    correct_one = 1.0 - BETA_ONE**STEP
    correct_two = 1.0 - BETA_TWO**STEP

    def kernel(ids_ref, inv_ref, m_ref, g_ref, fresh_ref, keep_ref, send_ref):
        t = pl.program_id(1)
        g = g_ref[0, 0].astype(F32) * inv_ref[0]
        first = BETA_ONE * m_ref[0, 0, 0] + (1.0 - BETA_ONE) * g
        second = BETA_TWO * m_ref[1, 0, 0] + (1.0 - BETA_TWO) * g * g
        fresh_ref[0, 0, 0] = first
        fresh_ref[1, 0, 0] = second
        update = ((first / correct_one) / (jnp.sqrt(second / correct_two) + ADAM_EPS)).astype(BF)

        @pl.when(t < 2)
        def _():
            send_ref[0, 0] = update

        @pl.when(t >= 2)
        def _():
            keep_ref[0, 0] = update

    def block(t, ids_ref):
        return (t % 2) * 2 + jnp.where(t < 2, 1 - ids_ref[0], ids_ref[0])

    pairs = pl.BlockSpec((2, 1, 1, piece, cols), lambda l, t, ids_ref, _: (0, l, block(t, ids_ref), 0, 0))
    side = struct((2, lead, piece, cols), BF)
    return call(
        kernel,
        (lead, 4),
        [
            pairs,
            pl.BlockSpec((1, 1, piece, cols), lambda l, t, ids_ref, _: (l, block(t, ids_ref), 0, 0)),
        ],
        [
            pairs,
            pl.BlockSpec((1, 1, piece, cols), lambda l, t, *_: (jnp.maximum(t - 2, 0), l, 0, 0)),
            pl.BlockSpec((1, 1, piece, cols), lambda l, t, *_: (jnp.minimum(t, 1), l, 0, 0)),
        ],
        [struct(moment.shape, F32), side, side],
        lead * piece * cols * 80,
        lead * piece * cols * 80,
        prefetch=2,
    )(ids, inv_count, moment, grad)


def outer_step(ids, state, keep, got, far, groups):
    _, lead, piece, cols = state.shape

    def kernel(ids_ref, s_ref, k_ref, g_ref, f_ref, out_ref):
        near = (k_ref[0, 0].astype(F32) + g_ref[0, 0].astype(F32)).astype(BF).astype(F32)
        total = near + f_ref[0].astype(F32)
        master = s_ref[0, 0]
        delta = LEARN_RATE * (total * (1.0 / groups) + DECAY_RATE * master)
        momentum = OUTER_MOMENT * s_ref[1, 0] + delta
        out_ref[0, 0] = master - OUTER_RATE * (delta + OUTER_MOMENT * momentum)
        out_ref[1, 0] = delta
        out_ref[2, 0] = momentum

    side = pl.BlockSpec((1, 1, piece, cols), lambda l, ids_ref: (ids_ref[2], l, 0, 0))
    return call(
        kernel,
        (lead,),
        [
            pl.BlockSpec((2, 1, piece, cols), lambda l, *_: (0, l, 0, 0)),
            side,
            side,
            pl.BlockSpec((1, piece, cols), lambda l, *_: (l, 0, 0)),
        ],
        pl.BlockSpec((3, 1, piece, cols), lambda l, *_: (0, l, 0, 0)),
        struct((3, lead, piece, cols), F32),
        lead * piece * cols * 10,
        lead * piece * cols * 26,
    )(ids, state, keep, got, far)


def solution(mesh):
    n_group, n_dp, n_mp = mesh.shape["group"], mesh.shape["dp"], mesh.shape["mp"]
    core_perm = [(g, g ^ 1) for g in range(n_group)]
    x_perm = [(g, g ^ 2) for g in range(n_group)]
    z_perm = [(m, m ^ 1) for m in range(n_mp)]
    y_perm = [(d, d ^ 1) for d in range(n_dp)]
    turn_perm = [
        (g * n_mp + m, ((g // 2) * 2 + m // 2) * n_mp + (g % 2) * 2 + m % 2)
        for g in range(n_group)
        for m in range(n_mp)
    ]

    def core_swap(a):
        return lax.ppermute(a, "group", core_perm)

    def x_swap(a):
        return lax.ppermute(a, "group", x_perm)

    def z_swap(a):
        return lax.ppermute(a, "mp", z_perm)

    def y_swap(a):
        return lax.ppermute(a, "dp", y_perm)

    def turn(a):
        return lax.ppermute(a, ("group", "mp"), turn_perm)

    def by(flag, a, b, axis):
        return jnp.where(flag == 0, jnp.concatenate([a, b], axis), jnp.concatenate([b, a], axis))

    def body(
        image_tokens, text_tokens, image_modulation, text_modulation, image_cotan, text_cotan,
        group_counts, *tensors,
    ):
        states, moments = tensors[:8], tensors[8:]
        g, d, m = lax.axis_index("group"), lax.axis_index("dp"), lax.axis_index("mp")
        c, xc, zl = g % 2, g // 2, m % 2
        place = (d % 2) * 2 + xc
        ids = jnp.stack([c, zl, xc, d % 2, 1 - d % 2, place, place ^ 1, place ^ 2, place ^ 3]).astype(jnp.int32)

        slots = image_tokens.shape[1]
        image_len, text_len = image_tokens.shape[2], text_tokens.shape[2]
        text_rows = -(-text_len // 32) * 32
        local = image_tokens.shape[3]
        width = local * n_mp
        rows_all = image_len + text_rows
        length = image_len + text_len

        last = []

        def hold(value, others):
            if not others:
                return value
            leaves, tree = jax.tree.flatten(value)
            held = lax.optimization_barrier(tuple(leaves) + tuple(others))
            return jax.tree.unflatten(tree, list(held[: len(leaves)]))

        def step(fn, first, *rest, need=()):
            out = fn(hold(first, last + jax.tree.leaves(need)), *rest)
            last[:] = [jax.tree.leaves(out)[0]]
            return out

        def send(move, value):
            return move(hold(value, last))

        turned, over_x, over_y, over_z = (lambda value, move=move: send(move, value) for move in (turn, x_swap, y_swap, z_swap))

        def sync(*need):
            if n_dp == 2:
                last.extend(jax.tree.leaves(need))

        def join(tokens):
            image, text = tokens
            return jnp.concatenate([image, jnp.pad(text, ((0, text_rows - text_len), (0, 0)))], 0)

        def mod_join(parts):
            image, text, counts = parts
            rows = jnp.concatenate(
                [
                    image[0].reshape(-1, local),
                    text[0].reshape(-1, local),
                    jnp.broadcast_to(counts[0].astype(F32), (1, local)),
                ],
                0,
            )
            return jnp.pad(rows, ((0, -rows.shape[0] % 8), (0, 0)))

        def lead_form(a):
            return a.transpose(0, 2, 1, 3) if a.ndim == 4 else a[:, None]

        def gather_one(a):
            if n_dp != 2:
                return (lax.all_gather(by(xc, a, over_x(a), 1), "dp", axis=1, tiled=True),)
            return a, over_x(a), over_y(a)

        def corner(parts, stream):
            if len(parts) == 1:
                return parts
            a, px, py = parts
            return a, px, py, (over_x(py) if stream == 0 else over_y(px))

        def assemble(parts, need=()):
            if len(parts) > 1:
                return step(lambda a, *rest: lay_quads(ids, (a,) + rest), *parts, need=need)
            return parts[0]

        def flat(w):
            return w if w.shape[0] > 1 else w[0]

        def z_pair(own):
            got = over_z(own)
            return lambda need=(): with_core(step(lambda a, b: by(zl, a, b, 1), own, got, need=need))

        def with_core(pair):
            return pair, send(core_swap, pair)

        def half_sum(keep, give, need=()):
            got = send(core_swap, give)
            return step(lambda a, b: (a.astype(F32) + b.astype(F32)).astype(BF), keep, got, need=need)

        def half_start(keep, give):
            got = send(core_swap, give)
            return lambda: step(lambda a, b: (a.astype(F32) + b.astype(F32)).astype(BF), keep, got)

        def full_sum(mine, got, need=()):
            return with_core(step(lambda a, b: (a.astype(F32) + b.astype(F32)).astype(BF), mine, got, need=need))

        def own_part(mine):
            away = lax.dynamic_slice_in_dim(mine, (1 - zl) * local, local, 1)
            here = lax.dynamic_slice_in_dim(mine, zl * local, local, 1)
            return here, over_z(away)

        def own_sum(here, got):
            return (here.astype(F32) + got.astype(F32)).astype(BF).astype(F32)

        def column_sums(a):
            return jnp.stack([jnp.sum(a[:image_len], 0), jnp.sum(a[image_len:], 0)])

        def per_row(index, s):
            return jnp.concatenate(
                [
                    jnp.broadcast_to(mod_own[s * 6 + index], (image_len, local)),
                    jnp.broadcast_to(mod_own[(slots + s) * 6 + index], (text_rows, local)),
                ],
                0,
            )

        places = [(image_len, s * 6, (slots + s) * 6) for s in range(slots)]

        def first_part(s, need=()):
            return step(lambda a, b: ln_qkv(ids, a, b, mod_full, *wq, *places[s]), *xs[s], need=need)

        def mixing(s, need=()):
            return step(lambda a: attend(a, length, image_len), firsts[s][1], need=need)

        def projection(s, need=()):
            keep, give = step(lambda a: out_project(ids, a, *wo, image_len), lses[s][0], need=need)
            mine = half_sum(keep, give)
            return mine, over_z(mine)

        def middle(s, need=()):
            return step(
                lambda a, b: mid_prepare(ids, lives[s].reshape(1), a, b, *atts[s], *cs[s], mod_full, *places[s]),
                *xs[s],
                need=need,
            )

        def dense(s):
            return step(lambda a, b: mlp(ids, a, b, *w1, *w2, image_len), mids[s][0], mids[s][1])

        def text_of(arrays):
            return jnp.concatenate([a[..., image_len:, :] for a in arrays], arrays[0].ndim - 2)

        lead_states = [lead_form(a) for a in states]
        mine = step(lambda a, b: cast_states((a, b)), lead_states[0], lead_states[4])
        got = send(core_swap, mine)
        rest_order = (1, 5, 2, 6, 7, 3)
        rest = step(lambda *a: cast_states(a), *(lead_states[i] for i in rest_order))
        rows_of = [a.shape[2] for a in lead_states]
        pairs = dict(zip((0, 4), step(lambda a, b: pair_pieces(ids, a, b, [[(3, rows_of[0])]] * 2), mine, got)))
        pairs = {i: turned(a) for i, a in pairs.items()}
        rest_got = send(core_swap, rest)
        mod_own = turned(mod_join((image_modulation, text_modulation, group_counts)))
        x_own = [turned(join((image_tokens[0, 0], text_tokens[0, 0])))]
        count = mod_own[slots * 12, 0]
        lives = [(s * n_dp + d < count).astype(F32) for s in range(slots)]
        pieces = step(
            lambda a, b: pair_pieces(
                ids, a, b, [[(1, rows_of[1])] * 2] + [[(1, rows_of[i])] for i in (2, 6, 7, 3)]
            ),
            rest, rest_got,
        )
        pieces = dict(zip((1, 2, 6, 7, 3), pieces))
        x_in = [join((image_tokens[0, s], text_tokens[0, s])) for s in range(slots)]
        c_in = [join((image_cotan[0, s], text_cotan[0, s])) for s in range(slots)]
        sync(pairs[0])
        quads = [gather_one(pairs[0])]
        sync(pairs[4], quads[0])
        quads.append(gather_one(pairs[4]))
        pairs[1] = turned(pieces[1])
        sync(quads[1], mod_own, x_own[0])
        ready = z_pair(x_own[0])
        mod_ready = z_pair(mod_own)
        quads = [corner(a, s) for s, a in enumerate(quads)]
        mod_pair = mod_ready()
        sync(quads)
        xs = [ready()]
        pairs[2] = turned(pieces[2])
        wq = [assemble(a) for a in quads]
        mod_full = jnp.concatenate(mod_pair, 1)
        sync(pairs[1])
        if n_dp == 2:
            outs = gather_one(pairs[1])
        firsts = [first_part(0)]
        sync(outs if n_dp == 2 else (), pairs[2])
        if n_dp == 2:
            outs = [corner(tuple(a[s : s + 1] for a in outs), s) for s in range(2)]
        else:
            outs = [gather_one(pairs[1][s : s + 1]) for s in range(2)]
        expand = [gather_one(pairs[2])]
        x_own += [turned(a) for a in x_in[1:]]
        lses = [mixing(0)]
        sync(outs, x_own, expand[0])
        wo = [flat(assemble(a)) for a in outs]
        pairs[6] = turned(pieces[6])
        ready = [z_pair(x_own[s]) for s in range(1, slots)]
        keep, give = step(lambda a: out_project(ids, a, *wo, image_len), lses[0][0])
        half = half_start(keep, give)
        sync(ready and x_own)
        xs += [a() for a in ready]
        mine = half()
        sums = [(mine, over_z(mine))]
        sync(pairs[6])
        expand.append(gather_one(pairs[6]))
        pairs[7] = turned(pieces[7])
        atts, mids, mlps, c_own, cots = [], [], [], [], []
        for s in range(1, slots):
            firsts.append(first_part(s))
            if s == 1:
                sync(expand[1], pairs[7])
                expand = [corner(a, e) for e, a in enumerate(expand)]
                reduce = [None, gather_one(pairs[7])]
                pairs[3] = turned(pieces[3])
            lses.append(mixing(s))
            sync(sums[s - 1], pairs[3], reduce[1], expand)
            atts.append(full_sum(*sums[s - 1]))
            if s == 1:
                c_own.append(turned(c_in[0]))
                w1 = [flat(assemble(a)) for a in expand]
                reduce[0] = gather_one(pairs[3])
                c_own += [turned(a) for a in c_in[1:]]
            keep, give = step(lambda a: out_project(ids, a, *wo, image_len), lses[s][0])
            mine = half_sum(keep, give)
            if s == 1:
                sync(c_own[0])
                cots = [z_pair(c_own[0])]
            sums.append((mine, over_z(mine)))
        sync(reduce[0])
        reduce = [corner(a, s) for s, a in enumerate(reduce)]
        cs = [cots[0]()]
        cots += [z_pair(c_own[s]) for s in range(1, slots)]
        mids.append(middle(0))
        sync(reduce)
        w2 = [flat(assemble(a)) for a in reduce]

        lefts_text, rights_text = {}, {}

        def text_left(k):
            def halves(a):
                part = a.shape[1] // 2
                return (
                    lax.dynamic_slice_in_dim(a, d * part, part, 1),
                    lax.dynamic_slice_in_dim(a, (1 - d) * part, part, 1),
                )

            mine, away = step(halves, lefts_text[k])
            return mine, over_y(away)

        def text_right(k):
            return rights_text[k], over_y(rights_text[k])

        def text_grad(k):
            def product(left, left_got, right, right_got):
                left = jnp.concatenate([left, left_got], 0)
                right = jnp.concatenate([right, right_got], right.ndim - 2)
                if right.ndim == 3:
                    return jnp.einsum("td,ctf->cdf", left, right, preferred_element_type=F32).astype(BF)
                return mm(left, right, TN).astype(BF)[None]

            return turned(step(product, *text_lefts[k], *text_rights[k]))

        def give_half(k, stream=0):
            left, right, height = ((lefts, rights, image_len), (lefts_text, rights_text, slots * text_rows))[stream]
            left, right = (a[k] if isinstance(a[k], list) else [a[k]] for a in (left, right))
            return over_y(step(lambda a: weight_grad(ids, 4, a, right, height), left))

        def keep_half(k, got, stream=0, need=()):
            left, right, height = ((lefts, rights, image_len), (lefts_text, rights_text, slots * text_rows))[stream]
            left, right = (a[k] if isinstance(a[k], list) else [a[k]] for a in (left, right))
            return turned(step(lambda a: weight_grad(ids, 3, a, right, height, got), left, need=need))

        def whole_grads(k):
            def one(left, right):
                if right.ndim == 3:
                    return jnp.einsum("td,ctf->cdf", left, right, preferred_element_type=F32)
                return mm(left, right, TN)[None]

            image = sum(one(a[:image_len], b[..., :image_len, :]) for a, b in zip(lefts[k], rights[k]))
            text = one(lefts_text[k], rights_text[k])
            return [
                turn(lax.psum_scatter(a.astype(BF), "dp", scatter_dimension=1, tiled=True)) for a in (image, text)
            ]

        two_way = n_dp == 2
        sent, text_lefts, text_rights, grads = {}, {}, {}, {}
        lefts, rights, backs, gqkvs, gh1_mine, branch_mine = {}, {}, [], [], [], []

        def backward(s, need=()):
            backs.append(
                step(
                    lambda a, b: back_prepare(
                        ids, lives[s].reshape(1), a, b, *atts[s], *cs[s], *gh2s[s], mod_full, *wo, *places[s]
                    ),
                    *xs[s],
                    need=need,
                )
            )

        def unmix(s, need=()):
            gqkvs.append(
                step(
                    lambda a, b: attend_back(a, b, lses[s][1], length, image_len),
                    firsts[s][1], backs[s][1],
                    need=need,
                )
            )

        def to_input(s, need=()):
            out = step(lambda a: input_partial(ids, a, *wq, image_len), gqkvs[s], need=need)
            gh1_mine.append(own_part(half_sum(*out)))

        def to_branch(s):
            branch_mine.append(own_part(half_sum(mlps[s][2], mlps[s][3])))

        results, grads_x, modgrads, gates = [], [], [], []

        def row_results(s):
            def first(here, got):
                branch = own_sum(here, got)
                res = (mids[s][2] + per_row(5, s) * branch).astype(BF)
                return res, column_sums(c_own[s].astype(F32) * lives[s] * branch)

            res, gate = step(first, *branch_mine[s])
            results.append(turned(res))
            gates.append(gate)

        def row_sums(s):
            _, _, n1o, _ = firsts[s]

            def first(here, got):
                gh1 = own_sum(here, got)
                q = gh1 * (1.0 + per_row(1, s))
                total = jnp.stack([jnp.sum(q, 1), jnp.sum(q * n1o, 1)])
                sums = jnp.sum(backs[s][3].reshape(2, 3, 8, local), 2)
                mods = jnp.stack(
                    [column_sums(gh1), column_sums(gh1 * n1o), sums[:, 2], sums[:, 0], sums[:, 1], gates[s]]
                )
                return total, mods

            total, mods = step(first, *gh1_mine[s])
            modgrads.append(mods)
            return total, over_z(total)

        def row_total(total, got):
            total = step(jnp.add, total, got)
            return total, send(core_swap, total)

        def row_grads(s, total, got):
            _, _, n1o, inv1 = firsts[s]

            def second(total, got, here, away):
                total = (total + got) / width
                q = own_sum(here, away) * (1.0 + per_row(1, s))
                gx = backs[s][2] + inv1[:, :1] * (q - total[0][:, None] - n1o * total[1][:, None])
                return gx.astype(BF)

            grads_x.append(turned(step(second, total, got, *gh1_mine[s])))

        fresh, outer, waiting = [None] * 8, [None] * 8, {}
        inv_count = (1.0 / group_counts[0].astype(F32)).reshape(1)

        updates = {}

        def optimize(idx):
            moment = lead_form(moments[idx][0])
            lead, rows, cols = moment.shape[1:]
            piece = rows // n_group
            new, keep, give = step(
                lambda grad: adam(ids, inv_count, moment.reshape(2, lead, n_group, piece, cols), grad),
                grads[idx].reshape(lead, n_group, piece, cols),
            )
            updates[idx] = keep, send(core_swap, give)
            new = new.reshape(2, lead, rows, cols)
            fresh[idx] = new.transpose(0, 2, 1, 3)[None] if moments[idx].ndim == 5 else new[:, 0][None]

        def finish(idx):
            keep, got = updates[idx]
            out = step(
                lambda a: outer_step(ids, lead_form(states[idx]), keep, got, a, n_group), waiting[idx]
            )
            outer[idx] = out.transpose(0, 2, 1, 3) if moments[idx].ndim == 5 else out[:, 0]

        def fill_dense():
            lefts.update({3: [a[0] for a in mlps], 2: [a[0] for a in mids], 1: [a[0] for a in lses], 0: [a[0] for a in firsts]})
            rights.update({3: [a[1] for a in mids], 2: [a[1] for a in mlps]})

        def fill_mixing():
            rights[1] = [a[0] for a in backs]
            rights[0] = gqkvs
            lefts_text[0] = step(text_of, lefts[0])
            rights_text[0] = step(text_of, gqkvs)
            lefts_text[1] = step(text_of, [a[0] for a in lses])
            rights_text[1] = step(text_of, rights[1])

        def fill_text(k):
            lefts_text[k] = step(text_of, lefts[k])
            rights_text[k] = step(text_of, rights[k])

        mlps.append(dense(0))
        sync(sums[-1], cots and c_own)
        gh_sums = []

        def gh_half(s):
            mine = half_sum(mlps[s][4], mlps[s][5])
            gh_sums.append((mine, over_z(mine)))

        def small_sum(idx):
            keep, got = updates[idx]
            pick = lambda a: lax.dynamic_index_in_dim(a, 1 - xc, 0, False)
            far = over_x(
                step(lambda a, b: (pick(a).astype(F32) + pick(b).astype(F32)).astype(BF), keep, got)
            )
            waiting[idx] = far

        if two_way and slots == 2:
            gh, br = half_start(mlps[0][4], mlps[0][5]), half_start(mlps[0][2], mlps[0][3])
            atts.append(full_sum(*sums[1]))
            mine = gh()
            gh_sums.append((mine, over_z(mine)))
            cs.append(cots[1]())
            branch_mine.append(own_part(br()))
            mids.append(middle(1))
            mlps.append(dense(1))
            sync(gh_sums[0], branch_mine[0])
            gh, br = half_start(mlps[1][4], mlps[1][5]), half_start(mlps[1][2], mlps[1][3])
            gh2s = [full_sum(*gh_sums[0])]
            fill_dense()
            fill_text(3)
            text_lefts[3] = text_left(3)
            text_rights[3] = text_right(3)
            mine = gh()
            gh_sums.append((mine, over_z(mine)))
            row_results(0)
            branch_half = br()
            backward(0)
            sync(text_lefts[3], text_rights[3], results[0])
            fill_text(2)
            text_rights[2] = text_right(2)
            text_lefts[2] = text_left(2)
            grads[7] = text_grad(3)
            sent[3] = give_half(3)
            sync(gh_sums[1], text_rights[2])
            gh2s.append(full_sum(*gh_sums[1]))
            branch_mine.append(own_part(branch_half))
            sent[2] = give_half(2)
            unmix(0)
            sync(text_lefts[2], grads[7], branch_mine[1])
            grads[6] = text_grad(2)
            row_results(1)
            out = step(lambda a: input_partial(ids, a, *wq, image_len), gqkvs[0])
            half = half_start(*out)
            optimize(7)
            gh1_mine.append(own_part(half()))
            small_sum(7)
            sync(sent[3])
            grads[3] = keep_half(3, sent[3])
            backward(1)
            sync(gh1_mine[0], waiting[7], grads[6])
            totals = [row_sums(0)]
            finish(7)
            totals[0] = row_total(*totals[0])
            unmix(1)
            sync(sent[2], results[1])
            grads[2] = keep_half(2, sent[2])
            row_grads(0, *totals[0])
            out = step(lambda a: input_partial(ids, a, *wq, image_len), gqkvs[1])
            half = half_start(*out)
            optimize(6)
            gh1_mine.append(own_part(half()))
            small_sum(6)
            fill_mixing()
            text_lefts[0] = text_left(0)
            text_rights[0] = text_right(0)
            sent[0] = give_half(0)
            sync(grads[3], waiting[6], gh1_mine[1])
            optimize(3)
            sent[5] = give_half(1, 1)
            sent[1] = give_half(1)
            small_sum(3)
            totals.append(row_sums(1))
            finish(6)
            totals[1] = row_total(*totals[1])
            sync(text_lefts[0], text_rights[0])
            grads[4] = text_grad(0)
            sync(grads[2], waiting[3])
            optimize(2)
            finish(3)
            row_grads(1, *totals[1])
            small_sum(2)
            sync(sent[0])
            grads[0] = keep_half(0, sent[0])
            sync(sent[5], sent[1])
            grads[5] = keep_half(1, sent[5], 1)
            grads[1] = keep_half(1, sent[1])
            finish(2)
            sync(grads[4])
            optimize(4)
            sync(grads[0])
            optimize(0)
            small_sum(4)
            small_sum(0)
            optimize(5)
            optimize(1)
            small_sum(5)
            small_sum(1)
            for i in (4, 0, 5, 1):
                finish(i)
        else:
            for s in range(1, slots):
                atts.append(full_sum(*sums[s]))
                cs.append(cots[s]())
                mids.append(middle(s))
                mlps.append(dense(s))
            fill_dense()
            for s in range(slots):
                gh_half(s)
            gh2s = [full_sum(*a) for a in gh_sums]
            for s in range(slots):
                backward(s)
                unmix(s)
                to_input(s)
                to_branch(s)
                row_results(s)
                row_grads(s, *row_total(*row_sums(s)))
            fill_mixing()
            fill_text(2)
            fill_text(3)
            for k in (3, 2, 1, 0):
                grads[k], grads[k + 4] = whole_grads(k)
            for i in range(8):
                optimize(i)
                small_sum(i)
                finish(i)
        mod_back = turn(jnp.stack(modgrads).reshape(slots * 12, local)).reshape(slots, 6, 2, local)

        res = jnp.stack(results)
        gx = jnp.stack(grads_x)
        return (
            res[None, :, :image_len],
            res[None, :, image_len:length],
            gx[None, :, :image_len],
            gx[None, :, image_len:length],
            mod_back[None, :, :, 0],
            mod_back[None, :, :, 1],
            *fresh,
            *outer,
        )

    tokens = P("group", "dp", None, "mp")
    weight_specs = (
        P(None, ("dp", "group"), None, "mp"),
        P(None, ("mp", "dp", "group"), None),
        P(None, ("dp", "group"), "mp"),
        P(None, ("mp", "dp", "group"), None),
    ) * 2
    moment_specs = (
        P("group", None, "dp", None, "mp"),
        P("group", None, ("mp", "dp"), None),
        P("group", None, "dp", "mp"),
        P("group", None, ("mp", "dp"), None),
    ) * 2
    return jax.shard_map(
        body,
        mesh=mesh,
        in_specs=(tokens,) * 6 + (P("group"),) + weight_specs + moment_specs,
        out_specs=(tokens,) * 6 + moment_specs + weight_specs,
        check_vma=False,
    )
```

```python
import jax
import jax.numpy as jnp
from jax import lax
from jax.experimental import pallas as pl
from jax.experimental.pallas import tpu as pltpu
from jax.sharding import PartitionSpec as P

BF = jnp.bfloat16
F32 = jnp.float32
EPS_NORM = 1e-06
STEP = 3
BETA_ONE = 0.9
BETA_TWO = 0.95
ADAM_EPS = 1e-08
LEARN_RATE = 0.02
DECAY_RATE = 0.1
OUTER_RATE = 0.7
OUTER_MOMENT = 0.9
BLOCK = 256
VMEM_BYTES = 60 * 1024 * 1024
COST_SHARE = 1000
NT = (((1,), (1,)), ((), ()))
NN = (((1,), (0,)), ((), ()))
TN = (((0,), (0,)), ((), ()))


def mm(a, b, dims=NN):
    return lax.dot_general(a, b, dims, preferred_element_type=F32)


def cost(flops, nbytes):
    return pl.CostEstimate(
        flops=int(flops) // COST_SHARE, bytes_accessed=int(nbytes) // COST_SHARE, transcendentals=0
    )


def call(kernel, grid, in_specs, out_specs, out_shape, flops, nbytes, scratch=(), prefetch=1):
    return pl.pallas_call(
        kernel,
        grid_spec=pltpu.PrefetchScalarGridSpec(
            num_scalar_prefetch=prefetch,
            grid=grid,
            in_specs=in_specs,
            out_specs=out_specs,
            scratch_shapes=list(scratch),
        ),
        out_shape=out_shape,
        compiler_params=pltpu.CompilerParams(
            vmem_limit_bytes=VMEM_BYTES, dimension_semantics=("arbitrary",) * len(grid)
        ),
        cost_estimate=cost(flops, nbytes),
    )


def rows_spec(width):
    return pl.BlockSpec((BLOCK, width), lambda i, *_: (i, 0))


def whole(shape):
    return pl.BlockSpec(shape, lambda *_: (0,) * len(shape), pipeline_mode=pl.Buffered(1))


def struct(shape, dtype):
    return jax.ShapeDtypeStruct(shape, dtype)


def cast_states(states):
    cols = states[0].shape[-1]
    sizes = [s.shape[1] * s.shape[2] for s in states]

    def kernel(*refs):
        out_ref, at = refs[-1], 0
        for ref, state in zip(refs, states):
            for lead in range(state.shape[1]):
                rows = state.shape[2]
                out_ref[at : at + rows, :] = ref[0, lead].astype(BF)
                at += rows

    return call(
        kernel,
        (1,),
        [pl.BlockSpec((1,) + s.shape[1:], lambda *_: (0, 0, 0, 0), pipeline_mode=pl.Buffered(1)) for s in states],
        whole((sum(sizes), cols)),
        struct((sum(sizes), cols), BF),
        sum(sizes) * cols,
        sum(sizes) * cols * 6,
        prefetch=0,
    )(*states)


def pair_pieces(ids, mine, other, shapes):
    cols = mine.shape[1]

    def kernel(ids_ref, m_ref, o_ref, *out_refs):
        def lay(first_ref, second_ref):
            at = 0
            for out_ref, group in zip(out_refs, shapes):
                for k, (lead, rows) in enumerate(group):
                    for j in range(lead):
                        out_ref[k * lead + j, :rows, :] = first_ref[at : at + rows, :]
                        out_ref[k * lead + j, rows:, :] = second_ref[at : at + rows, :]
                        at += rows

        @pl.when(ids_ref[0] == 0)
        def _():
            lay(m_ref, o_ref)

        @pl.when(ids_ref[0] == 1)
        def _():
            lay(o_ref, m_ref)

    outs = [(len(group) * group[0][0], 2 * group[0][1], cols) for group in shapes]
    return call(
        kernel,
        (1,),
        [whole(mine.shape), whole(mine.shape)],
        [whole(s) for s in outs],
        [struct(s, BF) for s in outs],
        mine.size,
        mine.size * 8,
    )(ids, mine, other)


def lay_quads(ids, parts):
    lead, rows, cols = parts[0].shape

    def kernel(ids_ref, *refs):
        copies = []
        for k in range(4):
            at = pl.multiple_of(ids_ref[5 + k] * rows, 16)
            copies.append(pltpu.make_async_copy(refs[k], refs[4].at[:, pl.ds(at, rows), :], refs[5].at[k]))
            copies[-1].start()
        for copy in copies:
            copy.wait()

    return pl.pallas_call(
        kernel,
        in_specs=[pl.BlockSpec(memory_space=pltpu.SMEM)] + [pl.BlockSpec(memory_space=pl.ANY)] * 4,
        out_specs=pl.BlockSpec(memory_space=pl.ANY),
        out_shape=struct((lead, 4 * rows, cols), BF),
        scratch_shapes=[pltpu.SemaphoreType.DMA((4,))],
        compiler_params=pltpu.CompilerParams(vmem_limit_bytes=1024 * 1024),
        cost_estimate=cost(0, lead * rows * cols * 16),
    )(ids, *parts)


def ln_qkv(ids, xm, xo, mod, wi, wt, image_len, image_row, text_row):
    rows, half = xm.shape
    width, local = 2 * half, half // 2
    cols = 3 * local
    image_blocks = image_len // BLOCK

    def kernel(ids_ref, xm_ref, xo_ref, mod_ref, wi_ref, wt_ref, h_ref, qkv_ref, n_ref, inv_ref):
        i = pl.program_id(0)
        base = jnp.where(i < image_blocks, image_row, text_row)
        shift = mod_ref[pl.ds(base, 1), :]
        scale = 1.0 + mod_ref[pl.ds(base + 1, 1), :]
        first = ids_ref[1] == 0
        here = pl.ds(pl.multiple_of(ids_ref[0] * half, 128), half)
        there = pl.ds(pl.multiple_of((1 - ids_ref[0]) * half, 128), half)

        def chunk(r, carry):
            at = pl.ds(pl.multiple_of(r * 32, 32), 32)
            a = xm_ref[at, :].astype(F32)
            b = xo_ref[at, :].astype(F32)
            mean = (jnp.sum(a, 1, keepdims=True) + jnp.sum(b, 1, keepdims=True)) / width
            a, b = a - mean, b - mean
            var = (jnp.sum(a * a, 1, keepdims=True) + jnp.sum(b * b, 1, keepdims=True)) / width
            inv = lax.rsqrt(var + EPS_NORM)
            a, b = a * inv, b * inv
            n_ref[at, :] = jnp.where(first, a[:, :local], a[:, local:])
            inv_ref[at, :] = jnp.broadcast_to(inv, (32, 128))
            h_ref[at, here] = (a * scale[:, :half] + shift[:, :half]).astype(BF)
            h_ref[at, there] = (b * scale[:, half:] + shift[:, half:]).astype(BF)
            return carry

        lax.fori_loop(0, BLOCK // 32, chunk, 0, unroll=BLOCK // 32)

        def project(w_ref):
            for j in range(3):
                qkv_ref[j] = mm(h_ref[...], w_ref[j]).astype(BF)

        @pl.when(i < image_blocks)
        def _():
            project(wi_ref)

        @pl.when(i >= image_blocks)
        def _():
            project(wt_ref)

    return call(
        kernel,
        (pl.cdiv(rows, BLOCK),),
        [rows_spec(half), rows_spec(half), whole(mod.shape), whole(wi.shape), whole(wt.shape)],
        [
            rows_spec(width),
            pl.BlockSpec((3, BLOCK, local), lambda i, *_: (0, i, 0)),
            rows_spec(local),
            rows_spec(128),
        ],
        [
            struct((rows, width), BF),
            struct((3, rows, local), BF),
            struct((rows, local), F32),
            struct((rows, 128), F32),
        ],
        2 * rows * width * cols,
        rows * width * 6 + 4 * width * cols,
    )(ids, xm, xo, mod, wi, wt)


def pair_mask(array, head, dim):
    lane = lax.broadcasted_iota(jnp.int32, array.shape, 1)
    return jnp.where(lane // dim == head, array, jnp.zeros_like(array))


def q_chunks(rows, image_len):
    return [(s, BLOCK) for s in range(0, image_len, BLOCK)] + [(image_len, rows - image_len)]


def attend(qkv, length, image_len, dim=64):
    _, rows, local = qkv.shape
    pairs = local // 128
    lanes = pl.cdiv(rows, BLOCK) * BLOCK
    tail = length // 8 * 8
    scale = dim**-0.5

    def kernel(qkv_ref, out_ref, lse_ref, s_ref):
        for start, size in q_chunks(rows, image_len):
            total = None
            for head in range(128 // dim):
                q = pair_mask(qkv_ref[0, start : start + size, :], head, dim) * jnp.asarray(scale, BF)
                s_ref[:, :size] = mm(qkv_ref[1], q, NT)
                if tail < rows:
                    last = s_ref[tail:, :size]
                    row = lax.broadcasted_iota(jnp.int32, last.shape, 0) + tail
                    s_ref[tail:, :size] = jnp.where(row < length, last, -1e30)
                s = s_ref[:, :size]
                top = jnp.max(s, 0, keepdims=True)
                e = jnp.exp(s - top)
                norm = jnp.sum(e, 0, keepdims=True)
                lse_ref[0, head : head + 1, start : start + size] = top + jnp.log(norm)
                p = (e * (1.0 / norm)).astype(BF)
                mix = mm(p, pair_mask(qkv_ref[2], head, dim), TN)
                total = mix if total is None else total + mix
            out_ref[start : start + size, :] = total.astype(BF)

    return pl.pallas_call(
        kernel,
        grid=(pairs,),
        in_specs=[pl.BlockSpec((3, rows, 128), lambda j: (0, 0, j))],
        out_specs=[
            pl.BlockSpec((rows, 128), lambda j: (0, j)),
            pl.BlockSpec((1, 8, lanes), lambda j: (j, 0, 0)),
        ],
        out_shape=[struct((rows, local), BF), struct((pairs, 8, lanes), F32)],
        scratch_shapes=[pltpu.VMEM((rows, BLOCK), F32)],
        compiler_params=pltpu.CompilerParams(vmem_limit_bytes=VMEM_BYTES),
        cost_estimate=cost(16 * rows * rows * local, rows * local * 8),
    )(qkv)


def attend_back(qkv, grad, lse, length, image_len, dim=64):
    _, rows, local = qkv.shape
    pairs = local // 128
    lanes = lse.shape[2]
    tail = length // 8 * 8
    scale = dim**-0.5

    def kernel(qkv_ref, grad_ref, lse_ref, out_ref, s_ref, gk_ref, gv_ref):
        gk_ref[...] = jnp.zeros_like(gk_ref)
        gv_ref[...] = jnp.zeros_like(gv_ref)
        for start, size in q_chunks(rows, image_len):
            total = None
            for head in range(128 // dim):
                q = pair_mask(qkv_ref[0, start : start + size, :], head, dim) * jnp.asarray(scale, BF)
                gm = pair_mask(grad_ref[start : start + size, :], head, dim)
                s_ref[:, :size] = mm(qkv_ref[1], q, NT)
                if tail < rows:
                    last = s_ref[tail:, :size]
                    row = lax.broadcasted_iota(jnp.int32, last.shape, 0) + tail
                    s_ref[tail:, :size] = jnp.where(row < length, last, -1e30)
                p = jnp.exp(s_ref[:, :size] - lse_ref[0, head : head + 1, start : start + size])
                gv_ref[...] += mm(p.astype(BF), gm)
                gp = mm(qkv_ref[2], gm, NT)
                delta = jnp.sum(p * gp, 0, keepdims=True)
                gs = (p * (gp - delta)).astype(BF)
                gk_ref[...] += mm(gs, q)
                gq = mm(gs, pair_mask(qkv_ref[1], head, dim), TN)
                total = gq if total is None else total + gq
            out_ref[0, start : start + size, :] = (total * scale).astype(BF)
        out_ref[1] = gk_ref[...].astype(BF)
        out_ref[2] = gv_ref[...].astype(BF)

    return pl.pallas_call(
        kernel,
        grid=(pairs,),
        in_specs=[
            pl.BlockSpec((3, rows, 128), lambda j: (0, 0, j)),
            pl.BlockSpec((rows, 128), lambda j: (0, j)),
            pl.BlockSpec((1, 8, lanes), lambda j: (j, 0, 0)),
        ],
        out_specs=pl.BlockSpec((3, rows, 128), lambda j: (0, 0, j)),
        out_shape=struct((3, rows, local), BF),
        scratch_shapes=[
            pltpu.VMEM((rows, BLOCK), F32),
            pltpu.VMEM((rows, 128), F32),
            pltpu.VMEM((rows, 128), F32),
        ],
        compiler_params=pltpu.CompilerParams(vmem_limit_bytes=VMEM_BYTES),
        cost_estimate=cost(40 * rows * rows * local, rows * local * 14),
    )(qkv, grad, lse)


def out_project(ids, mixed, wi, wt, image_len):
    rows, local = mixed.shape
    width = wi.shape[1]
    half = width // 2
    image_blocks = image_len // BLOCK

    def kernel(ids_ref, a_ref, wi_ref, wt_ref, keep_ref, send_ref):
        i = pl.program_id(0)
        here = pl.ds(pl.multiple_of(ids_ref[0] * half, 128), half)
        there = pl.ds(pl.multiple_of((1 - ids_ref[0]) * half, 128), half)

        def project(w_ref):
            keep_ref[...] = mm(a_ref[...], w_ref[:, here]).astype(BF)
            send_ref[...] = mm(a_ref[...], w_ref[:, there]).astype(BF)

        @pl.when(i < image_blocks)
        def _():
            project(wi_ref)

        @pl.when(i >= image_blocks)
        def _():
            project(wt_ref)

    return call(
        kernel,
        (pl.cdiv(rows, BLOCK),),
        [rows_spec(local), whole(wi.shape), whole(wt.shape)],
        [rows_spec(half), rows_spec(half)],
        [struct((rows, half), BF), struct((rows, half), BF)],
        2 * rows * width * local,
        rows * width * 3 + 4 * width * local,
    )(ids, mixed, wi, wt)


def input_partial(ids, gqkv, wi, wt, image_len):
    _, rows, local = gqkv.shape
    width = wi.shape[1]
    half = width // 2
    image_blocks = image_len // BLOCK

    def kernel(ids_ref, a_ref, wi_ref, wt_ref, keep_ref, send_ref):
        i = pl.program_id(0)
        here = pl.ds(pl.multiple_of(ids_ref[0] * half, 128), half)
        there = pl.ds(pl.multiple_of((1 - ids_ref[0]) * half, 128), half)

        def project(w_ref):
            for out_ref, lo in ((keep_ref, here), (send_ref, there)):
                total = None
                for j in range(3):
                    part = mm(a_ref[j], w_ref[j, lo, :], NT)
                    total = part if total is None else total + part
                out_ref[...] = total.astype(BF)

        @pl.when(i < image_blocks)
        def _():
            project(wi_ref)

        @pl.when(i >= image_blocks)
        def _():
            project(wt_ref)

    return call(
        kernel,
        (pl.cdiv(rows, BLOCK),),
        [pl.BlockSpec((3, BLOCK, local), lambda i, *_: (0, i, 0)), whole(wi.shape), whole(wt.shape)],
        [rows_spec(half), rows_spec(half)],
        [struct((rows, half), BF), struct((rows, half), BF)],
        2 * rows * width * local * 3,
        rows * width * 5 + 12 * width * local,
    )(ids, gqkv, wi, wt)


def after_norm(xa, xb, aa, ab, gate, half, width):
    a = xa.astype(F32) + gate[:, :half] * aa.astype(F32)
    b = xb.astype(F32) + gate[:, half:] * ab.astype(F32)
    mean = (jnp.sum(a, 1, keepdims=True) + jnp.sum(b, 1, keepdims=True)) / width
    ca, cb = a - mean, b - mean
    var = (jnp.sum(ca * ca, 1, keepdims=True) + jnp.sum(cb * cb, 1, keepdims=True)) / width
    inv = lax.rsqrt(var + EPS_NORM)
    return a, ca * inv, cb * inv, inv


def mid_prepare(ids, live, xm, xo, am, ao, cm, co, mod, image_len, image_row, text_row):
    rows, half = xm.shape
    width, local = 2 * half, half // 2
    image_blocks = image_len // BLOCK
    step = 32

    def kernel(ids_ref, live_ref, xm_ref, xo_ref, am_ref, ao_ref, cm_ref, co_ref, mod_ref, h_ref, g_ref, own_ref):
        i = pl.program_id(0)
        base = jnp.where(i < image_blocks, image_row, text_row)
        gate_a = mod_ref[pl.ds(base + 2, 1), :]
        shift = mod_ref[pl.ds(base + 3, 1), :]
        scale = 1.0 + mod_ref[pl.ds(base + 4, 1), :]
        gate_m = mod_ref[pl.ds(base + 5, 1), :] * live_ref[0]
        first = ids_ref[1] == 0
        here = pl.ds(pl.multiple_of(ids_ref[0] * half, 128), half)
        there = pl.ds(pl.multiple_of((1 - ids_ref[0]) * half, 128), half)

        def chunk(r, carry):
            at = pl.ds(pl.multiple_of(r * step, step), step)
            a, na, nb, _ = after_norm(xm_ref[at, :], xo_ref[at, :], am_ref[at, :], ao_ref[at, :], gate_a, half, width)
            own_ref[at, :] = jnp.where(first, a[:, :local], a[:, local:])
            h_ref[at, here] = (na * scale[:, :half] + shift[:, :half]).astype(BF)
            h_ref[at, there] = (nb * scale[:, half:] + shift[:, half:]).astype(BF)
            g_ref[at, here] = (cm_ref[at, :].astype(F32) * gate_m[:, :half]).astype(BF)
            g_ref[at, there] = (co_ref[at, :].astype(F32) * gate_m[:, half:]).astype(BF)
            return carry

        lax.fori_loop(0, BLOCK // step, chunk, 0, unroll=BLOCK // step)

    return call(
        kernel,
        (pl.cdiv(rows, BLOCK),),
        [rows_spec(half)] * 6 + [whole(mod.shape)],
        [rows_spec(width), rows_spec(width), rows_spec(local)],
        [struct((rows, width), BF), struct((rows, width), BF), struct((rows, local), F32)],
        rows * width * 20,
        rows * width * 11,
        prefetch=2,
    )(ids, live, xm, xo, am, ao, cm, co, mod)


def gelu_pair(v):
    k, c3 = 0.7978845608028654, 0.044715
    v2 = v * v
    t = jnp.tanh(k * v * (1.0 + c3 * v2))
    up = 0.5 * (1.0 + t)
    return v * up, up + 0.5 * v * (1.0 - t * t) * (k * (1.0 + 3.0 * c3 * v2))


def mlp(ids, h, g, w1i, w1t, w2i, w2t, image_len, tile=512):
    rows, width = h.shape
    half = width // 2
    hidden = w1i.shape[1]
    steps = hidden // tile
    piece = 512

    def kernel(
        ids_ref, h_ref, g_ref, w1i_ref, w1t_ref, w2i_ref, w2t_ref,
        act_ref, gin_ref, bk_ref, bs_ref, gk_ref, gs_ref, b_acc, g_acc,
    ):
        i = pl.program_id(0)
        here = pl.ds(pl.multiple_of(ids_ref[0] * half, 128), half)
        there = pl.ds(pl.multiple_of((1 - ids_ref[0]) * half, 128), half)

        def work(at, w1_ref, w2_ref):
            inner = mm(h_ref[at, :], w1_ref[...])
            ag = mm(g_ref[at, :], w2_ref[...], NT)
            act, slope = gelu_pair(inner)
            act = act.astype(BF)
            gin = (ag * slope).astype(BF)
            act_ref[at, :] = act
            gin_ref[at, :] = gin
            parts = ((b_acc, mm(act, w2_ref[...])), (g_acc, mm(gin, w1_ref[...], NT)))

            @pl.when(i == 0)
            def _():
                for ref, value in parts:
                    ref[at, :] = value

            @pl.when(i > 0)
            def _():
                for ref, value in parts:
                    ref[at, :] += value

        def image_piece(r, carry):
            work(pl.ds(pl.multiple_of(r * piece, piece), piece), w1i_ref, w2i_ref)
            return carry

        lax.fori_loop(0, image_len // piece, image_piece, 0)
        work(slice(image_len, rows), w1t_ref, w2t_ref)

        @pl.when(i == steps - 1)
        def _():
            bk_ref[...] = b_acc[:, here].astype(BF)
            bs_ref[...] = b_acc[:, there].astype(BF)
            gk_ref[...] = g_acc[:, here].astype(BF)
            gs_ref[...] = g_acc[:, there].astype(BF)

    w1_spec = pl.BlockSpec((width, tile), lambda i, *_: (0, i))
    w2_spec = pl.BlockSpec((tile, width), lambda i, *_: (i, 0))
    out_tile = pl.BlockSpec((rows, tile), lambda i, *_: (0, i))
    return call(
        kernel,
        (steps,),
        [whole((rows, width)), whole((rows, width)), w1_spec, w1_spec, w2_spec, w2_spec],
        [out_tile, out_tile] + [whole((rows, half))] * 4,
        [struct((rows, hidden), BF)] * 2 + [struct((rows, half), BF)] * 4,
        8 * rows * width * hidden,
        rows * width * 12 + 8 * width * hidden,
        scratch=[pltpu.VMEM((rows, width), F32), pltpu.VMEM((rows, width), F32)],
    )(ids, h, g, w1i, w1t, w2i, w2t)


def back_prepare(ids, live, xm, xo, am, ao, cm, co, gm, go, mod, wi, wt, image_len, image_row, text_row):
    rows, half = xm.shape
    width, local = 2 * half, half // 2
    image_blocks = image_len // BLOCK
    step = 32

    def kernel(
        ids_ref, live_ref, xm_ref, xo_ref, am_ref, ao_ref, cm_ref, co_ref, gm_ref, go_ref, mod_ref, wi_ref, wt_ref,
        ga_ref, gmix_ref, own_ref, sums_ref,
    ):
        i = pl.program_id(0)
        base = jnp.where(i < image_blocks, image_row, text_row)
        gate_a = mod_ref[pl.ds(base + 2, 1), :]
        scale = 1.0 + mod_ref[pl.ds(base + 4, 1), :]
        first = ids_ref[1] == 0
        live_now = live_ref[0]
        here = pl.ds(pl.multiple_of(ids_ref[0] * half, 128), half)
        there = pl.ds(pl.multiple_of((1 - ids_ref[0]) * half, 128), half)

        @pl.when((i == 0) | (i == image_blocks))
        def _():
            sums_ref[...] = jnp.zeros_like(sums_ref)

        def own(v):
            return jnp.where(first, v[:, :local], v[:, local:])

        def chunk(r, carry):
            at = pl.ds(pl.multiple_of(r * step, step), step)
            _, na, nb, inv = after_norm(xm_ref[at, :], xo_ref[at, :], am_ref[at, :], ao_ref[at, :], gate_a, half, width)
            ga = gm_ref[at, :].astype(F32)
            gb = go_ref[at, :].astype(F32)
            qa, qb = ga * scale[:, :half], gb * scale[:, half:]
            mean = (jnp.sum(qa, 1, keepdims=True) + jnp.sum(qb, 1, keepdims=True)) / width
            cross = (jnp.sum(qa * na, 1, keepdims=True) + jnp.sum(qb * nb, 1, keepdims=True)) / width
            fa = cm_ref[at, :].astype(F32) * live_now + inv * (qa - mean - na * cross)
            fb = co_ref[at, :].astype(F32) * live_now + inv * (qb - mean - nb * cross)
            ga_ref[at, here] = (gate_a[:, :half] * fa).astype(BF)
            ga_ref[at, there] = (gate_a[:, half:] * fb).astype(BF)
            fo, go_own = own(fa), own(ga)
            own_ref[at, :] = fo
            row = i * BLOCK + r * step + lax.broadcasted_iota(jnp.int32, (step, local), 0)
            inside = row < rows
            for k, value in enumerate((go_own, go_own * own(na), fo * own(am_ref[at, :].astype(F32)))):
                value = jnp.where(inside, value, 0.0)
                sums_ref[0, k * 8 : (k + 1) * 8, :] += jnp.sum(value.reshape(step // 8, 8, local), 0)
            return carry

        lax.fori_loop(0, BLOCK // step, chunk, 0, unroll=BLOCK // step)

        def project(w_ref):
            gmix_ref[...] = mm(ga_ref[...], w_ref[...], NT).astype(BF)

        @pl.when(i < image_blocks)
        def _():
            project(wi_ref)

        @pl.when(i >= image_blocks)
        def _():
            project(wt_ref)

    return call(
        kernel,
        (pl.cdiv(rows, BLOCK),),
        [rows_spec(half)] * 8 + [whole(mod.shape), whole(wi.shape), whole(wt.shape)],
        [
            rows_spec(width),
            rows_spec(local),
            rows_spec(local),
            pl.BlockSpec((1, 24, local), lambda i, *_: (jnp.where(i < image_blocks, 0, 1), 0, 0)),
        ],
        [
            struct((rows, width), BF),
            struct((rows, local), BF),
            struct((rows, local), F32),
            struct((2, 24, local), F32),
        ],
        2 * rows * width * local,
        rows * width * 12,
        prefetch=2,
    )(ids, live, xm, xo, am, ao, cm, co, gm, go, mod, wi, wt)


def grad_specs(right, tile, height, row_block):
    if right.ndim == 3:
        return (
            pl.BlockSpec((1, height, right.shape[2]), lambda j, *_: (j, row_block, 0)),
            right.shape[0],
            right.shape[2],
        )
    return pl.BlockSpec((height, tile), lambda j, *_: (row_block, j)), right.shape[1] // tile, tile


def grad_out(right, tile, part):
    if right.ndim == 3:
        lead, _, cols = right.shape
        return pl.BlockSpec((1, part, cols), lambda j, *_: (j, 0, 0)), struct((lead, part, cols), BF)
    return (
        pl.BlockSpec((1, part, tile), lambda j, *_: (0, 0, j)),
        struct((1, part, right.shape[1]), BF),
    )


def weight_grad(ids, which, lefts, rights, height, add=None, tile=512):
    part = lefts[0].shape[1] // (1 if which is None else 2)
    n = len(lefts)
    right_spec, steps, _ = grad_specs(rights[0], tile, height, 0)
    narrow = which is not None and part % 128 != 0
    left_spec = pl.BlockSpec(
        (height, 2 * part if narrow else part),
        lambda j, ids_ref: (0, 0 if narrow or which is None else ids_ref[which]),
        pipeline_mode=pl.Buffered(1),
    )
    out_spec, out_shape = grad_out(rights[0], tile, part)
    flat = rights[0].ndim == 2

    def kernel(ids_ref, *refs):
        total = None
        for left_ref, right_ref in zip(refs[:n], refs[n : 2 * n]):
            value = mm(left_ref[...], right_ref[...] if flat else right_ref[0], TN)
            total = value if total is None else total + value
        if narrow:
            total = jnp.where(ids_ref[which] == 0, total[:part], total[part:])
        if add is not None:
            total = total + refs[2 * n][0].astype(F32)
        refs[-1][0] = total.astype(BF)

    more = [] if add is None else [add]
    return call(
        kernel,
        (steps,),
        [left_spec] * n + [right_spec] * n + [out_spec] * len(more),
        out_spec,
        out_shape,
        2 * n * height * part * out_shape.shape[0] * out_shape.shape[2],
        n * height * (part + out_shape.shape[0] * out_shape.shape[2]) * 2,
    )(ids, *lefts, *rights, *more)


def adam(ids, inv_count, moment, near, far):
    _, lead, _, piece, cols = moment.shape
    correct_one = 1.0 - BETA_ONE**STEP
    correct_two = 1.0 - BETA_TWO**STEP

    def kernel(ids_ref, inv_ref, m_ref, near_ref, far_ref, fresh_ref, keep_ref, send_ref):
        t = pl.program_id(0)
        for l in range(lead):
            g = jnp.where(ids_ref[9] == 1, near_ref[l, 0], far_ref[l, 0]).astype(F32) * inv_ref[0]
            first = BETA_ONE * m_ref[0, l, 0] + (1.0 - BETA_ONE) * g
            second = BETA_TWO * m_ref[1, l, 0] + (1.0 - BETA_TWO) * g * g
            fresh_ref[0, l, 0] = first
            fresh_ref[1, l, 0] = second
            update = (first * (1.0 / correct_one) / (jnp.sqrt(second * (1.0 / correct_two)) + ADAM_EPS)).astype(BF)

            @pl.when(t < 2)
            def _(l=l, update=update):
                send_ref[0, l] = update

            @pl.when(t >= 2)
            def _(l=l, update=update):
                keep_ref[0, l] = update

    def block(t, ids_ref):
        return (t % 2) * 2 + jnp.where(t < 2, 1 - ids_ref[0], ids_ref[0])

    pairs = pl.BlockSpec((2, lead, 1, piece, cols), lambda t, ids_ref, _: (0, 0, block(t, ids_ref), 0, 0))
    grad = pl.BlockSpec((lead, 1, piece, cols), lambda t, ids_ref, _: (0, block(t, ids_ref), 0, 0))
    side = struct((2, lead, piece, cols), BF)
    return call(
        kernel,
        (4,),
        [pairs, grad, grad],
        [
            pairs,
            pl.BlockSpec((1, lead, piece, cols), lambda t, *_: (jnp.maximum(t - 2, 0), 0, 0, 0)),
            pl.BlockSpec((1, lead, piece, cols), lambda t, *_: (jnp.minimum(t, 1), 0, 0, 0)),
        ],
        [struct(moment.shape, F32), side, side],
        lead * piece * cols * 80,
        lead * piece * cols * 80,
        prefetch=2,
    )(ids, inv_count, moment, near, far)


def outer_step(ids, state, keep, got, far, groups):
    _, lead, piece, cols = state.shape

    def kernel(ids_ref, s_ref, k_ref, g_ref, f_ref, out_ref):
        near = (k_ref[0].astype(F32) + g_ref[0].astype(F32)).astype(BF).astype(F32)
        total = near + f_ref[...].astype(F32)
        master = s_ref[0]
        delta = LEARN_RATE * (total * (1.0 / groups) + DECAY_RATE * master)
        momentum = OUTER_MOMENT * s_ref[1] + delta
        out_ref[0] = master - OUTER_RATE * (delta + OUTER_MOMENT * momentum)
        out_ref[1] = delta
        out_ref[2] = momentum

    side = pl.BlockSpec((1, lead, piece, cols), lambda i, ids_ref: (ids_ref[2], 0, 0, 0))
    return call(
        kernel,
        (1,),
        [
            pl.BlockSpec((2, lead, piece, cols), lambda i, *_: (0, 0, 0, 0)),
            side,
            side,
            pl.BlockSpec((lead, piece, cols), lambda i, *_: (0, 0, 0)),
        ],
        pl.BlockSpec((3, lead, piece, cols), lambda i, *_: (0, 0, 0, 0)),
        struct((3, lead, piece, cols), F32),
        lead * piece * cols * 10,
        lead * piece * cols * 26,
    )(ids, state, keep, got, far)


def solution(mesh):
    n_group, n_dp, n_mp = mesh.shape["group"], mesh.shape["dp"], mesh.shape["mp"]
    core_perm = [(g, g ^ 1) for g in range(n_group)]
    x_perm = [(g, g ^ 2) for g in range(n_group)]
    z_perm = [(m, m ^ 1) for m in range(n_mp)]
    y_perm = [(d, d ^ 1) for d in range(n_dp)]
    turn_perm = [
        (g * n_mp + m, ((g // 2) * 2 + m // 2) * n_mp + (g % 2) * 2 + m % 2)
        for g in range(n_group)
        for m in range(n_mp)
    ]

    trade_perm = [(i, j if i != j else (i // n_mp ^ 2) * n_mp + i % n_mp) for i, j in turn_perm]

    def core_swap(a):
        return lax.ppermute(a, "group", core_perm)

    def x_swap(a):
        return lax.ppermute(a, "group", x_perm)

    def z_swap(a):
        return lax.ppermute(a, "mp", z_perm)

    def y_swap(a):
        return lax.ppermute(a, "dp", y_perm)

    def turn(a):
        return lax.ppermute(a, ("group", "mp"), turn_perm)

    def trade(a):
        return lax.ppermute(a, ("group", "mp"), trade_perm)

    def by(flag, a, b, axis):
        return jnp.where(flag == 0, jnp.concatenate([a, b], axis), jnp.concatenate([b, a], axis))

    def body(
        image_tokens, text_tokens, image_modulation, text_modulation, image_cotan, text_cotan,
        group_counts, *tensors,
    ):
        states, moments = tensors[:8], tensors[8:]
        g, d, m = lax.axis_index("group"), lax.axis_index("dp"), lax.axis_index("mp")
        c, xc, zl = g % 2, g // 2, m % 2
        place = (d % 2) * 2 + xc
        ids = jnp.stack([c, zl, xc, d % 2, 1 - d % 2, place, place ^ 1, place ^ 2, place ^ 3, c == m // 2]).astype(jnp.int32)

        slots = image_tokens.shape[1]
        image_len, text_len = image_tokens.shape[2], text_tokens.shape[2]
        text_rows = -(-text_len // 32) * 32
        local = image_tokens.shape[3]
        width = local * n_mp
        rows_all = image_len + text_rows
        length = image_len + text_len

        last = []

        def hold(value, others):
            if not others:
                return value
            leaves, tree = jax.tree.flatten(value)
            held = lax.optimization_barrier(tuple(leaves) + tuple(others))
            return jax.tree.unflatten(tree, list(held[: len(leaves)]))

        def step(fn, first, *rest, need=()):
            out = fn(hold(first, last + jax.tree.leaves(need)), *rest)
            last[:] = [jax.tree.leaves(out)[0]]
            return out

        def send(move, value):
            return move(hold(value, last))

        turned, over_x, over_y, over_z = (lambda value, move=move: send(move, value) for move in (turn, x_swap, y_swap, z_swap))
        stays = c == m // 2

        def owned(value):
            return value, send(trade, value)


        def sync(*need):
            if n_dp == 2:
                last.extend(jax.tree.leaves(need))

        def join(tokens):
            image, text = tokens
            return jnp.concatenate([image, jnp.pad(text, ((0, text_rows - text_len), (0, 0)))], 0)

        def mod_join(parts):
            image, text, counts = parts
            rows = jnp.concatenate(
                [
                    image[0].reshape(-1, local),
                    text[0].reshape(-1, local),
                    jnp.broadcast_to(counts[0].astype(F32), (1, local)),
                ],
                0,
            )
            return jnp.pad(rows, ((0, -rows.shape[0] % 8), (0, 0)))

        def lead_form(a):
            return a.transpose(0, 2, 1, 3) if a.ndim == 4 else a[:, None]

        def gather_one(a):
            if n_dp != 2:
                return (lax.all_gather(by(xc, a, over_x(a), 1), "dp", axis=1, tiled=True),)
            return a, over_x(a), over_y(a)

        def corner(parts, stream):
            if len(parts) == 1:
                return parts
            a, px, py = parts
            return a, px, py, (over_x(py) if stream == 0 else over_y(px))

        def assemble(parts, need=()):
            if len(parts) > 1:
                return step(lambda a, *rest: lay_quads(ids, (a,) + rest), *parts, need=need)
            return parts[0]

        def flat(w):
            return w if w.shape[0] > 1 else w[0]

        def z_pair(own):
            got = over_z(own)
            return lambda need=(): with_core(step(lambda a, b: by(zl, a, b, 1), own, got, need=need))

        def with_core(pair):
            return pair, send(core_swap, pair)

        def half_sum(keep, give, need=()):
            got = send(core_swap, give)
            return step(lambda a, b: (a.astype(F32) + b.astype(F32)).astype(BF), keep, got, need=need)

        def half_start(keep, give):
            got = send(core_swap, give)
            return lambda: step(lambda a, b: (a.astype(F32) + b.astype(F32)).astype(BF), keep, got)

        def full_sum(mine, got, need=()):
            return with_core(step(lambda a, b: (a.astype(F32) + b.astype(F32)).astype(BF), mine, got, need=need))

        def own_part(mine):
            away = lax.dynamic_slice_in_dim(mine, (1 - zl) * local, local, 1)
            here = lax.dynamic_slice_in_dim(mine, zl * local, local, 1)
            return here, over_z(away)

        def own_sum(here, got):
            return (here.astype(F32) + got.astype(F32)).astype(BF).astype(F32)

        def column_sums(a):
            return jnp.stack([jnp.sum(a[:image_len], 0), jnp.sum(a[image_len:], 0)])

        def per_row(index, s):
            return jnp.concatenate(
                [
                    jnp.broadcast_to(mod_own[s * 6 + index], (image_len, local)),
                    jnp.broadcast_to(mod_own[(slots + s) * 6 + index], (text_rows, local)),
                ],
                0,
            )

        places = [(image_len, s * 6, (slots + s) * 6) for s in range(slots)]

        def first_part(s, need=()):
            return step(lambda a, b: ln_qkv(ids, a, b, mod_full, *wq, *places[s]), *xs[s], need=need)

        def mixing(s, need=()):
            return step(lambda a: attend(a, length, image_len), firsts[s][1], need=need)

        def projection(s, need=()):
            keep, give = step(lambda a: out_project(ids, a, *wo, image_len), lses[s][0], need=need)
            mine = half_sum(keep, give)
            return mine, over_z(mine)

        def middle(s, need=()):
            return step(
                lambda a, b: mid_prepare(ids, lives[s].reshape(1), a, b, *atts[s], *cs[s], mod_full, *places[s]),
                *xs[s],
                need=need,
            )

        def dense(s):
            return step(lambda a, b: mlp(ids, a, b, *w1, *w2, image_len), mids[s][0], mids[s][1])

        def text_of(arrays):
            return jnp.concatenate([a[..., image_len:, :] for a in arrays], arrays[0].ndim - 2)

        lead_states = [lead_form(a) for a in states]
        mine = step(lambda a, b: cast_states((a, b)), lead_states[0], lead_states[4])
        got = send(core_swap, mine)
        rest_order = (1, 5, 2, 6, 7, 3)
        rest = step(lambda *a: cast_states(a), *(lead_states[i] for i in rest_order))
        rows_of = [a.shape[2] for a in lead_states]
        def pair_start(own):
            got = over_z(own)
            return lambda: step(lambda a, b: by(zl, a, b, 1), own, got), got

        pairs = dict(zip((0, 4), step(lambda a, b: pair_pieces(ids, a, b, [[(3, rows_of[0])]] * 2), mine, got)))
        pairs = {i: turned(a) for i, a in pairs.items()}
        rest_got = send(core_swap, rest)
        pieces = step(
            lambda a, b: pair_pieces(
                ids, a, b, [[(1, rows_of[1])] * 2] + [[(1, rows_of[i])] for i in (2, 6, 7, 3)]
            ),
            rest, rest_got,
        )
        pieces = dict(zip((1, 2, 6, 7, 3), pieces))
        x_in = [join((image_tokens[0, s], text_tokens[0, s])) for s in range(slots)]
        c_in = [join((image_cotan[0, s], text_cotan[0, s])) for s in range(slots)]
        sync(pairs[0])
        quads = [gather_one(pairs[0])]
        x_own = [turned(x_in[0])]
        sync(pairs[4], quads[0])
        quads.append(gather_one(pairs[4]))
        mod_own = turned(mod_join((image_modulation, text_modulation, group_counts)))
        count = mod_own[slots * 12, 0]
        lives = [(s * n_dp + d < count).astype(F32) for s in range(slots)]
        sync(quads[1], x_own[0], mod_own)
        x_pair, x_got = pair_start(x_own[0])
        quads = [corner(a, s) for s, a in enumerate(quads)]
        mod_pair, mod_got = pair_start(mod_own)
        pairs[1] = turned(pieces[1])
        sync(quads, x_got, mod_got)
        xs = [with_core(x_pair())]
        mod_pair = with_core(mod_pair())
        sync(pairs[1])
        outs = gather_one(pairs[1]) if n_dp == 2 else None
        pairs[2] = turned(pieces[2])
        wq = [assemble(a) for a in quads]
        mod_full = jnp.concatenate(mod_pair, 1)
        firsts = [first_part(0)]
        sync(outs if n_dp == 2 else (), pairs[2])
        if n_dp == 2:
            outs = [corner(tuple(a[s : s + 1] for a in outs), s) for s in range(2)]
        else:
            outs = [gather_one(pairs[1][s : s + 1]) for s in range(2)]
        pairs[6] = turned(pieces[6])
        sync(outs)
        expand = [gather_one(pairs[2])]
        x_own += [turned(a) for a in x_in[1:]]
        wo = [flat(assemble(a)) for a in outs]
        lses = [mixing(0)]
        keep, give = step(lambda a: out_project(ids, a, *wo, image_len), lses[0][0])
        sync(expand[0], pairs[6], x_own)
        half = half_start(keep, give)
        expand.append(gather_one(pairs[6]))
        pairs[7] = turned(pieces[7])
        more_x = [pair_start(x_own[s]) for s in range(1, slots)]
        mine = half()
        sync(expand[1], pairs[7], [a[1] for a in more_x])
        expand = [corner(a, e) for e, a in enumerate(expand)]
        pairs[3] = turned(pieces[3])
        xs += [with_core(a[0]()) for a in more_x]
        sums = [(mine, over_z(mine))]
        atts, mids, mlps, c_own = [], [], [], []
        for s in range(1, slots):
            firsts.append(first_part(s))
            if s == 1:
                sync(expand, pairs[3])
                reduce = [None, gather_one(pairs[7])]
                c_own.append(turned(c_in[0]))
                w1 = [flat(assemble(a)) for a in expand]
            lses.append(mixing(s))
            if s == 1:
                sync(reduce[1], c_own[0], sums[0])
                reduce[0] = gather_one(pairs[3])
                cots = [pair_start(c_own[0])]
                c_own += [turned(a) for a in c_in[1:]]
            keep, give = step(lambda a: out_project(ids, a, *wo, image_len), lses[s][0])
            half = half_start(keep, give)
            atts.append(full_sum(*sums[s - 1]))
            mine = half()
            if s == 1:
                sync(reduce[0], cots[0][1])
                reduce = [corner(a, e) for e, a in enumerate(reduce)]
                cs = [with_core(cots[0][0]())]
            sums.append((mine, over_z(mine)))
        mids.append(middle(0))
        sync(reduce, c_own)
        cots += [pair_start(c_own[s]) for s in range(1, slots)]
        w2 = [flat(assemble(a)) for a in reduce]

        lefts_text, rights_text = {}, {}

        def text_left(k):
            def halves(a):
                part = a.shape[1] // 2
                return (
                    lax.dynamic_slice_in_dim(a, d * part, part, 1),
                    lax.dynamic_slice_in_dim(a, (1 - d) * part, part, 1),
                )

            mine, away = step(halves, lefts_text[k])
            return mine, over_y(away)

        def text_right(k):
            return rights_text[k], over_y(rights_text[k])

        def text_grad(k):
            def product(left, left_got, right, right_got):
                return weight_grad(ids, None, [left, left_got], [right, right_got], slots * text_rows)

            return owned(step(product, *text_lefts[k], *text_rights[k]))

        def give_later(k, right=None, stream=0):
            left, rights_now, height = ((lefts, rights, image_len), (lefts_text, rights_text, slots * text_rows))[stream]
            right = rights_now[k] if right is None else right
            left, right = (a if isinstance(a, list) else [a] for a in (left[k], right))
            return step(lambda a: weight_grad(ids, 4, a, right, height), left)

        def keep_half(k, got, stream=0, need=()):
            left, right, height = ((lefts, rights, image_len), (lefts_text, rights_text, slots * text_rows))[stream]
            left, right = (a[k] if isinstance(a[k], list) else [a[k]] for a in (left, right))
            return owned(step(lambda a: weight_grad(ids, 3, a, right, height, got), left, need=need))

        def whole_grads(k):
            def one(left, right):
                if right.ndim == 3:
                    return jnp.einsum("td,ctf->cdf", left, right, preferred_element_type=F32)
                return mm(left, right, TN)[None]

            image = sum(one(a[:image_len], b[..., :image_len, :]) for a, b in zip(lefts[k], rights[k]))
            text = one(lefts_text[k], rights_text[k])
            return [
                owned(lax.psum_scatter(a.astype(BF), "dp", scatter_dimension=1, tiled=True)) for a in (image, text)
            ]

        two_way = n_dp == 2
        sent, text_lefts, text_rights, grads = {}, {}, {}, {}
        lefts, rights, backs, gqkvs, gh1_mine, branch_mine = {}, {}, [], [], [], []

        def backward(s, need=()):
            backs.append(
                step(
                    lambda a, b: back_prepare(
                        ids, lives[s].reshape(1), a, b, *atts[s], *cs[s], *gh2s[s], mod_full, *wo, *places[s]
                    ),
                    *xs[s],
                    need=need,
                )
            )

        def unmix(s, need=()):
            gqkvs.append(
                step(
                    lambda a, b: attend_back(a, b, lses[s][1], length, image_len),
                    firsts[s][1], backs[s][1],
                    need=need,
                )
            )

        def to_input(s, need=()):
            out = step(lambda a: input_partial(ids, a, *wq, image_len), gqkvs[s], need=need)
            gh1_mine.append(own_part(half_sum(*out)))

        def to_branch(s):
            branch_mine.append(own_part(half_sum(mlps[s][2], mlps[s][3])))

        results, grads_x, modgrads, gates = [], [], [], []

        def row_results(s):
            def first(here, got):
                branch = own_sum(here, got)
                res = (mids[s][2] + per_row(5, s) * branch).astype(BF)
                return res, column_sums(c_own[s].astype(F32) * lives[s] * branch)

            res, gate = step(first, *branch_mine[s])
            gates.append(gate)
            return res

        def row_sums(s):
            _, _, n1o, _ = firsts[s]

            def first(here, got):
                gh1 = own_sum(here, got)
                q = gh1 * (1.0 + per_row(1, s))
                total = jnp.stack([jnp.sum(q, 1), jnp.sum(q * n1o, 1)])
                sums = jnp.sum(backs[s][3].reshape(2, 3, 8, local), 2)
                mods = jnp.stack(
                    [column_sums(gh1), column_sums(gh1 * n1o), sums[:, 2], sums[:, 0], sums[:, 1], gates[s]]
                )
                return total, mods

            total, mods = step(first, *gh1_mine[s])
            modgrads.append(mods)
            return total, over_z(total)

        def row_total(total, got):
            total = step(jnp.add, total, got)
            return total, send(core_swap, total)

        def row_grads(s, total, got):
            _, _, n1o, inv1 = firsts[s]

            def second(total, got, here, away):
                total = (total + got) / width
                q = own_sum(here, away) * (1.0 + per_row(1, s))
                gx = backs[s][2] + inv1[:, :1] * (q - total[0][:, None] - n1o * total[1][:, None])
                return gx.astype(BF)

            grads_x.append(owned(step(second, total, got, *gh1_mine[s])))

        fresh, outer, waiting = [None] * 8, [None] * 8, {}
        inv_count = (1.0 / group_counts[0].astype(F32)).reshape(1)

        updates = {}

        def optimize(idx):
            moment = lead_form(moments[idx][0])
            lead, rows, cols = moment.shape[1:]
            piece = rows // n_group
            new, keep, give = step(
                lambda near, far: adam(ids, inv_count, moment.reshape(2, lead, n_group, piece, cols), near, far),
                *(a.reshape(lead, n_group, piece, cols) for a in grads[idx]),
            )
            updates[idx] = keep, give
            new = new.reshape(2, lead, rows, cols)
            fresh[idx] = new.transpose(0, 2, 1, 3)[None] if moments[idx].ndim == 5 else new[:, 0][None]

        def send_update(idx):
            updates[idx] = updates[idx][0], send(core_swap, updates[idx][1])

        def finish(idx):
            keep, got = updates[idx]
            out = step(
                lambda a: outer_step(ids, lead_form(states[idx]), keep, got, a, n_group), waiting[idx]
            )
            outer[idx] = out.transpose(0, 2, 1, 3) if moments[idx].ndim == 5 else out[:, 0]

        def fill_dense():
            lefts.update({3: [a[0] for a in mlps], 2: [a[0] for a in mids], 1: [a[0] for a in lses], 0: [a[0] for a in firsts]})
            rights.update({3: [a[1] for a in mids], 2: [a[1] for a in mlps]})

        def fill_mixing():
            rights[1] = [a[0] for a in backs]
            rights[0] = gqkvs
            rights_text[0] = step(text_of, gqkvs)
            lefts_text[1] = step(text_of, [a[0] for a in lses])
            rights_text[1] = step(text_of, rights[1])

        def fill_text(k):
            lefts_text[k] = step(text_of, lefts[k])
            rights_text[k] = step(text_of, rights[k])

        mlps.append(dense(0))
        sync(sums[-1], [a[1] for a in cots])
        gh_sums = []

        def gh_half(s):
            mine = half_sum(mlps[s][4], mlps[s][5])
            gh_sums.append((mine, over_z(mine)))

        def small_sum(idx):
            keep, got = updates[idx]
            pick = lambda a: lax.dynamic_index_in_dim(a, 1 - xc, 0, False)
            far = over_x(
                step(lambda a, b: (pick(a).astype(F32) + pick(b).astype(F32)).astype(BF), keep, got)
            )
            waiting[idx] = far

        if two_way and slots == 2:
            gh = half_start(mlps[0][4], mlps[0][5])
            atts.append(full_sum(*sums[1]))
            cs.append(with_core(cots[1][0]()))
            mine = gh()
            gh_sums.append((mine, over_z(mine)))
            mids.append(middle(1))
            lefts_text[0] = step(text_of, [a[0] for a in firsts])
            text_lefts[0] = text_left(0)
            mlps.append(dense(1))
            sync(gh_sums[0], text_lefts[0])
            gh = half_start(mlps[1][4], mlps[1][5])
            gh2s = [full_sum(*gh_sums[0])]
            fill_dense()
            fill_text(3)
            text_lefts[3] = text_left(3)
            text_rights[3] = text_right(3)
            mine = gh()
            gh_sums.append((mine, over_z(mine)))
            backward(0)
            sent_three = give_later(3)
            sent_two = give_later(2)
            fill_text(2)
            sync(text_lefts[3], text_rights[3], gh_sums[1])
            gh2s.append(full_sum(*gh_sums[1]))
            br = [half_start(mlps[s][2], mlps[s][3]) for s in range(2)]
            grads[7] = text_grad(3)
            text_rights[2] = text_right(2)
            text_lefts[2] = text_left(2)
            br = [a() for a in br]
            branch_mine.append(own_part(br[0]))
            unmix(0)
            sync(grads[7], text_rights[2], text_lefts[2], branch_mine[0])
            sent[3] = over_y(sent_three)
            grads[6] = text_grad(2)
            branch_mine.append(own_part(br[1]))
            res = [row_results(0)]
            backward(1)
            out = step(lambda a: input_partial(ids, a, *wq, image_len), gqkvs[0])
            optimize(7)
            sync(sent[3], grads[6], branch_mine[1])
            half = half_start(*out)
            send_update(7)
            grads[3] = keep_half(3, sent[3])
            gh1_mine.append(own_part(half()))
            small_sum(7)
            sent[2] = over_y(sent_two)
            unmix(1)
            sync(grads[3], gh1_mine[0], waiting[7], sent[2])
            grads[2] = keep_half(2, sent[2])
            results.append(owned(res[0]))
            totals = [row_sums(0)]
            sent_zero = give_later(0, gqkvs)
            out = step(lambda a: input_partial(ids, a, *wq, image_len), gqkvs[1])
            finish(7)
            res.append(row_results(1))
            fill_mixing()
            text_rights[0] = text_right(0)
            optimize(6)
            sync(grads[2], totals[0], text_rights[0], results[0])
            half = half_start(*out)
            send_update(6)
            totals[0] = row_total(*totals[0])
            grads[4] = text_grad(0)
            sent[0] = over_y(sent_zero)
            gh1_mine.append(own_part(half()))
            small_sum(6)
            row_grads(0, *totals[0])
            optimize(3)
            sent_text, sent_one = give_later(1, None, 1), give_later(1)
            sync(grads[4], gh1_mine[1], waiting[6], sent[0])
            send_update(3)
            grads[0] = keep_half(0, sent[0])
            results.append(owned(res[1]))
            totals.append(row_sums(1))
            sent[5], sent[1] = over_y(sent_text), over_y(sent_one)
            small_sum(3)
            finish(6)
            optimize(2)
            optimize(4)
            sync(totals[1], sent[5], sent[1], grads[0], waiting[3], results[1], grads_x[0])
            totals[1] = row_total(*totals[1])
            send_update(2)
            send_update(4)
            grads[5] = keep_half(1, sent[5], 1)
            grads[1] = keep_half(1, sent[1])
            small_sum(2)
            small_sum(4)
            row_grads(1, *totals[1])
            finish(3)
            optimize(0)
            sync(waiting[2], waiting[4], grads[5], grads[1])
            send_update(0)
            optimize(5)
            optimize(1)
            small_sum(0)
            send_update(5)
            send_update(1)
            finish(2)
            finish(4)
            small_sum(5)
            small_sum(1)
            for i in (0, 5, 1):
                finish(i)
        else:
            for s in range(1, slots):
                if len(atts) == s:
                    atts.append(full_sum(*sums[s]))
                cs.append(with_core(cots[s][0]()))
                mids.append(middle(s))
                mlps.append(dense(s))
            fill_dense()
            for s in range(slots):
                gh_half(s)
            gh2s = [full_sum(*a) for a in gh_sums]
            for s in range(slots):
                backward(s)
                unmix(s)
                to_input(s)
                to_branch(s)
                results.append(owned(row_results(s)))
                row_grads(s, *row_total(*row_sums(s)))
            fill_mixing()
            lefts_text[0] = step(text_of, lefts[0])
            fill_text(2)
            fill_text(3)
            for k in (3, 2, 1, 0):
                grads[k], grads[k + 4] = whole_grads(k)
            for i in range(8):
                optimize(i)
                send_update(i)
                small_sum(i)
                finish(i)
        mod_back = turn(jnp.stack(modgrads).reshape(slots * 12, local)).reshape(slots, 6, 2, local)

        res, gx = (jnp.stack([jnp.where(stays, a, b) for a, b in pairs]) for pairs in (results, grads_x))
        return (
            res[None, :, :image_len],
            res[None, :, image_len:length],
            gx[None, :, :image_len],
            gx[None, :, image_len:length],
            mod_back[None, :, :, 0],
            mod_back[None, :, :, 1],
            *fresh,
            *outer,
        )

    tokens = P("group", "dp", None, "mp")
    weight_specs = (
        P(None, ("dp", "group"), None, "mp"),
        P(None, ("mp", "dp", "group"), None),
        P(None, ("dp", "group"), "mp"),
        P(None, ("mp", "dp", "group"), None),
    ) * 2
    moment_specs = (
        P("group", None, "dp", None, "mp"),
        P("group", None, ("mp", "dp"), None),
        P("group", None, "dp", "mp"),
        P("group", None, ("mp", "dp"), None),
    ) * 2
    return jax.shard_map(
        body,
        mesh=mesh,
        in_specs=(tokens,) * 6 + (P("group"),) + weight_specs + moment_specs,
        out_specs=(tokens,) * 6 + moment_specs + weight_specs,
        check_vma=False,
    )
```

```python
import jax
import jax.numpy as jnp
from jax import lax
from jax.experimental import pallas as pl
from jax.experimental.pallas import tpu as pltpu
from jax.sharding import PartitionSpec as P

BF = jnp.bfloat16
F32 = jnp.float32
EPS_NORM = 1e-06
STEP = 3
BETA_ONE = 0.9
BETA_TWO = 0.95
ADAM_EPS = 1e-08
LEARN_RATE = 0.02
DECAY_RATE = 0.1
OUTER_RATE = 0.7
OUTER_MOMENT = 0.9
BLOCK = 256
VMEM_BYTES = 60 * 1024 * 1024
COST_SHARE = 1000
NT = (((1,), (1,)), ((), ()))
NN = (((1,), (0,)), ((), ()))
TN = (((0,), (0,)), ((), ()))


def mm(a, b, dims=NN):
    return lax.dot_general(a, b, dims, preferred_element_type=F32)


def cost(flops, nbytes):
    return pl.CostEstimate(
        flops=int(flops) // COST_SHARE, bytes_accessed=int(nbytes) // COST_SHARE, transcendentals=0
    )


def call(kernel, grid, in_specs, out_specs, out_shape, flops, nbytes, scratch=(), prefetch=1):
    return pl.pallas_call(
        kernel,
        grid_spec=pltpu.PrefetchScalarGridSpec(
            num_scalar_prefetch=prefetch,
            grid=grid,
            in_specs=in_specs,
            out_specs=out_specs,
            scratch_shapes=list(scratch),
        ),
        out_shape=out_shape,
        compiler_params=pltpu.CompilerParams(
            vmem_limit_bytes=VMEM_BYTES, dimension_semantics=("arbitrary",) * len(grid)
        ),
        cost_estimate=cost(flops, nbytes),
    )


def rows_spec(width):
    return pl.BlockSpec((BLOCK, width), lambda i, *_: (i, 0))


def whole(shape):
    return pl.BlockSpec(shape, lambda *_: (0,) * len(shape), pipeline_mode=pl.Buffered(1))


def struct(shape, dtype):
    return jax.ShapeDtypeStruct(shape, dtype)


def cast_states(states):
    cols = states[0].shape[-1]
    sizes = [s.shape[1] * s.shape[2] for s in states]

    def kernel(*refs):
        out_ref, at = refs[-1], 0
        for ref, state in zip(refs, states):
            for lead in range(state.shape[1]):
                rows = state.shape[2]
                out_ref[at : at + rows, :] = ref[0, lead].astype(BF)
                at += rows

    return call(
        kernel,
        (1,),
        [pl.BlockSpec((1,) + s.shape[1:], lambda *_: (0, 0, 0, 0), pipeline_mode=pl.Buffered(1)) for s in states],
        whole((sum(sizes), cols)),
        struct((sum(sizes), cols), BF),
        sum(sizes) * cols,
        sum(sizes) * cols * 6,
        prefetch=0,
    )(*states)


def pair_pieces(ids, mine, other, shapes):
    cols = mine.shape[1]

    def kernel(ids_ref, m_ref, o_ref, *out_refs):
        def lay(first_ref, second_ref):
            at = 0
            for out_ref, group in zip(out_refs, shapes):
                for k, (lead, rows) in enumerate(group):
                    for j in range(lead):
                        out_ref[k * lead + j, :rows, :] = first_ref[at : at + rows, :]
                        out_ref[k * lead + j, rows:, :] = second_ref[at : at + rows, :]
                        at += rows

        @pl.when(ids_ref[0] == 0)
        def _():
            lay(m_ref, o_ref)

        @pl.when(ids_ref[0] == 1)
        def _():
            lay(o_ref, m_ref)

    outs = [(len(group) * group[0][0], 2 * group[0][1], cols) for group in shapes]
    return call(
        kernel,
        (1,),
        [whole(mine.shape), whole(mine.shape)],
        [whole(s) for s in outs],
        [struct(s, BF) for s in outs],
        mine.size,
        mine.size * 8,
    )(ids, mine, other)


def lay_quads(ids, parts):
    lead, rows, cols = parts[0].shape

    def kernel(ids_ref, *refs):
        copies = []
        for k in range(4):
            at = pl.multiple_of(ids_ref[5 + k] * rows, 16)
            copies.append(pltpu.make_async_copy(refs[k], refs[4].at[:, pl.ds(at, rows), :], refs[5].at[k]))
            copies[-1].start()
        for copy in copies:
            copy.wait()

    return pl.pallas_call(
        kernel,
        in_specs=[pl.BlockSpec(memory_space=pltpu.SMEM)] + [pl.BlockSpec(memory_space=pl.ANY)] * 4,
        out_specs=pl.BlockSpec(memory_space=pl.ANY),
        out_shape=struct((lead, 4 * rows, cols), BF),
        scratch_shapes=[pltpu.SemaphoreType.DMA((4,))],
        compiler_params=pltpu.CompilerParams(vmem_limit_bytes=1024 * 1024),
        cost_estimate=cost(0, lead * rows * cols * 16),
    )(ids, *parts)


def ln_qkv(ids, xm, xo, mod, wi, wt, image_len, image_row, text_row):
    rows, half = xm.shape
    width, local = 2 * half, half // 2
    cols = 3 * local
    image_blocks = image_len // BLOCK

    def kernel(ids_ref, xm_ref, xo_ref, mod_ref, wi_ref, wt_ref, h_ref, qkv_ref, n_ref, inv_ref):
        i = pl.program_id(0)
        base = jnp.where(i < image_blocks, image_row, text_row)
        shift = mod_ref[pl.ds(base, 1), :]
        scale = 1.0 + mod_ref[pl.ds(base + 1, 1), :]
        first = ids_ref[1] == 0
        here = pl.ds(pl.multiple_of(ids_ref[0] * half, 128), half)
        there = pl.ds(pl.multiple_of((1 - ids_ref[0]) * half, 128), half)

        def chunk(r, carry):
            at = pl.ds(pl.multiple_of(r * 32, 32), 32)
            a = xm_ref[at, :].astype(F32)
            b = xo_ref[at, :].astype(F32)
            mean = (jnp.sum(a, 1, keepdims=True) + jnp.sum(b, 1, keepdims=True)) / width
            a, b = a - mean, b - mean
            var = (jnp.sum(a * a, 1, keepdims=True) + jnp.sum(b * b, 1, keepdims=True)) / width
            inv = lax.rsqrt(var + EPS_NORM)
            a, b = a * inv, b * inv
            n_ref[at, :] = jnp.where(first, a[:, :local], a[:, local:])
            inv_ref[at, :] = jnp.broadcast_to(inv, (32, 128))
            h_ref[at, here] = (a * scale[:, :half] + shift[:, :half]).astype(BF)
            h_ref[at, there] = (b * scale[:, half:] + shift[:, half:]).astype(BF)
            return carry

        lax.fori_loop(0, BLOCK // 32, chunk, 0, unroll=BLOCK // 32)

        def project(w_ref):
            for j in range(3):
                qkv_ref[j] = mm(h_ref[...], w_ref[j]).astype(BF)

        @pl.when(i < image_blocks)
        def _():
            project(wi_ref)

        @pl.when(i >= image_blocks)
        def _():
            project(wt_ref)

    return call(
        kernel,
        (pl.cdiv(rows, BLOCK),),
        [rows_spec(half), rows_spec(half), whole(mod.shape), whole(wi.shape), whole(wt.shape)],
        [
            rows_spec(width),
            pl.BlockSpec((3, BLOCK, local), lambda i, *_: (0, i, 0)),
            rows_spec(local),
            rows_spec(128),
        ],
        [
            struct((rows, width), BF),
            struct((3, rows, local), BF),
            struct((rows, local), F32),
            struct((rows, 128), F32),
        ],
        2 * rows * width * cols,
        rows * width * 6 + 4 * width * cols,
    )(ids, xm, xo, mod, wi, wt)


def pair_mask(array, head, dim):
    lane = lax.broadcasted_iota(jnp.int32, array.shape, 1)
    return jnp.where(lane // dim == head, array, jnp.zeros_like(array))


def q_chunks(rows, image_len):
    return [(s, BLOCK) for s in range(0, image_len, BLOCK)] + [(image_len, rows - image_len)]


def attend(qkv, length, image_len, dim=64):
    _, rows, local = qkv.shape
    pairs = local // 128
    lanes = pl.cdiv(rows, BLOCK) * BLOCK
    tail = length // 8 * 8
    scale = dim**-0.5

    def kernel(qkv_ref, out_ref, lse_ref, s_ref):
        for start, size in q_chunks(rows, image_len):
            total = None
            for head in range(128 // dim):
                q = pair_mask(qkv_ref[0, start : start + size, :], head, dim) * jnp.asarray(scale, BF)
                s_ref[:, :size] = mm(qkv_ref[1], q, NT)
                if tail < rows:
                    last = s_ref[tail:, :size]
                    row = lax.broadcasted_iota(jnp.int32, last.shape, 0) + tail
                    s_ref[tail:, :size] = jnp.where(row < length, last, -1e30)
                s = s_ref[:, :size]
                top = jnp.max(s, 0, keepdims=True)
                e = jnp.exp(s - top)
                norm = jnp.sum(e, 0, keepdims=True)
                lse_ref[0, head : head + 1, start : start + size] = top + jnp.log(norm)
                p = (e * (1.0 / norm)).astype(BF)
                mix = mm(p, pair_mask(qkv_ref[2], head, dim), TN)
                total = mix if total is None else total + mix
            out_ref[start : start + size, :] = total.astype(BF)

    return pl.pallas_call(
        kernel,
        grid=(pairs,),
        in_specs=[pl.BlockSpec((3, rows, 128), lambda j: (0, 0, j))],
        out_specs=[
            pl.BlockSpec((rows, 128), lambda j: (0, j)),
            pl.BlockSpec((1, 8, lanes), lambda j: (j, 0, 0)),
        ],
        out_shape=[struct((rows, local), BF), struct((pairs, 8, lanes), F32)],
        scratch_shapes=[pltpu.VMEM((rows, BLOCK), F32)],
        compiler_params=pltpu.CompilerParams(vmem_limit_bytes=VMEM_BYTES),
        cost_estimate=cost(16 * rows * rows * local, rows * local * 8),
    )(qkv)


def attend_back(qkv, grad, lse, length, image_len, dim=64):
    _, rows, local = qkv.shape
    pairs = local // 128
    lanes = lse.shape[2]
    tail = length // 8 * 8
    scale = dim**-0.5

    def kernel(qkv_ref, grad_ref, lse_ref, out_ref, s_ref, gk_ref, gv_ref):
        gk_ref[...] = jnp.zeros_like(gk_ref)
        gv_ref[...] = jnp.zeros_like(gv_ref)
        for start, size in q_chunks(rows, image_len):
            total = None
            for head in range(128 // dim):
                q = pair_mask(qkv_ref[0, start : start + size, :], head, dim) * jnp.asarray(scale, BF)
                gm = pair_mask(grad_ref[start : start + size, :], head, dim)
                s_ref[:, :size] = mm(qkv_ref[1], q, NT)
                if tail < rows:
                    last = s_ref[tail:, :size]
                    row = lax.broadcasted_iota(jnp.int32, last.shape, 0) + tail
                    s_ref[tail:, :size] = jnp.where(row < length, last, -1e30)
                p = jnp.exp(s_ref[:, :size] - lse_ref[0, head : head + 1, start : start + size])
                gv_ref[...] += mm(p.astype(BF), gm)
                gp = mm(qkv_ref[2], gm, NT)
                delta = jnp.sum(p * gp, 0, keepdims=True)
                gs = (p * (gp - delta)).astype(BF)
                gk_ref[...] += mm(gs, q)
                gq = mm(gs, pair_mask(qkv_ref[1], head, dim), TN)
                total = gq if total is None else total + gq
            out_ref[0, start : start + size, :] = (total * scale).astype(BF)
        out_ref[1] = gk_ref[...].astype(BF)
        out_ref[2] = gv_ref[...].astype(BF)

    return pl.pallas_call(
        kernel,
        grid=(pairs,),
        in_specs=[
            pl.BlockSpec((3, rows, 128), lambda j: (0, 0, j)),
            pl.BlockSpec((rows, 128), lambda j: (0, j)),
            pl.BlockSpec((1, 8, lanes), lambda j: (j, 0, 0)),
        ],
        out_specs=pl.BlockSpec((3, rows, 128), lambda j: (0, 0, j)),
        out_shape=struct((3, rows, local), BF),
        scratch_shapes=[
            pltpu.VMEM((rows, BLOCK), F32),
            pltpu.VMEM((rows, 128), F32),
            pltpu.VMEM((rows, 128), F32),
        ],
        compiler_params=pltpu.CompilerParams(vmem_limit_bytes=VMEM_BYTES),
        cost_estimate=cost(40 * rows * rows * local, rows * local * 14),
    )(qkv, grad, lse)


def out_project(ids, mixed, wi, wt, image_len):
    rows, local = mixed.shape
    width = wi.shape[1]
    half = width // 2
    image_blocks = image_len // BLOCK

    def kernel(ids_ref, a_ref, wi_ref, wt_ref, keep_ref, send_ref):
        i = pl.program_id(0)
        here = pl.ds(pl.multiple_of(ids_ref[0] * half, 128), half)
        there = pl.ds(pl.multiple_of((1 - ids_ref[0]) * half, 128), half)

        def project(w_ref):
            keep_ref[...] = mm(a_ref[...], w_ref[:, here]).astype(BF)
            send_ref[...] = mm(a_ref[...], w_ref[:, there]).astype(BF)

        @pl.when(i < image_blocks)
        def _():
            project(wi_ref)

        @pl.when(i >= image_blocks)
        def _():
            project(wt_ref)

    return call(
        kernel,
        (pl.cdiv(rows, BLOCK),),
        [rows_spec(local), whole(wi.shape), whole(wt.shape)],
        [rows_spec(half), rows_spec(half)],
        [struct((rows, half), BF), struct((rows, half), BF)],
        2 * rows * width * local,
        rows * width * 3 + 4 * width * local,
    )(ids, mixed, wi, wt)


def input_partial(ids, gqkv, wi, wt, image_len):
    _, rows, local = gqkv.shape
    width = wi.shape[1]
    half = width // 2
    image_blocks = image_len // BLOCK

    def kernel(ids_ref, a_ref, wi_ref, wt_ref, keep_ref, send_ref):
        i = pl.program_id(0)
        here = pl.ds(pl.multiple_of(ids_ref[0] * half, 128), half)
        there = pl.ds(pl.multiple_of((1 - ids_ref[0]) * half, 128), half)

        def project(w_ref):
            for out_ref, lo in ((keep_ref, here), (send_ref, there)):
                total = None
                for j in range(3):
                    part = mm(a_ref[j], w_ref[j, lo, :], NT)
                    total = part if total is None else total + part
                out_ref[...] = total.astype(BF)

        @pl.when(i < image_blocks)
        def _():
            project(wi_ref)

        @pl.when(i >= image_blocks)
        def _():
            project(wt_ref)

    return call(
        kernel,
        (pl.cdiv(rows, BLOCK),),
        [pl.BlockSpec((3, BLOCK, local), lambda i, *_: (0, i, 0)), whole(wi.shape), whole(wt.shape)],
        [rows_spec(half), rows_spec(half)],
        [struct((rows, half), BF), struct((rows, half), BF)],
        2 * rows * width * local * 3,
        rows * width * 5 + 12 * width * local,
    )(ids, gqkv, wi, wt)


def after_norm(xa, xb, aa, ab, gate, half, width):
    a = xa.astype(F32) + gate[:, :half] * aa.astype(F32)
    b = xb.astype(F32) + gate[:, half:] * ab.astype(F32)
    mean = (jnp.sum(a, 1, keepdims=True) + jnp.sum(b, 1, keepdims=True)) / width
    ca, cb = a - mean, b - mean
    var = (jnp.sum(ca * ca, 1, keepdims=True) + jnp.sum(cb * cb, 1, keepdims=True)) / width
    inv = lax.rsqrt(var + EPS_NORM)
    return a, ca * inv, cb * inv, inv


def mid_prepare(ids, live, xm, xo, am, ao, cm, co, mod, image_len, image_row, text_row):
    rows, half = xm.shape
    width, local = 2 * half, half // 2
    image_blocks = image_len // BLOCK
    step = 32

    def kernel(ids_ref, live_ref, xm_ref, xo_ref, am_ref, ao_ref, cm_ref, co_ref, mod_ref, h_ref, g_ref, own_ref):
        i = pl.program_id(0)
        base = jnp.where(i < image_blocks, image_row, text_row)
        gate_a = mod_ref[pl.ds(base + 2, 1), :]
        shift = mod_ref[pl.ds(base + 3, 1), :]
        scale = 1.0 + mod_ref[pl.ds(base + 4, 1), :]
        gate_m = mod_ref[pl.ds(base + 5, 1), :] * live_ref[0]
        first = ids_ref[1] == 0
        here = pl.ds(pl.multiple_of(ids_ref[0] * half, 128), half)
        there = pl.ds(pl.multiple_of((1 - ids_ref[0]) * half, 128), half)

        def chunk(r, carry):
            at = pl.ds(pl.multiple_of(r * step, step), step)
            a, na, nb, _ = after_norm(xm_ref[at, :], xo_ref[at, :], am_ref[at, :], ao_ref[at, :], gate_a, half, width)
            own_ref[at, :] = jnp.where(first, a[:, :local], a[:, local:])
            h_ref[at, here] = (na * scale[:, :half] + shift[:, :half]).astype(BF)
            h_ref[at, there] = (nb * scale[:, half:] + shift[:, half:]).astype(BF)
            g_ref[at, here] = (cm_ref[at, :].astype(F32) * gate_m[:, :half]).astype(BF)
            g_ref[at, there] = (co_ref[at, :].astype(F32) * gate_m[:, half:]).astype(BF)
            return carry

        lax.fori_loop(0, BLOCK // step, chunk, 0, unroll=BLOCK // step)

    return call(
        kernel,
        (pl.cdiv(rows, BLOCK),),
        [rows_spec(half)] * 6 + [whole(mod.shape)],
        [rows_spec(width), rows_spec(width), rows_spec(local)],
        [struct((rows, width), BF), struct((rows, width), BF), struct((rows, local), F32)],
        rows * width * 20,
        rows * width * 11,
        prefetch=2,
    )(ids, live, xm, xo, am, ao, cm, co, mod)


def gelu_pair(v):
    k, c3 = 0.7978845608028654, 0.044715
    v2 = v * v
    t = jnp.tanh(k * v * (1.0 + c3 * v2))
    up = 0.5 * (1.0 + t)
    return v * up, up + 0.5 * v * (1.0 - t * t) * (k * (1.0 + 3.0 * c3 * v2))


def mlp(ids, h, g, w1i, w1t, w2i, w2t, image_len, tile=512):
    rows, width = h.shape
    half = width // 2
    hidden = w1i.shape[1]
    steps = hidden // tile
    piece = 512

    def kernel(
        ids_ref, h_ref, g_ref, w1i_ref, w1t_ref, w2i_ref, w2t_ref,
        act_ref, gin_ref, bk_ref, bs_ref, gk_ref, gs_ref, b_acc, g_acc,
    ):
        i = pl.program_id(0)
        here = pl.ds(pl.multiple_of(ids_ref[0] * half, 128), half)
        there = pl.ds(pl.multiple_of((1 - ids_ref[0]) * half, 128), half)

        def work(at, w1_ref, w2_ref):
            inner = mm(h_ref[at, :], w1_ref[...])
            ag = mm(g_ref[at, :], w2_ref[...], NT)
            act, slope = gelu_pair(inner)
            act = act.astype(BF)
            gin = (ag * slope).astype(BF)
            act_ref[at, :] = act
            gin_ref[at, :] = gin
            parts = ((b_acc, mm(act, w2_ref[...])), (g_acc, mm(gin, w1_ref[...], NT)))

            @pl.when(i == 0)
            def _():
                for ref, value in parts:
                    ref[at, :] = value

            @pl.when(i > 0)
            def _():
                for ref, value in parts:
                    ref[at, :] += value

        def image_piece(r, carry):
            work(pl.ds(pl.multiple_of(r * piece, piece), piece), w1i_ref, w2i_ref)
            return carry

        lax.fori_loop(0, image_len // piece, image_piece, 0)
        work(slice(image_len, rows), w1t_ref, w2t_ref)

        @pl.when(i == steps - 1)
        def _():
            bk_ref[...] = b_acc[:, here].astype(BF)
            bs_ref[...] = b_acc[:, there].astype(BF)
            gk_ref[...] = g_acc[:, here].astype(BF)
            gs_ref[...] = g_acc[:, there].astype(BF)

    w1_spec = pl.BlockSpec((width, tile), lambda i, *_: (0, i))
    w2_spec = pl.BlockSpec((tile, width), lambda i, *_: (i, 0))
    out_tile = pl.BlockSpec((rows, tile), lambda i, *_: (0, i))
    return call(
        kernel,
        (steps,),
        [whole((rows, width)), whole((rows, width)), w1_spec, w1_spec, w2_spec, w2_spec],
        [out_tile, out_tile] + [whole((rows, half))] * 4,
        [struct((rows, hidden), BF)] * 2 + [struct((rows, half), BF)] * 4,
        8 * rows * width * hidden,
        rows * width * 12 + 8 * width * hidden,
        scratch=[pltpu.VMEM((rows, width), F32), pltpu.VMEM((rows, width), F32)],
    )(ids, h, g, w1i, w1t, w2i, w2t)


def back_prepare(ids, live, xm, xo, am, ao, cm, co, gm, go, mod, wi, wt, image_len, image_row, text_row):
    rows, half = xm.shape
    width, local = 2 * half, half // 2
    image_blocks = image_len // BLOCK
    step = 32

    def kernel(
        ids_ref, live_ref, xm_ref, xo_ref, am_ref, ao_ref, cm_ref, co_ref, gm_ref, go_ref, mod_ref, wi_ref, wt_ref,
        ga_ref, gmix_ref, own_ref, sums_ref,
    ):
        i = pl.program_id(0)
        base = jnp.where(i < image_blocks, image_row, text_row)
        gate_a = mod_ref[pl.ds(base + 2, 1), :]
        scale = 1.0 + mod_ref[pl.ds(base + 4, 1), :]
        first = ids_ref[1] == 0
        live_now = live_ref[0]
        here = pl.ds(pl.multiple_of(ids_ref[0] * half, 128), half)
        there = pl.ds(pl.multiple_of((1 - ids_ref[0]) * half, 128), half)

        @pl.when((i == 0) | (i == image_blocks))
        def _():
            sums_ref[...] = jnp.zeros_like(sums_ref)

        def own(v):
            return jnp.where(first, v[:, :local], v[:, local:])

        def chunk(r, carry):
            at = pl.ds(pl.multiple_of(r * step, step), step)
            _, na, nb, inv = after_norm(xm_ref[at, :], xo_ref[at, :], am_ref[at, :], ao_ref[at, :], gate_a, half, width)
            ga = gm_ref[at, :].astype(F32)
            gb = go_ref[at, :].astype(F32)
            qa, qb = ga * scale[:, :half], gb * scale[:, half:]
            mean = (jnp.sum(qa, 1, keepdims=True) + jnp.sum(qb, 1, keepdims=True)) / width
            cross = (jnp.sum(qa * na, 1, keepdims=True) + jnp.sum(qb * nb, 1, keepdims=True)) / width
            fa = cm_ref[at, :].astype(F32) * live_now + inv * (qa - mean - na * cross)
            fb = co_ref[at, :].astype(F32) * live_now + inv * (qb - mean - nb * cross)
            ga_ref[at, here] = (gate_a[:, :half] * fa).astype(BF)
            ga_ref[at, there] = (gate_a[:, half:] * fb).astype(BF)
            fo, go_own = own(fa), own(ga)
            own_ref[at, :] = fo
            row = i * BLOCK + r * step + lax.broadcasted_iota(jnp.int32, (step, local), 0)
            inside = row < rows
            for k, value in enumerate((go_own, go_own * own(na), fo * own(am_ref[at, :].astype(F32)))):
                value = jnp.where(inside, value, 0.0)
                sums_ref[0, k * 8 : (k + 1) * 8, :] += jnp.sum(value.reshape(step // 8, 8, local), 0)
            return carry

        lax.fori_loop(0, BLOCK // step, chunk, 0, unroll=BLOCK // step)

        def project(w_ref):
            gmix_ref[...] = mm(ga_ref[...], w_ref[...], NT).astype(BF)

        @pl.when(i < image_blocks)
        def _():
            project(wi_ref)

        @pl.when(i >= image_blocks)
        def _():
            project(wt_ref)

    return call(
        kernel,
        (pl.cdiv(rows, BLOCK),),
        [rows_spec(half)] * 8 + [whole(mod.shape), whole(wi.shape), whole(wt.shape)],
        [
            rows_spec(width),
            rows_spec(local),
            rows_spec(local),
            pl.BlockSpec((1, 24, local), lambda i, *_: (jnp.where(i < image_blocks, 0, 1), 0, 0)),
        ],
        [
            struct((rows, width), BF),
            struct((rows, local), BF),
            struct((rows, local), F32),
            struct((2, 24, local), F32),
        ],
        2 * rows * width * local,
        rows * width * 12,
        prefetch=2,
    )(ids, live, xm, xo, am, ao, cm, co, gm, go, mod, wi, wt)


def grad_specs(right, tile, height, row_block):
    if right.ndim == 3:
        return (
            pl.BlockSpec((1, height, right.shape[2]), lambda j, *_: (j, row_block, 0)),
            right.shape[0],
            right.shape[2],
        )
    return pl.BlockSpec((height, tile), lambda j, *_: (row_block, j)), right.shape[1] // tile, tile


def grad_out(right, tile, part):
    if right.ndim == 3:
        lead, _, cols = right.shape
        return pl.BlockSpec((1, part, cols), lambda j, *_: (j, 0, 0)), struct((lead, part, cols), BF)
    return (
        pl.BlockSpec((1, part, tile), lambda j, *_: (0, 0, j)),
        struct((1, part, right.shape[1]), BF),
    )


def weight_grad(ids, which, lefts, rights, height, add=None, tile=512):
    part = lefts[0].shape[1] // (1 if which is None else 2)
    n = len(lefts)
    right_spec, steps, _ = grad_specs(rights[0], tile, height, 0)
    narrow = which is not None and part % 128 != 0
    left_spec = pl.BlockSpec(
        (height, 2 * part if narrow else part),
        lambda j, ids_ref: (0, 0 if narrow or which is None else ids_ref[which]),
        pipeline_mode=pl.Buffered(1),
    )
    out_spec, out_shape = grad_out(rights[0], tile, part)
    flat = rights[0].ndim == 2

    def kernel(ids_ref, *refs):
        total = None
        for left_ref, right_ref in zip(refs[:n], refs[n : 2 * n]):
            value = mm(left_ref[...], right_ref[...] if flat else right_ref[0], TN)
            total = value if total is None else total + value
        if narrow:
            total = jnp.where(ids_ref[which] == 0, total[:part], total[part:])
        if add is not None:
            total = total + refs[2 * n][0].astype(F32)
        refs[-1][0] = total.astype(BF)

    more = [] if add is None else [add]
    return call(
        kernel,
        (steps,),
        [left_spec] * n + [right_spec] * n + [out_spec] * len(more),
        out_spec,
        out_shape,
        2 * n * height * part * out_shape.shape[0] * out_shape.shape[2],
        n * height * (part + out_shape.shape[0] * out_shape.shape[2]) * 2,
    )(ids, *lefts, *rights, *more)


def adam(ids, inv_count, moment, near, far):
    _, lead, _, piece, cols = moment.shape
    correct_one = 1.0 - BETA_ONE**STEP
    correct_two = 1.0 - BETA_TWO**STEP

    def kernel(ids_ref, inv_ref, m_ref, near_ref, far_ref, fresh_ref, keep_ref, send_ref):
        t = pl.program_id(0)
        for l in range(lead):
            g = jnp.where(ids_ref[9] == 1, near_ref[l, 0], far_ref[l, 0]).astype(F32) * inv_ref[0]
            first = BETA_ONE * m_ref[0, l, 0] + (1.0 - BETA_ONE) * g
            second = BETA_TWO * m_ref[1, l, 0] + (1.0 - BETA_TWO) * g * g
            fresh_ref[0, l, 0] = first
            fresh_ref[1, l, 0] = second
            update = (first * (1.0 / correct_one) / (jnp.sqrt(second * (1.0 / correct_two)) + ADAM_EPS)).astype(BF)

            @pl.when(t < 2)
            def _(l=l, update=update):
                send_ref[0, l] = update

            @pl.when(t >= 2)
            def _(l=l, update=update):
                keep_ref[0, l] = update

    def block(t, ids_ref):
        return (t % 2) * 2 + jnp.where(t < 2, 1 - ids_ref[0], ids_ref[0])

    pairs = pl.BlockSpec((2, lead, 1, piece, cols), lambda t, ids_ref, _: (0, 0, block(t, ids_ref), 0, 0))
    grad = pl.BlockSpec((lead, 1, piece, cols), lambda t, ids_ref, _: (0, block(t, ids_ref), 0, 0))
    side = struct((2, lead, piece, cols), BF)
    return call(
        kernel,
        (4,),
        [pairs, grad, grad],
        [
            pairs,
            pl.BlockSpec((1, lead, piece, cols), lambda t, *_: (jnp.maximum(t - 2, 0), 0, 0, 0)),
            pl.BlockSpec((1, lead, piece, cols), lambda t, *_: (jnp.minimum(t, 1), 0, 0, 0)),
        ],
        [struct(moment.shape, F32), side, side],
        lead * piece * cols * 80,
        lead * piece * cols * 80,
        prefetch=2,
    )(ids, inv_count, moment, near, far)


def outer_step(ids, state, keep, got, far, groups):
    _, lead, piece, cols = state.shape

    def kernel(ids_ref, s_ref, k_ref, g_ref, f_ref, out_ref):
        near = (k_ref[0].astype(F32) + g_ref[0].astype(F32)).astype(BF).astype(F32)
        total = near + f_ref[...].astype(F32)
        master = s_ref[0]
        delta = LEARN_RATE * (total * (1.0 / groups) + DECAY_RATE * master)
        momentum = OUTER_MOMENT * s_ref[1] + delta
        out_ref[0] = master - OUTER_RATE * (delta + OUTER_MOMENT * momentum)
        out_ref[1] = delta
        out_ref[2] = momentum

    side = pl.BlockSpec((1, lead, piece, cols), lambda i, ids_ref: (ids_ref[2], 0, 0, 0))
    return call(
        kernel,
        (1,),
        [
            pl.BlockSpec((2, lead, piece, cols), lambda i, *_: (0, 0, 0, 0)),
            side,
            side,
            pl.BlockSpec((lead, piece, cols), lambda i, *_: (0, 0, 0)),
        ],
        pl.BlockSpec((3, lead, piece, cols), lambda i, *_: (0, 0, 0, 0)),
        struct((3, lead, piece, cols), F32),
        lead * piece * cols * 10,
        lead * piece * cols * 26,
    )(ids, state, keep, got, far)


def solution(mesh):
    n_group, n_dp, n_mp = mesh.shape["group"], mesh.shape["dp"], mesh.shape["mp"]
    core_perm = [(g, g ^ 1) for g in range(n_group)]
    x_perm = [(g, g ^ 2) for g in range(n_group)]
    z_perm = [(m, m ^ 1) for m in range(n_mp)]
    y_perm = [(d, d ^ 1) for d in range(n_dp)]
    turn_perm = [
        (g * n_mp + m, ((g // 2) * 2 + m // 2) * n_mp + (g % 2) * 2 + m % 2)
        for g in range(n_group)
        for m in range(n_mp)
    ]

    trade_perm = [(i, j if i != j else (i // n_mp ^ 2) * n_mp + i % n_mp) for i, j in turn_perm]

    def core_swap(a):
        return lax.ppermute(a, "group", core_perm)

    def x_swap(a):
        return lax.ppermute(a, "group", x_perm)

    def z_swap(a):
        return lax.ppermute(a, "mp", z_perm)

    def y_swap(a):
        return lax.ppermute(a, "dp", y_perm)

    def turn(a):
        return lax.ppermute(a, ("group", "mp"), turn_perm)

    def trade(a):
        return lax.ppermute(a, ("group", "mp"), trade_perm)

    def by(flag, a, b, axis):
        return jnp.where(flag == 0, jnp.concatenate([a, b], axis), jnp.concatenate([b, a], axis))

    def body(
        image_tokens, text_tokens, image_modulation, text_modulation, image_cotan, text_cotan,
        group_counts, *tensors,
    ):
        states, moments = tensors[:8], tensors[8:]
        g, d, m = lax.axis_index("group"), lax.axis_index("dp"), lax.axis_index("mp")
        c, xc, zl = g % 2, g // 2, m % 2
        place = (d % 2) * 2 + xc
        ids = jnp.stack([c, zl, xc, d % 2, 1 - d % 2, place, place ^ 1, place ^ 2, place ^ 3, c == m // 2]).astype(jnp.int32)

        slots = image_tokens.shape[1]
        image_len, text_len = image_tokens.shape[2], text_tokens.shape[2]
        text_rows = -(-text_len // 32) * 32
        local = image_tokens.shape[3]
        width = local * n_mp
        rows_all = image_len + text_rows
        length = image_len + text_len

        last = []

        def hold(value, others):
            if not others:
                return value
            leaves, tree = jax.tree.flatten(value)
            held = lax.optimization_barrier(tuple(leaves) + tuple(others))
            return jax.tree.unflatten(tree, list(held[: len(leaves)]))

        def step(fn, first, *rest, need=()):
            out = fn(hold(first, last + jax.tree.leaves(need)), *rest)
            last[:] = [jax.tree.leaves(out)[0]]
            return out

        def send(move, value):
            return move(hold(value, last))

        turned, over_x, over_y, over_z = (lambda value, move=move: send(move, value) for move in (turn, x_swap, y_swap, z_swap))
        stays = c == m // 2

        def owned(value):
            return value, send(trade, value)


        def sync(*need):
            if n_dp == 2:
                last.extend(jax.tree.leaves(need))

        def join(tokens):
            image, text = tokens
            return jnp.concatenate([image, jnp.pad(text, ((0, text_rows - text_len), (0, 0)))], 0)

        def mod_join(parts):
            image, text, counts = parts
            rows = jnp.concatenate(
                [
                    image[0].reshape(-1, local),
                    text[0].reshape(-1, local),
                    jnp.broadcast_to(counts[0].astype(F32), (1, local)),
                ],
                0,
            )
            return jnp.pad(rows, ((0, -rows.shape[0] % 8), (0, 0)))

        def lead_form(a):
            return a.transpose(0, 2, 1, 3) if a.ndim == 4 else a[:, None]

        def gather_one(a):
            if n_dp != 2:
                return (lax.all_gather(by(xc, a, over_x(a), 1), "dp", axis=1, tiled=True),)
            return a, over_x(a), over_y(a)

        def corner(parts, stream):
            if len(parts) == 1:
                return parts
            a, px, py = parts
            return a, px, py, (over_x(py) if stream == 0 else over_y(px))

        def assemble(parts, need=()):
            if len(parts) > 1:
                return step(lambda a, *rest: lay_quads(ids, (a,) + rest), *parts, need=need)
            return parts[0]

        def flat(w):
            return w if w.shape[0] > 1 else w[0]

        def z_pair(own):
            got = over_z(own)
            return lambda need=(): with_core(step(lambda a, b: by(zl, a, b, 1), own, got, need=need))

        def with_core(pair):
            return pair, send(core_swap, pair)

        def half_sum(keep, give, need=()):
            got = send(core_swap, give)
            return step(lambda a, b: (a.astype(F32) + b.astype(F32)).astype(BF), keep, got, need=need)

        def half_start(keep, give):
            got = send(core_swap, give)
            return lambda: step(lambda a, b: (a.astype(F32) + b.astype(F32)).astype(BF), keep, got)

        def full_sum(mine, got, need=()):
            return with_core(step(lambda a, b: (a.astype(F32) + b.astype(F32)).astype(BF), mine, got, need=need))

        def own_part(mine):
            away = lax.dynamic_slice_in_dim(mine, (1 - zl) * local, local, 1)
            here = lax.dynamic_slice_in_dim(mine, zl * local, local, 1)
            return here, over_z(away)

        def own_sum(here, got):
            return (here.astype(F32) + got.astype(F32)).astype(BF).astype(F32)

        def column_sums(a):
            return jnp.stack([jnp.sum(a[:image_len], 0), jnp.sum(a[image_len:], 0)])

        def per_row(index, s):
            return jnp.concatenate(
                [
                    jnp.broadcast_to(mod_own[s * 6 + index], (image_len, local)),
                    jnp.broadcast_to(mod_own[(slots + s) * 6 + index], (text_rows, local)),
                ],
                0,
            )

        places = [(image_len, s * 6, (slots + s) * 6) for s in range(slots)]

        def first_part(s, need=()):
            return step(lambda a, b: ln_qkv(ids, a, b, mod_full, *wq, *places[s]), *xs[s], need=need)

        def mixing(s, need=()):
            return step(lambda a: attend(a, length, image_len), firsts[s][1], need=need)

        def projection(s, need=()):
            keep, give = step(lambda a: out_project(ids, a, *wo, image_len), lses[s][0], need=need)
            mine = half_sum(keep, give)
            return mine, over_z(mine)

        def middle(s, need=()):
            return step(
                lambda a, b: mid_prepare(ids, lives[s].reshape(1), a, b, *atts[s], *cs[s], mod_full, *places[s]),
                *xs[s],
                need=need,
            )

        def dense(s):
            return step(lambda a, b: mlp(ids, a, b, *w1, *w2, image_len), mids[s][0], mids[s][1])

        def text_of(arrays):
            return jnp.concatenate([a[..., image_len:, :] for a in arrays], arrays[0].ndim - 2)

        lead_states = [lead_form(a) for a in states]
        mine = step(lambda a, b: cast_states((a, b)), lead_states[0], lead_states[4])
        got = send(core_swap, mine)
        rest_order = (1, 5, 2, 6, 7, 3)
        rest = step(lambda *a: cast_states(a), *(lead_states[i] for i in rest_order))
        rows_of = [a.shape[2] for a in lead_states]
        def pair_start(own):
            got = over_z(own)
            return lambda: step(lambda a, b: by(zl, a, b, 1), own, got), got

        pairs = dict(zip((0, 4), step(lambda a, b: pair_pieces(ids, a, b, [[(3, rows_of[0])]] * 2), mine, got)))
        pairs = {i: turned(a) for i, a in pairs.items()}
        rest_got = send(core_swap, rest)
        pieces = step(
            lambda a, b: pair_pieces(
                ids, a, b, [[(1, rows_of[1])] * 2] + [[(1, rows_of[i])] for i in (2, 6, 7, 3)]
            ),
            rest, rest_got,
        )
        pieces = dict(zip((1, 2, 6, 7, 3), pieces))
        x_in = [join((image_tokens[0, s], text_tokens[0, s])) for s in range(slots)]
        c_in = [join((image_cotan[0, s], text_cotan[0, s])) for s in range(slots)]
        sync(pairs[0])
        quads = [gather_one(pairs[0])]
        x_own = [turned(x_in[0])]
        sync(pairs[4], quads[0])
        quads.append(gather_one(pairs[4]))
        mod_own = turned(mod_join((image_modulation, text_modulation, group_counts)))
        count = mod_own[slots * 12, 0]
        lives = [(s * n_dp + d < count).astype(F32) for s in range(slots)]
        sync(quads[1], x_own[0], mod_own)
        x_pair, x_got = pair_start(x_own[0])
        quads = [corner(a, s) for s, a in enumerate(quads)]
        mod_pair, mod_got = pair_start(mod_own)
        pairs[1] = turned(pieces[1])
        sync(quads, x_got, mod_got)
        xs = [with_core(x_pair())]
        mod_pair = with_core(mod_pair())
        sync(pairs[1])
        outs = gather_one(pairs[1]) if n_dp == 2 else None
        pairs[2] = turned(pieces[2])
        wq = [assemble(a) for a in quads]
        mod_full = jnp.concatenate(mod_pair, 1)
        firsts = [first_part(0)]
        sync(outs if n_dp == 2 else (), pairs[2])
        if n_dp == 2:
            outs = [corner(tuple(a[s : s + 1] for a in outs), s) for s in range(2)]
        else:
            outs = [gather_one(pairs[1][s : s + 1]) for s in range(2)]
        pairs[6] = turned(pieces[6])
        sync(outs)
        expand = [gather_one(pairs[2])]
        x_own += [turned(a) for a in x_in[1:]]
        wo = [flat(assemble(a)) for a in outs]
        lses = [mixing(0)]
        keep, give = step(lambda a: out_project(ids, a, *wo, image_len), lses[0][0])
        sync(expand[0], pairs[6], x_own)
        half = half_start(keep, give)
        expand.append(gather_one(pairs[6]))
        pairs[7] = turned(pieces[7])
        more_x = [pair_start(x_own[s]) for s in range(1, slots)]
        mine = half()
        sync(expand[1], pairs[7], [a[1] for a in more_x])
        expand = [corner(a, e) for e, a in enumerate(expand)]
        pairs[3] = turned(pieces[3])
        xs += [with_core(a[0]()) for a in more_x]
        sums = [(mine, over_z(mine))]
        atts, mids, mlps, c_own = [], [], [], []
        for s in range(1, slots):
            firsts.append(first_part(s))
            if s == 1:
                sync(expand, pairs[3])
                reduce = [None, gather_one(pairs[7])]
                c_own.append(turned(c_in[0]))
                w1 = [flat(assemble(a)) for a in expand]
            lses.append(mixing(s))
            if s == 1:
                sync(reduce[1], c_own[0], sums[0])
                reduce[0] = gather_one(pairs[3])
                cots = [pair_start(c_own[0])]
                c_own += [turned(a) for a in c_in[1:]]
            keep, give = step(lambda a: out_project(ids, a, *wo, image_len), lses[s][0])
            half = half_start(keep, give)
            atts.append(full_sum(*sums[s - 1]))
            mine = half()
            if s == 1:
                sync(reduce[0], cots[0][1])
                reduce = [corner(a, e) for e, a in enumerate(reduce)]
                cs = [with_core(cots[0][0]())]
            sums.append((mine, over_z(mine)))
        mids.append(middle(0))
        sync(reduce, c_own)
        cots += [pair_start(c_own[s]) for s in range(1, slots)]
        w2 = [flat(assemble(a)) for a in reduce]

        lefts_text, rights_text = {}, {}

        def text_left(k):
            def halves(a):
                part = a.shape[1] // 2
                return (
                    lax.dynamic_slice_in_dim(a, d * part, part, 1),
                    lax.dynamic_slice_in_dim(a, (1 - d) * part, part, 1),
                )

            mine, away = step(halves, lefts_text[k])
            return mine, over_y(away)

        def text_right(k):
            return rights_text[k], over_y(rights_text[k])

        def text_grad(k):
            def product(left, left_got, right, right_got):
                return weight_grad(ids, None, [left, left_got], [right, right_got], slots * text_rows)

            return owned(step(product, *text_lefts[k], *text_rights[k]))

        def give_later(k, right=None, stream=0):
            left, rights_now, height = ((lefts, rights, image_len), (lefts_text, rights_text, slots * text_rows))[stream]
            right = rights_now[k] if right is None else right
            left, right = (a if isinstance(a, list) else [a] for a in (left[k], right))
            return step(lambda a: weight_grad(ids, 4, a, right, height), left)

        def keep_half(k, got, stream=0, need=()):
            left, right, height = ((lefts, rights, image_len), (lefts_text, rights_text, slots * text_rows))[stream]
            left, right = (a[k] if isinstance(a[k], list) else [a[k]] for a in (left, right))
            return owned(step(lambda a: weight_grad(ids, 3, a, right, height, got), left, need=need))

        def whole_grads(k):
            def one(left, right):
                if right.ndim == 3:
                    return jnp.einsum("td,ctf->cdf", left, right, preferred_element_type=F32)
                return mm(left, right, TN)[None]

            image = sum(one(a[:image_len], b[..., :image_len, :]) for a, b in zip(lefts[k], rights[k]))
            text = one(lefts_text[k], rights_text[k])
            return [
                owned(lax.psum_scatter(a.astype(BF), "dp", scatter_dimension=1, tiled=True)) for a in (image, text)
            ]

        two_way = n_dp == 2
        sent, text_lefts, text_rights, grads = {}, {}, {}, {}
        lefts, rights, backs, gqkvs, gh1_mine, branch_mine = {}, {}, [], [], [], []

        def backward(s, need=()):
            backs.append(
                step(
                    lambda a, b: back_prepare(
                        ids, lives[s].reshape(1), a, b, *atts[s], *cs[s], *gh2s[s], mod_full, *wo, *places[s]
                    ),
                    *xs[s],
                    need=need,
                )
            )

        def unmix(s, need=()):
            gqkvs.append(
                step(
                    lambda a, b: attend_back(a, b, lses[s][1], length, image_len),
                    firsts[s][1], backs[s][1],
                    need=need,
                )
            )

        def to_input(s, need=()):
            out = step(lambda a: input_partial(ids, a, *wq, image_len), gqkvs[s], need=need)
            gh1_mine.append(own_part(half_sum(*out)))

        def to_branch(s):
            branch_mine.append(own_part(half_sum(mlps[s][2], mlps[s][3])))

        results, grads_x, modgrads, gates = [], [], [], []

        def row_results(s):
            def first(here, got):
                branch = own_sum(here, got)
                res = (mids[s][2] + per_row(5, s) * branch).astype(BF)
                return res, column_sums(c_own[s].astype(F32) * lives[s] * branch)

            res, gate = step(first, *branch_mine[s])
            gates.append(gate)
            return res

        def row_sums(s):
            _, _, n1o, _ = firsts[s]

            def first(here, got):
                gh1 = own_sum(here, got)
                q = gh1 * (1.0 + per_row(1, s))
                total = jnp.stack([jnp.sum(q, 1), jnp.sum(q * n1o, 1)])
                sums = jnp.sum(backs[s][3].reshape(2, 3, 8, local), 2)
                mods = jnp.stack(
                    [column_sums(gh1), column_sums(gh1 * n1o), sums[:, 2], sums[:, 0], sums[:, 1], gates[s]]
                )
                return total, mods

            total, mods = step(first, *gh1_mine[s])
            modgrads.append(mods)
            return total, over_z(total)

        def row_total(total, got):
            total = step(jnp.add, total, got)
            return total, send(core_swap, total)

        def row_grads(s, total, got):
            _, _, n1o, inv1 = firsts[s]

            def second(total, got, here, away):
                total = (total + got) / width
                q = own_sum(here, away) * (1.0 + per_row(1, s))
                gx = backs[s][2] + inv1[:, :1] * (q - total[0][:, None] - n1o * total[1][:, None])
                return gx.astype(BF)

            grads_x.append(owned(step(second, total, got, *gh1_mine[s])))

        fresh, outer, waiting = [None] * 8, [None] * 8, {}
        inv_count = (1.0 / group_counts[0].astype(F32)).reshape(1)

        updates = {}

        def optimize(idx):
            moment = lead_form(moments[idx][0])
            lead, rows, cols = moment.shape[1:]
            piece = rows // n_group
            new, keep, give = step(
                lambda near, far: adam(ids, inv_count, moment.reshape(2, lead, n_group, piece, cols), near, far),
                *(a.reshape(lead, n_group, piece, cols) for a in grads[idx]),
            )
            updates[idx] = keep, give
            new = new.reshape(2, lead, rows, cols)
            fresh[idx] = new.transpose(0, 2, 1, 3)[None] if moments[idx].ndim == 5 else new[:, 0][None]

        def send_update(idx):
            updates[idx] = updates[idx][0], send(core_swap, updates[idx][1])

        def finish(idx):
            keep, got = updates[idx]
            out = step(
                lambda a: outer_step(ids, lead_form(states[idx]), keep, got, a, n_group), waiting[idx]
            )
            outer[idx] = out.transpose(0, 2, 1, 3) if moments[idx].ndim == 5 else out[:, 0]

        def fill_dense():
            lefts.update({3: [a[0] for a in mlps], 2: [a[0] for a in mids], 1: [a[0] for a in lses], 0: [a[0] for a in firsts]})
            rights.update({3: [a[1] for a in mids], 2: [a[1] for a in mlps]})

        def fill_mixing():
            rights[1] = [a[0] for a in backs]
            rights[0] = gqkvs
            rights_text[0] = step(text_of, gqkvs)
            lefts_text[1] = step(text_of, [a[0] for a in lses])
            rights_text[1] = step(text_of, rights[1])

        def fill_text(k):
            lefts_text[k] = step(text_of, lefts[k])
            rights_text[k] = step(text_of, rights[k])

        mlps.append(dense(0))
        sync(sums[-1], [a[1] for a in cots])
        gh_sums = []

        def gh_half(s):
            mine = half_sum(mlps[s][4], mlps[s][5])
            gh_sums.append((mine, over_z(mine)))

        def small_sum(idx):
            keep, got = updates[idx]
            pick = lambda a: lax.dynamic_index_in_dim(a, 1 - xc, 0, False)
            far = over_x(
                step(lambda a, b: (pick(a).astype(F32) + pick(b).astype(F32)).astype(BF), keep, got)
            )
            waiting[idx] = far

        if two_way and slots == 2:
            gh = half_start(mlps[0][4], mlps[0][5])
            atts.append(full_sum(*sums[1]))
            cs.append(with_core(cots[1][0]()))
            mine = gh()
            gh_sums.append((mine, over_z(mine)))
            mids.append(middle(1))
            lefts_text[0] = step(text_of, [a[0] for a in firsts])
            text_lefts[0] = text_left(0)
            mlps.append(dense(1))
            sync(gh_sums[0], text_lefts[0])
            gh = half_start(mlps[1][4], mlps[1][5])
            gh2s = [full_sum(*gh_sums[0])]
            fill_dense()
            fill_text(3)
            text_lefts[3] = text_left(3)
            text_rights[3] = text_right(3)
            mine = gh()
            gh_sums.append((mine, over_z(mine)))
            backward(0)
            sent_three = give_later(3)
            sent_two = give_later(2)
            fill_text(2)
            sync(text_lefts[3], text_rights[3], gh_sums[1])
            gh2s.append(full_sum(*gh_sums[1]))
            br = [half_start(mlps[s][2], mlps[s][3]) for s in range(2)]
            grads[7] = text_grad(3)
            text_rights[2] = text_right(2)
            text_lefts[2] = text_left(2)
            br = [a() for a in br]
            branch_mine.append(own_part(br[0]))
            unmix(0)
            sync(grads[7], text_rights[2], text_lefts[2], branch_mine[0])
            sent[3] = over_y(sent_three)
            grads[6] = text_grad(2)
            branch_mine.append(own_part(br[1]))
            res = [row_results(0)]
            backward(1)
            out = step(lambda a: input_partial(ids, a, *wq, image_len), gqkvs[0])
            optimize(7)
            sync(sent[3], branch_mine[1])
            grads[3] = keep_half(3, sent[3])
            sync(grads[6])
            half = half_start(*out)
            send_update(7)
            gh1_mine.append(own_part(half()))
            small_sum(7)
            sent[2] = over_y(sent_two)
            unmix(1)
            sync(grads[3], gh1_mine[0], waiting[7], sent[2])
            grads[2] = keep_half(2, sent[2])
            results.append(owned(res[0]))
            totals = [row_sums(0)]
            sent_zero = give_later(0, gqkvs)
            out = step(lambda a: input_partial(ids, a, *wq, image_len), gqkvs[1])
            finish(7)
            res.append(row_results(1))
            fill_mixing()
            text_rights[0] = text_right(0)
            optimize(6)
            sync(grads[2], totals[0], text_rights[0])
            half = half_start(*out)
            send_update(6)
            totals[0] = row_total(*totals[0])
            grads[4] = text_grad(0)
            sent[0] = over_y(sent_zero)
            gh1_mine.append(own_part(half()))
            small_sum(6)
            row_grads(0, *totals[0])
            optimize(3)
            sent_text, sent_one = give_later(1, None, 1), give_later(1)
            sync(grads[4], gh1_mine[1], waiting[6], sent[0], results[0])
            send_update(3)
            grads[0] = keep_half(0, sent[0])
            results.append(owned(res[1]))
            totals.append(row_sums(1))
            sent[5], sent[1] = over_y(sent_text), over_y(sent_one)
            small_sum(3)
            finish(6)
            optimize(2)
            sync(totals[1], sent[5], sent[1], grads_x[0])
            grads[5] = keep_half(1, sent[5], 1)
            grads[1] = keep_half(1, sent[1])
            optimize(4)
            sync(grads[0], waiting[3], results[1], grads[5], grads[1])
            totals[1] = row_total(*totals[1])
            send_update(2)
            send_update(4)
            finish(3)
            small_sum(2)
            small_sum(4)
            row_grads(1, *totals[1])
            optimize(0)
            optimize(5)
            optimize(1)
            sync(waiting[2], waiting[4])
            send_update(0)
            send_update(5)
            send_update(1)
            small_sum(0)
            small_sum(5)
            small_sum(1)
            finish(2)
            finish(4)
            sync(waiting[0], waiting[5], waiting[1])
            for i in (0, 5, 1):
                finish(i)
        else:
            for s in range(1, slots):
                if len(atts) == s:
                    atts.append(full_sum(*sums[s]))
                cs.append(with_core(cots[s][0]()))
                mids.append(middle(s))
                mlps.append(dense(s))
            fill_dense()
            for s in range(slots):
                gh_half(s)
            gh2s = [full_sum(*a) for a in gh_sums]
            for s in range(slots):
                backward(s)
                unmix(s)
                to_input(s)
                to_branch(s)
                results.append(owned(row_results(s)))
                row_grads(s, *row_total(*row_sums(s)))
            fill_mixing()
            lefts_text[0] = step(text_of, lefts[0])
            fill_text(2)
            fill_text(3)
            for k in (3, 2, 1, 0):
                grads[k], grads[k + 4] = whole_grads(k)
            for i in range(8):
                optimize(i)
                send_update(i)
                small_sum(i)
                finish(i)
        mod_back = turn(jnp.stack(modgrads).reshape(slots * 12, local)).reshape(slots, 6, 2, local)

        res, gx = (jnp.stack([jnp.where(stays, a, b) for a, b in pairs]) for pairs in (results, grads_x))
        return (
            res[None, :, :image_len],
            res[None, :, image_len:length],
            gx[None, :, :image_len],
            gx[None, :, image_len:length],
            mod_back[None, :, :, 0],
            mod_back[None, :, :, 1],
            *fresh,
            *outer,
        )

    tokens = P("group", "dp", None, "mp")
    weight_specs = (
        P(None, ("dp", "group"), None, "mp"),
        P(None, ("mp", "dp", "group"), None),
        P(None, ("dp", "group"), "mp"),
        P(None, ("mp", "dp", "group"), None),
    ) * 2
    moment_specs = (
        P("group", None, "dp", None, "mp"),
        P("group", None, ("mp", "dp"), None),
        P("group", None, "dp", "mp"),
        P("group", None, ("mp", "dp"), None),
    ) * 2
    return jax.shard_map(
        body,
        mesh=mesh,
        in_specs=(tokens,) * 6 + (P("group"),) + weight_specs + moment_specs,
        out_specs=(tokens,) * 6 + moment_specs + weight_specs,
        check_vma=False,
    )
```

```python
import jax
import jax.numpy as jnp
from jax import lax
from jax.experimental import pallas as pl
from jax.experimental.pallas import tpu as pltpu
from jax.sharding import PartitionSpec as P

BF = jnp.bfloat16
F32 = jnp.float32
EPS_NORM = 1e-06
STEP = 3
BETA_ONE = 0.9
BETA_TWO = 0.95
ADAM_EPS = 1e-08
LEARN_RATE = 0.02
DECAY_RATE = 0.1
OUTER_RATE = 0.7
OUTER_MOMENT = 0.9
BLOCK = 256
VMEM_BYTES = 60 * 1024 * 1024
COST_SHARE = 1000
NT = (((1,), (1,)), ((), ()))
NN = (((1,), (0,)), ((), ()))
TN = (((0,), (0,)), ((), ()))


def mm(a, b, dims=NN):
    return lax.dot_general(a, b, dims, preferred_element_type=F32)


def cost(flops, nbytes):
    return pl.CostEstimate(
        flops=int(flops) // COST_SHARE, bytes_accessed=int(nbytes) // COST_SHARE, transcendentals=0
    )


def call(kernel, grid, in_specs, out_specs, out_shape, flops, nbytes, scratch=(), prefetch=1):
    return pl.pallas_call(
        kernel,
        grid_spec=pltpu.PrefetchScalarGridSpec(
            num_scalar_prefetch=prefetch,
            grid=grid,
            in_specs=in_specs,
            out_specs=out_specs,
            scratch_shapes=list(scratch),
        ),
        out_shape=out_shape,
        compiler_params=pltpu.CompilerParams(
            vmem_limit_bytes=VMEM_BYTES, dimension_semantics=("arbitrary",) * len(grid)
        ),
        cost_estimate=cost(flops, nbytes),
    )


def rows_spec(width):
    return pl.BlockSpec((BLOCK, width), lambda i, *_: (i, 0))


def whole(shape):
    return pl.BlockSpec(shape, lambda *_: (0,) * len(shape), pipeline_mode=pl.Buffered(1))


def struct(shape, dtype):
    return jax.ShapeDtypeStruct(shape, dtype)


def cast_states(states):
    cols = states[0].shape[-1]
    sizes = [s.shape[1] * s.shape[2] for s in states]

    def kernel(*refs):
        out_ref, at = refs[-1], 0
        for ref, state in zip(refs, states):
            for lead in range(state.shape[1]):
                rows = state.shape[2]
                out_ref[at : at + rows, :] = ref[0, lead].astype(BF)
                at += rows

    return call(
        kernel,
        (1,),
        [pl.BlockSpec((1,) + s.shape[1:], lambda *_: (0, 0, 0, 0), pipeline_mode=pl.Buffered(1)) for s in states],
        whole((sum(sizes), cols)),
        struct((sum(sizes), cols), BF),
        sum(sizes) * cols,
        sum(sizes) * cols * 6,
        prefetch=0,
    )(*states)


def pair_pieces(ids, mine, other, shapes):
    cols = mine.shape[1]

    def kernel(ids_ref, m_ref, o_ref, *out_refs):
        def lay(first_ref, second_ref):
            at = 0
            for out_ref, group in zip(out_refs, shapes):
                for k, (lead, rows) in enumerate(group):
                    for j in range(lead):
                        out_ref[k * lead + j, :rows, :] = first_ref[at : at + rows, :]
                        out_ref[k * lead + j, rows:, :] = second_ref[at : at + rows, :]
                        at += rows

        @pl.when(ids_ref[0] == 0)
        def _():
            lay(m_ref, o_ref)

        @pl.when(ids_ref[0] == 1)
        def _():
            lay(o_ref, m_ref)

    outs = [(len(group) * group[0][0], 2 * group[0][1], cols) for group in shapes]
    return call(
        kernel,
        (1,),
        [whole(mine.shape), whole(mine.shape)],
        [whole(s) for s in outs],
        [struct(s, BF) for s in outs],
        mine.size,
        mine.size * 8,
    )(ids, mine, other)


def lay_quads(ids, parts):
    lead, rows, cols = parts[0].shape

    def kernel(ids_ref, *refs):
        copies = []
        for k in range(4):
            at = pl.multiple_of(ids_ref[5 + k] * rows, 16)
            copies.append(pltpu.make_async_copy(refs[k], refs[4].at[:, pl.ds(at, rows), :], refs[5].at[k]))
            copies[-1].start()
        for copy in copies:
            copy.wait()

    return pl.pallas_call(
        kernel,
        in_specs=[pl.BlockSpec(memory_space=pltpu.SMEM)] + [pl.BlockSpec(memory_space=pl.ANY)] * 4,
        out_specs=pl.BlockSpec(memory_space=pl.ANY),
        out_shape=struct((lead, 4 * rows, cols), BF),
        scratch_shapes=[pltpu.SemaphoreType.DMA((4,))],
        compiler_params=pltpu.CompilerParams(vmem_limit_bytes=1024 * 1024),
        cost_estimate=cost(0, lead * rows * cols * 16),
    )(ids, *parts)


def ln_qkv(ids, xm, xo, mod, wi, wt, image_len, image_row, text_row):
    rows, half = xm.shape
    width, local = 2 * half, half // 2
    cols = 3 * local
    image_blocks = image_len // BLOCK

    def kernel(ids_ref, xm_ref, xo_ref, mod_ref, wi_ref, wt_ref, h_ref, qkv_ref, n_ref, inv_ref):
        i = pl.program_id(0)
        base = jnp.where(i < image_blocks, image_row, text_row)
        shift = mod_ref[pl.ds(base, 1), :]
        scale = 1.0 + mod_ref[pl.ds(base + 1, 1), :]
        first = ids_ref[1] == 0
        here = pl.ds(pl.multiple_of(ids_ref[0] * half, 128), half)
        there = pl.ds(pl.multiple_of((1 - ids_ref[0]) * half, 128), half)

        def chunk(r, carry):
            at = pl.ds(pl.multiple_of(r * 32, 32), 32)
            a = xm_ref[at, :].astype(F32)
            b = xo_ref[at, :].astype(F32)
            mean = (jnp.sum(a, 1, keepdims=True) + jnp.sum(b, 1, keepdims=True)) / width
            a, b = a - mean, b - mean
            var = (jnp.sum(a * a, 1, keepdims=True) + jnp.sum(b * b, 1, keepdims=True)) / width
            inv = lax.rsqrt(var + EPS_NORM)
            a, b = a * inv, b * inv
            n_ref[at, :] = jnp.where(first, a[:, :local], a[:, local:])
            inv_ref[at, :] = jnp.broadcast_to(inv, (32, 128))
            h_ref[at, here] = (a * scale[:, :half] + shift[:, :half]).astype(BF)
            h_ref[at, there] = (b * scale[:, half:] + shift[:, half:]).astype(BF)
            return carry

        lax.fori_loop(0, BLOCK // 32, chunk, 0, unroll=BLOCK // 32)

        def project(w_ref):
            for j in range(3):
                qkv_ref[j] = mm(h_ref[...], w_ref[j]).astype(BF)

        @pl.when(i < image_blocks)
        def _():
            project(wi_ref)

        @pl.when(i >= image_blocks)
        def _():
            project(wt_ref)

    return call(
        kernel,
        (pl.cdiv(rows, BLOCK),),
        [rows_spec(half), rows_spec(half), whole(mod.shape), whole(wi.shape), whole(wt.shape)],
        [
            rows_spec(width),
            pl.BlockSpec((3, BLOCK, local), lambda i, *_: (0, i, 0)),
            rows_spec(local),
            rows_spec(128),
        ],
        [
            struct((rows, width), BF),
            struct((3, rows, local), BF),
            struct((rows, local), F32),
            struct((rows, 128), F32),
        ],
        2 * rows * width * cols,
        rows * width * 6 + 4 * width * cols,
    )(ids, xm, xo, mod, wi, wt)


def pair_mask(array, head, dim):
    lane = lax.broadcasted_iota(jnp.int32, array.shape, 1)
    return jnp.where(lane // dim == head, array, jnp.zeros_like(array))


def q_chunks(rows, image_len):
    return [(s, BLOCK) for s in range(0, image_len, BLOCK)] + [(image_len, rows - image_len)]


def attend(qkv, length, image_len, dim=64):
    _, rows, local = qkv.shape
    pairs = local // 128
    lanes = pl.cdiv(rows, BLOCK) * BLOCK
    tail = length // 8 * 8
    scale = dim**-0.5

    def kernel(qkv_ref, out_ref, lse_ref, s_ref):
        for start, size in q_chunks(rows, image_len):
            total = None
            for head in range(128 // dim):
                q = pair_mask(qkv_ref[0, start : start + size, :], head, dim) * jnp.asarray(scale, BF)
                s_ref[:, :size] = mm(qkv_ref[1], q, NT)
                if tail < rows:
                    last = s_ref[tail:, :size]
                    row = lax.broadcasted_iota(jnp.int32, last.shape, 0) + tail
                    s_ref[tail:, :size] = jnp.where(row < length, last, -1e30)
                s = s_ref[:, :size]
                top = jnp.max(s, 0, keepdims=True)
                e = jnp.exp(s - top)
                norm = jnp.sum(e, 0, keepdims=True)
                lse_ref[0, head : head + 1, start : start + size] = top + jnp.log(norm)
                p = (e * (1.0 / norm)).astype(BF)
                mix = mm(p, pair_mask(qkv_ref[2], head, dim), TN)
                total = mix if total is None else total + mix
            out_ref[start : start + size, :] = total.astype(BF)

    return pl.pallas_call(
        kernel,
        grid=(pairs,),
        in_specs=[pl.BlockSpec((3, rows, 128), lambda j: (0, 0, j))],
        out_specs=[
            pl.BlockSpec((rows, 128), lambda j: (0, j)),
            pl.BlockSpec((1, 8, lanes), lambda j: (j, 0, 0)),
        ],
        out_shape=[struct((rows, local), BF), struct((pairs, 8, lanes), F32)],
        scratch_shapes=[pltpu.VMEM((rows, BLOCK), F32)],
        compiler_params=pltpu.CompilerParams(vmem_limit_bytes=VMEM_BYTES),
        cost_estimate=cost(16 * rows * rows * local, rows * local * 8),
    )(qkv)


def attend_back(qkv, grad, lse, length, image_len, dim=64):
    _, rows, local = qkv.shape
    pairs = local // 128
    lanes = lse.shape[2]
    tail = length // 8 * 8
    scale = dim**-0.5

    def kernel(qkv_ref, grad_ref, lse_ref, out_ref, s_ref, gk_ref, gv_ref):
        gk_ref[...] = jnp.zeros_like(gk_ref)
        gv_ref[...] = jnp.zeros_like(gv_ref)
        for start, size in q_chunks(rows, image_len):
            total = None
            for head in range(128 // dim):
                q = pair_mask(qkv_ref[0, start : start + size, :], head, dim) * jnp.asarray(scale, BF)
                gm = pair_mask(grad_ref[start : start + size, :], head, dim)
                s_ref[:, :size] = mm(qkv_ref[1], q, NT)
                if tail < rows:
                    last = s_ref[tail:, :size]
                    row = lax.broadcasted_iota(jnp.int32, last.shape, 0) + tail
                    s_ref[tail:, :size] = jnp.where(row < length, last, -1e30)
                p = jnp.exp(s_ref[:, :size] - lse_ref[0, head : head + 1, start : start + size])
                gv_ref[...] += mm(p.astype(BF), gm)
                gp = mm(qkv_ref[2], gm, NT)
                delta = jnp.sum(p * gp, 0, keepdims=True)
                gs = (p * (gp - delta)).astype(BF)
                gk_ref[...] += mm(gs, q)
                gq = mm(gs, pair_mask(qkv_ref[1], head, dim), TN)
                total = gq if total is None else total + gq
            out_ref[0, start : start + size, :] = (total * scale).astype(BF)
        out_ref[1] = gk_ref[...].astype(BF)
        out_ref[2] = gv_ref[...].astype(BF)

    return pl.pallas_call(
        kernel,
        grid=(pairs,),
        in_specs=[
            pl.BlockSpec((3, rows, 128), lambda j: (0, 0, j)),
            pl.BlockSpec((rows, 128), lambda j: (0, j)),
            pl.BlockSpec((1, 8, lanes), lambda j: (j, 0, 0)),
        ],
        out_specs=pl.BlockSpec((3, rows, 128), lambda j: (0, 0, j)),
        out_shape=struct((3, rows, local), BF),
        scratch_shapes=[
            pltpu.VMEM((rows, BLOCK), F32),
            pltpu.VMEM((rows, 128), F32),
            pltpu.VMEM((rows, 128), F32),
        ],
        compiler_params=pltpu.CompilerParams(vmem_limit_bytes=VMEM_BYTES),
        cost_estimate=cost(40 * rows * rows * local, rows * local * 14),
    )(qkv, grad, lse)


def out_project(ids, mixed, wi, wt, image_len):
    rows, local = mixed.shape
    width = wi.shape[1]
    half = width // 2
    image_blocks = image_len // BLOCK

    def kernel(ids_ref, a_ref, wi_ref, wt_ref, keep_ref, send_ref):
        i = pl.program_id(0)
        here = pl.ds(pl.multiple_of(ids_ref[0] * half, 128), half)
        there = pl.ds(pl.multiple_of((1 - ids_ref[0]) * half, 128), half)

        def project(w_ref):
            keep_ref[...] = mm(a_ref[...], w_ref[:, here]).astype(BF)
            send_ref[...] = mm(a_ref[...], w_ref[:, there]).astype(BF)

        @pl.when(i < image_blocks)
        def _():
            project(wi_ref)

        @pl.when(i >= image_blocks)
        def _():
            project(wt_ref)

    return call(
        kernel,
        (pl.cdiv(rows, BLOCK),),
        [rows_spec(local), whole(wi.shape), whole(wt.shape)],
        [rows_spec(half), rows_spec(half)],
        [struct((rows, half), BF), struct((rows, half), BF)],
        2 * rows * width * local,
        rows * width * 3 + 4 * width * local,
    )(ids, mixed, wi, wt)


def input_partial(ids, gqkv, wi, wt, image_len):
    _, rows, local = gqkv.shape
    width = wi.shape[1]
    half = width // 2
    image_blocks = image_len // BLOCK

    def kernel(ids_ref, a_ref, wi_ref, wt_ref, keep_ref, send_ref):
        i = pl.program_id(0)
        here = pl.ds(pl.multiple_of(ids_ref[0] * half, 128), half)
        there = pl.ds(pl.multiple_of((1 - ids_ref[0]) * half, 128), half)

        def project(w_ref):
            for out_ref, lo in ((keep_ref, here), (send_ref, there)):
                total = None
                for j in range(3):
                    part = mm(a_ref[j], w_ref[j, lo, :], NT)
                    total = part if total is None else total + part
                out_ref[...] = total.astype(BF)

        @pl.when(i < image_blocks)
        def _():
            project(wi_ref)

        @pl.when(i >= image_blocks)
        def _():
            project(wt_ref)

    return call(
        kernel,
        (pl.cdiv(rows, BLOCK),),
        [pl.BlockSpec((3, BLOCK, local), lambda i, *_: (0, i, 0)), whole(wi.shape), whole(wt.shape)],
        [rows_spec(half), rows_spec(half)],
        [struct((rows, half), BF), struct((rows, half), BF)],
        2 * rows * width * local * 3,
        rows * width * 5 + 12 * width * local,
    )(ids, gqkv, wi, wt)


def after_norm(xa, xb, aa, ab, gate, half, width):
    a = xa.astype(F32) + gate[:, :half] * aa.astype(F32)
    b = xb.astype(F32) + gate[:, half:] * ab.astype(F32)
    mean = (jnp.sum(a, 1, keepdims=True) + jnp.sum(b, 1, keepdims=True)) / width
    ca, cb = a - mean, b - mean
    var = (jnp.sum(ca * ca, 1, keepdims=True) + jnp.sum(cb * cb, 1, keepdims=True)) / width
    inv = lax.rsqrt(var + EPS_NORM)
    return a, ca * inv, cb * inv, inv


def mid_prepare(ids, live, xm, xo, am, ao, cm, co, mod, image_len, image_row, text_row):
    rows, half = xm.shape
    width, local = 2 * half, half // 2
    image_blocks = image_len // BLOCK
    step = 32

    def kernel(ids_ref, live_ref, xm_ref, xo_ref, am_ref, ao_ref, cm_ref, co_ref, mod_ref, h_ref, g_ref, own_ref):
        i = pl.program_id(0)
        base = jnp.where(i < image_blocks, image_row, text_row)
        gate_a = mod_ref[pl.ds(base + 2, 1), :]
        shift = mod_ref[pl.ds(base + 3, 1), :]
        scale = 1.0 + mod_ref[pl.ds(base + 4, 1), :]
        gate_m = mod_ref[pl.ds(base + 5, 1), :] * live_ref[0]
        first = ids_ref[1] == 0
        here = pl.ds(pl.multiple_of(ids_ref[0] * half, 128), half)
        there = pl.ds(pl.multiple_of((1 - ids_ref[0]) * half, 128), half)

        def chunk(r, carry):
            at = pl.ds(pl.multiple_of(r * step, step), step)
            a, na, nb, _ = after_norm(xm_ref[at, :], xo_ref[at, :], am_ref[at, :], ao_ref[at, :], gate_a, half, width)
            own_ref[at, :] = jnp.where(first, a[:, :local], a[:, local:])
            h_ref[at, here] = (na * scale[:, :half] + shift[:, :half]).astype(BF)
            h_ref[at, there] = (nb * scale[:, half:] + shift[:, half:]).astype(BF)
            g_ref[at, here] = (cm_ref[at, :].astype(F32) * gate_m[:, :half]).astype(BF)
            g_ref[at, there] = (co_ref[at, :].astype(F32) * gate_m[:, half:]).astype(BF)
            return carry

        lax.fori_loop(0, BLOCK // step, chunk, 0, unroll=BLOCK // step)

    return call(
        kernel,
        (pl.cdiv(rows, BLOCK),),
        [rows_spec(half)] * 6 + [whole(mod.shape)],
        [rows_spec(width), rows_spec(width), rows_spec(local)],
        [struct((rows, width), BF), struct((rows, width), BF), struct((rows, local), F32)],
        rows * width * 20,
        rows * width * 11,
        prefetch=2,
    )(ids, live, xm, xo, am, ao, cm, co, mod)


def gelu_pair(v):
    k, c3 = 0.7978845608028654, 0.044715
    v2 = v * v
    t = jnp.tanh(k * v * (1.0 + c3 * v2))
    up = 0.5 * (1.0 + t)
    return v * up, up + 0.5 * v * (1.0 - t * t) * (k * (1.0 + 3.0 * c3 * v2))


def mlp(ids, h, g, w1i, w1t, w2i, w2t, image_len, tile=512):
    rows, width = h.shape
    half = width // 2
    hidden = w1i.shape[1]
    steps = hidden // tile
    piece = 512

    def kernel(
        ids_ref, h_ref, g_ref, w1i_ref, w1t_ref, w2i_ref, w2t_ref,
        act_ref, gin_ref, bk_ref, bs_ref, gk_ref, gs_ref, b_acc, g_acc,
    ):
        i = pl.program_id(0)
        here = pl.ds(pl.multiple_of(ids_ref[0] * half, 128), half)
        there = pl.ds(pl.multiple_of((1 - ids_ref[0]) * half, 128), half)

        def work(at, w1_ref, w2_ref):
            inner = mm(h_ref[at, :], w1_ref[...])
            ag = mm(g_ref[at, :], w2_ref[...], NT)
            act, slope = gelu_pair(inner)
            act = act.astype(BF)
            gin = (ag * slope).astype(BF)
            act_ref[at, :] = act
            gin_ref[at, :] = gin
            parts = ((b_acc, mm(act, w2_ref[...])), (g_acc, mm(gin, w1_ref[...], NT)))

            @pl.when(i == 0)
            def _():
                for ref, value in parts:
                    ref[at, :] = value

            @pl.when(i > 0)
            def _():
                for ref, value in parts:
                    ref[at, :] += value

        def image_piece(r, carry):
            work(pl.ds(pl.multiple_of(r * piece, piece), piece), w1i_ref, w2i_ref)
            return carry

        lax.fori_loop(0, image_len // piece, image_piece, 0)
        work(slice(image_len, rows), w1t_ref, w2t_ref)

        @pl.when(i == steps - 1)
        def _():
            bk_ref[...] = b_acc[:, here].astype(BF)
            bs_ref[...] = b_acc[:, there].astype(BF)
            gk_ref[...] = g_acc[:, here].astype(BF)
            gs_ref[...] = g_acc[:, there].astype(BF)

    w1_spec = pl.BlockSpec((width, tile), lambda i, *_: (0, i))
    w2_spec = pl.BlockSpec((tile, width), lambda i, *_: (i, 0))
    out_tile = pl.BlockSpec((rows, tile), lambda i, *_: (0, i))
    return call(
        kernel,
        (steps,),
        [whole((rows, width)), whole((rows, width)), w1_spec, w1_spec, w2_spec, w2_spec],
        [out_tile, out_tile] + [whole((rows, half))] * 4,
        [struct((rows, hidden), BF)] * 2 + [struct((rows, half), BF)] * 4,
        8 * rows * width * hidden,
        rows * width * 12 + 8 * width * hidden,
        scratch=[pltpu.VMEM((rows, width), F32), pltpu.VMEM((rows, width), F32)],
    )(ids, h, g, w1i, w1t, w2i, w2t)


def back_prepare(ids, live, xm, xo, am, ao, cm, co, gm, go, mod, wi, wt, image_len, image_row, text_row):
    rows, half = xm.shape
    width, local = 2 * half, half // 2
    image_blocks = image_len // BLOCK
    step = 32

    def kernel(
        ids_ref, live_ref, xm_ref, xo_ref, am_ref, ao_ref, cm_ref, co_ref, gm_ref, go_ref, mod_ref, wi_ref, wt_ref,
        ga_ref, gmix_ref, own_ref, sums_ref,
    ):
        i = pl.program_id(0)
        base = jnp.where(i < image_blocks, image_row, text_row)
        gate_a = mod_ref[pl.ds(base + 2, 1), :]
        scale = 1.0 + mod_ref[pl.ds(base + 4, 1), :]
        first = ids_ref[1] == 0
        live_now = live_ref[0]
        here = pl.ds(pl.multiple_of(ids_ref[0] * half, 128), half)
        there = pl.ds(pl.multiple_of((1 - ids_ref[0]) * half, 128), half)

        @pl.when((i == 0) | (i == image_blocks))
        def _():
            sums_ref[...] = jnp.zeros_like(sums_ref)

        def own(v):
            return jnp.where(first, v[:, :local], v[:, local:])

        def chunk(r, carry):
            at = pl.ds(pl.multiple_of(r * step, step), step)
            _, na, nb, inv = after_norm(xm_ref[at, :], xo_ref[at, :], am_ref[at, :], ao_ref[at, :], gate_a, half, width)
            ga = gm_ref[at, :].astype(F32)
            gb = go_ref[at, :].astype(F32)
            qa, qb = ga * scale[:, :half], gb * scale[:, half:]
            mean = (jnp.sum(qa, 1, keepdims=True) + jnp.sum(qb, 1, keepdims=True)) / width
            cross = (jnp.sum(qa * na, 1, keepdims=True) + jnp.sum(qb * nb, 1, keepdims=True)) / width
            fa = cm_ref[at, :].astype(F32) * live_now + inv * (qa - mean - na * cross)
            fb = co_ref[at, :].astype(F32) * live_now + inv * (qb - mean - nb * cross)
            ga_ref[at, here] = (gate_a[:, :half] * fa).astype(BF)
            ga_ref[at, there] = (gate_a[:, half:] * fb).astype(BF)
            fo, go_own = own(fa), own(ga)
            own_ref[at, :] = fo
            row = i * BLOCK + r * step + lax.broadcasted_iota(jnp.int32, (step, local), 0)
            inside = row < rows
            for k, value in enumerate((go_own, go_own * own(na), fo * own(am_ref[at, :].astype(F32)))):
                value = jnp.where(inside, value, 0.0)
                sums_ref[0, k * 8 : (k + 1) * 8, :] += jnp.sum(value.reshape(step // 8, 8, local), 0)
            return carry

        lax.fori_loop(0, BLOCK // step, chunk, 0, unroll=BLOCK // step)

        def project(w_ref):
            gmix_ref[...] = mm(ga_ref[...], w_ref[...], NT).astype(BF)

        @pl.when(i < image_blocks)
        def _():
            project(wi_ref)

        @pl.when(i >= image_blocks)
        def _():
            project(wt_ref)

    return call(
        kernel,
        (pl.cdiv(rows, BLOCK),),
        [rows_spec(half)] * 8 + [whole(mod.shape), whole(wi.shape), whole(wt.shape)],
        [
            rows_spec(width),
            rows_spec(local),
            rows_spec(local),
            pl.BlockSpec((1, 24, local), lambda i, *_: (jnp.where(i < image_blocks, 0, 1), 0, 0)),
        ],
        [
            struct((rows, width), BF),
            struct((rows, local), BF),
            struct((rows, local), F32),
            struct((2, 24, local), F32),
        ],
        2 * rows * width * local,
        rows * width * 12,
        prefetch=2,
    )(ids, live, xm, xo, am, ao, cm, co, gm, go, mod, wi, wt)


def grad_specs(right, tile, height, row_block):
    if right.ndim == 3:
        return (
            pl.BlockSpec((1, height, right.shape[2]), lambda j, *_: (j, row_block, 0)),
            right.shape[0],
            right.shape[2],
        )
    return pl.BlockSpec((height, tile), lambda j, *_: (row_block, j)), right.shape[1] // tile, tile


def grad_out(right, tile, part):
    if right.ndim == 3:
        lead, _, cols = right.shape
        return pl.BlockSpec((1, part, cols), lambda j, *_: (j, 0, 0)), struct((lead, part, cols), BF)
    return (
        pl.BlockSpec((1, part, tile), lambda j, *_: (0, 0, j)),
        struct((1, part, right.shape[1]), BF),
    )


def weight_grad(ids, which, lefts, rights, height, add=None, tile=512):
    part = lefts[0].shape[1] // (1 if which is None else 2)
    n = len(lefts)
    right_spec, steps, _ = grad_specs(rights[0], tile, height, 0)
    narrow = which is not None and part % 128 != 0
    left_spec = pl.BlockSpec(
        (height, 2 * part if narrow else part),
        lambda j, ids_ref: (0, 0 if narrow or which is None else ids_ref[which]),
        pipeline_mode=pl.Buffered(1),
    )
    out_spec, out_shape = grad_out(rights[0], tile, part)
    flat = rights[0].ndim == 2

    def kernel(ids_ref, *refs):
        total = None
        for left_ref, right_ref in zip(refs[:n], refs[n : 2 * n]):
            value = mm(left_ref[...], right_ref[...] if flat else right_ref[0], TN)
            total = value if total is None else total + value
        if narrow:
            total = jnp.where(ids_ref[which] == 0, total[:part], total[part:])
        if add is not None:
            total = total + refs[2 * n][0].astype(F32)
        refs[-1][0] = total.astype(BF)

    more = [] if add is None else [add]
    return call(
        kernel,
        (steps,),
        [left_spec] * n + [right_spec] * n + [out_spec] * len(more),
        out_spec,
        out_shape,
        2 * n * height * part * out_shape.shape[0] * out_shape.shape[2],
        n * height * (part + out_shape.shape[0] * out_shape.shape[2]) * 2,
    )(ids, *lefts, *rights, *more)


def adam(ids, inv_count, moment, near, far):
    _, lead, _, piece, cols = moment.shape
    correct_one = 1.0 - BETA_ONE**STEP
    correct_two = 1.0 - BETA_TWO**STEP

    def kernel(ids_ref, inv_ref, m_ref, near_ref, far_ref, fresh_ref, keep_ref, send_ref):
        t = pl.program_id(0)
        for l in range(lead):
            g = jnp.where(ids_ref[9] == 1, near_ref[l, 0], far_ref[l, 0]).astype(F32) * inv_ref[0]
            first = BETA_ONE * m_ref[0, l, 0] + (1.0 - BETA_ONE) * g
            second = BETA_TWO * m_ref[1, l, 0] + (1.0 - BETA_TWO) * g * g
            fresh_ref[0, l, 0] = first
            fresh_ref[1, l, 0] = second
            update = (first * (1.0 / correct_one) / (jnp.sqrt(second * (1.0 / correct_two)) + ADAM_EPS)).astype(BF)

            @pl.when(t < 2)
            def _(l=l, update=update):
                send_ref[0, l] = update

            @pl.when(t >= 2)
            def _(l=l, update=update):
                keep_ref[0, l] = update

    def block(t, ids_ref):
        return (t % 2) * 2 + jnp.where(t < 2, 1 - ids_ref[0], ids_ref[0])

    pairs = pl.BlockSpec((2, lead, 1, piece, cols), lambda t, ids_ref, _: (0, 0, block(t, ids_ref), 0, 0))
    grad = pl.BlockSpec((lead, 1, piece, cols), lambda t, ids_ref, _: (0, block(t, ids_ref), 0, 0))
    side = struct((2, lead, piece, cols), BF)
    return call(
        kernel,
        (4,),
        [pairs, grad, grad],
        [
            pairs,
            pl.BlockSpec((1, lead, piece, cols), lambda t, *_: (jnp.maximum(t - 2, 0), 0, 0, 0)),
            pl.BlockSpec((1, lead, piece, cols), lambda t, *_: (jnp.minimum(t, 1), 0, 0, 0)),
        ],
        [struct(moment.shape, F32), side, side],
        lead * piece * cols * 80,
        lead * piece * cols * 80,
        prefetch=2,
    )(ids, inv_count, moment, near, far)


def outer_step(ids, state, keep, got, far, groups):
    _, lead, piece, cols = state.shape

    def kernel(ids_ref, s_ref, k_ref, g_ref, f_ref, out_ref):
        near = (k_ref[0].astype(F32) + g_ref[0].astype(F32)).astype(BF).astype(F32)
        total = near + f_ref[...].astype(F32)
        master = s_ref[0]
        delta = LEARN_RATE * (total * (1.0 / groups) + DECAY_RATE * master)
        momentum = OUTER_MOMENT * s_ref[1] + delta
        out_ref[0] = master - OUTER_RATE * (delta + OUTER_MOMENT * momentum)
        out_ref[1] = delta
        out_ref[2] = momentum

    side = pl.BlockSpec((1, lead, piece, cols), lambda i, ids_ref: (ids_ref[2], 0, 0, 0))
    return call(
        kernel,
        (1,),
        [
            pl.BlockSpec((2, lead, piece, cols), lambda i, *_: (0, 0, 0, 0)),
            side,
            side,
            pl.BlockSpec((lead, piece, cols), lambda i, *_: (0, 0, 0)),
        ],
        pl.BlockSpec((3, lead, piece, cols), lambda i, *_: (0, 0, 0, 0)),
        struct((3, lead, piece, cols), F32),
        lead * piece * cols * 10,
        lead * piece * cols * 26,
    )(ids, state, keep, got, far)


def solution(mesh):
    n_group, n_dp, n_mp = mesh.shape["group"], mesh.shape["dp"], mesh.shape["mp"]
    core_perm = [(g, g ^ 1) for g in range(n_group)]
    x_perm = [(g, g ^ 2) for g in range(n_group)]
    z_perm = [(m, m ^ 1) for m in range(n_mp)]
    y_perm = [(d, d ^ 1) for d in range(n_dp)]
    turn_perm = [
        (g * n_mp + m, ((g // 2) * 2 + m // 2) * n_mp + (g % 2) * 2 + m % 2)
        for g in range(n_group)
        for m in range(n_mp)
    ]

    trade_perm = [(i, j if i != j else (i // n_mp ^ 2) * n_mp + i % n_mp) for i, j in turn_perm]

    def core_swap(a):
        return lax.ppermute(a, "group", core_perm)

    def x_swap(a):
        return lax.ppermute(a, "group", x_perm)

    def z_swap(a):
        return lax.ppermute(a, "mp", z_perm)

    def y_swap(a):
        return lax.ppermute(a, "dp", y_perm)

    def turn(a):
        return lax.ppermute(a, ("group", "mp"), turn_perm)

    def trade(a):
        return lax.ppermute(a, ("group", "mp"), trade_perm)

    def by(flag, a, b, axis):
        return jnp.where(flag == 0, jnp.concatenate([a, b], axis), jnp.concatenate([b, a], axis))

    def body(
        image_tokens, text_tokens, image_modulation, text_modulation, image_cotan, text_cotan,
        group_counts, *tensors,
    ):
        states, moments = tensors[:8], tensors[8:]
        g, d, m = lax.axis_index("group"), lax.axis_index("dp"), lax.axis_index("mp")
        c, xc, zl = g % 2, g // 2, m % 2
        place = (d % 2) * 2 + xc
        ids = jnp.stack([c, zl, xc, d % 2, 1 - d % 2, place, place ^ 1, place ^ 2, place ^ 3, c == m // 2]).astype(jnp.int32)

        slots = image_tokens.shape[1]
        image_len, text_len = image_tokens.shape[2], text_tokens.shape[2]
        text_rows = -(-text_len // 32) * 32
        local = image_tokens.shape[3]
        width = local * n_mp
        rows_all = image_len + text_rows
        length = image_len + text_len

        last = []

        def hold(value, others):
            if not others:
                return value
            leaves, tree = jax.tree.flatten(value)
            held = lax.optimization_barrier(tuple(leaves) + tuple(others))
            return jax.tree.unflatten(tree, list(held[: len(leaves)]))

        def step(fn, first, *rest, need=()):
            out = fn(hold(first, last + jax.tree.leaves(need)), *rest)
            last[:] = [jax.tree.leaves(out)[0]]
            return out

        def send(move, value):
            return move(hold(value, last))

        turned, over_x, over_y, over_z = (lambda value, move=move: send(move, value) for move in (turn, x_swap, y_swap, z_swap))
        stays = c == m // 2

        def owned(value):
            return value, send(trade, value)


        def sync(*need):
            if n_dp == 2:
                last.extend(jax.tree.leaves(need))

        def join(tokens):
            image, text = tokens
            return jnp.concatenate([image, jnp.pad(text, ((0, text_rows - text_len), (0, 0)))], 0)

        def mod_join(parts):
            image, text, counts = parts
            rows = jnp.concatenate(
                [
                    image[0].reshape(-1, local),
                    text[0].reshape(-1, local),
                    jnp.broadcast_to(counts[0].astype(F32), (1, local)),
                ],
                0,
            )
            return jnp.pad(rows, ((0, -rows.shape[0] % 8), (0, 0)))

        def lead_form(a):
            return a.transpose(0, 2, 1, 3) if a.ndim == 4 else a[:, None]

        def gather_one(a):
            if n_dp != 2:
                return (lax.all_gather(by(xc, a, over_x(a), 1), "dp", axis=1, tiled=True),)
            return a, over_x(a), over_y(a)

        def corner(parts, stream):
            if len(parts) == 1:
                return parts
            a, px, py = parts
            return a, px, py, (over_x(py) if stream == 0 else over_y(px))

        def assemble(parts, need=()):
            if len(parts) > 1:
                return step(lambda a, *rest: lay_quads(ids, (a,) + rest), *parts, need=need)
            return parts[0]

        def flat(w):
            return w if w.shape[0] > 1 else w[0]

        def z_pair(own):
            got = over_z(own)
            return lambda need=(): with_core(step(lambda a, b: by(zl, a, b, 1), own, got, need=need))

        def with_core(pair):
            return pair, send(core_swap, pair)

        def half_sum(keep, give, need=()):
            got = send(core_swap, give)
            return step(lambda a, b: (a.astype(F32) + b.astype(F32)).astype(BF), keep, got, need=need)

        def half_start(keep, give):
            got = send(core_swap, give)
            return lambda: step(lambda a, b: (a.astype(F32) + b.astype(F32)).astype(BF), keep, got)

        def full_sum(mine, got, need=()):
            return with_core(step(lambda a, b: (a.astype(F32) + b.astype(F32)).astype(BF), mine, got, need=need))

        def own_part(mine):
            away = lax.dynamic_slice_in_dim(mine, (1 - zl) * local, local, 1)
            here = lax.dynamic_slice_in_dim(mine, zl * local, local, 1)
            return here, over_z(away)

        def own_sum(here, got):
            return (here.astype(F32) + got.astype(F32)).astype(BF).astype(F32)

        def column_sums(a):
            return jnp.stack([jnp.sum(a[:image_len], 0), jnp.sum(a[image_len:], 0)])

        def per_row(index, s):
            return jnp.concatenate(
                [
                    jnp.broadcast_to(mod_own[s * 6 + index], (image_len, local)),
                    jnp.broadcast_to(mod_own[(slots + s) * 6 + index], (text_rows, local)),
                ],
                0,
            )

        places = [(image_len, s * 6, (slots + s) * 6) for s in range(slots)]

        def first_part(s, need=()):
            return step(lambda a, b: ln_qkv(ids, a, b, mod_full, *wq, *places[s]), *xs[s], need=need)

        def mixing(s, need=()):
            return step(lambda a: attend(a, length, image_len), firsts[s][1], need=need)

        def projection(s, need=()):
            keep, give = step(lambda a: out_project(ids, a, *wo, image_len), lses[s][0], need=need)
            mine = half_sum(keep, give)
            return mine, over_z(mine)

        def middle(s, need=()):
            return step(
                lambda a, b: mid_prepare(ids, lives[s].reshape(1), a, b, *atts[s], *cs[s], mod_full, *places[s]),
                *xs[s],
                need=need,
            )

        def dense(s):
            return step(lambda a, b: mlp(ids, a, b, *w1, *w2, image_len), mids[s][0], mids[s][1])

        def text_of(arrays):
            return jnp.concatenate([a[..., image_len:, :] for a in arrays], arrays[0].ndim - 2)

        lead_states = [lead_form(a) for a in states]
        mine = step(lambda a, b: cast_states((a, b)), lead_states[0], lead_states[4])
        got = send(core_swap, mine)
        rest_order = (1, 5, 2, 6, 7, 3)
        rest = step(lambda *a: cast_states(a), *(lead_states[i] for i in rest_order))
        rows_of = [a.shape[2] for a in lead_states]
        def pair_start(own):
            got = over_z(own)
            return lambda: step(lambda a, b: by(zl, a, b, 1), own, got), got

        pairs = dict(zip((0, 4), step(lambda a, b: pair_pieces(ids, a, b, [[(3, rows_of[0])]] * 2), mine, got)))
        pairs = {i: turned(a) for i, a in pairs.items()}
        rest_got = send(core_swap, rest)
        pieces = step(
            lambda a, b: pair_pieces(
                ids, a, b, [[(1, rows_of[1])] * 2] + [[(1, rows_of[i])] for i in (2, 6, 7, 3)]
            ),
            rest, rest_got,
        )
        pieces = dict(zip((1, 2, 6, 7, 3), pieces))
        x_in = [join((image_tokens[0, s], text_tokens[0, s])) for s in range(slots)]
        c_in = [join((image_cotan[0, s], text_cotan[0, s])) for s in range(slots)]
        sync(pairs[0])
        quads = [gather_one(pairs[0])]
        x_own = [turned(x_in[0])]
        sync(pairs[4], quads[0])
        quads.append(gather_one(pairs[4]))
        mod_own = turned(mod_join((image_modulation, text_modulation, group_counts)))
        count = mod_own[slots * 12, 0]
        lives = [(s * n_dp + d < count).astype(F32) for s in range(slots)]
        sync(quads[1], x_own[0], mod_own)
        x_pair, x_got = pair_start(x_own[0])
        quads = [corner(a, s) for s, a in enumerate(quads)]
        mod_pair, mod_got = pair_start(mod_own)
        pairs[1] = turned(pieces[1])
        sync(quads, x_got, mod_got)
        xs = [with_core(x_pair())]
        mod_pair = with_core(mod_pair())
        sync(pairs[1])
        outs = gather_one(pairs[1]) if n_dp == 2 else None
        pairs[2] = turned(pieces[2])
        wq = [assemble(a) for a in quads]
        mod_full = jnp.concatenate(mod_pair, 1)
        firsts = [first_part(0)]
        sync(outs if n_dp == 2 else (), pairs[2])
        if n_dp == 2:
            outs = [corner(tuple(a[s : s + 1] for a in outs), s) for s in range(2)]
        else:
            outs = [gather_one(pairs[1][s : s + 1]) for s in range(2)]
        pairs[6] = turned(pieces[6])
        sync(outs)
        expand = [gather_one(pairs[2])]
        x_own += [turned(a) for a in x_in[1:]]
        wo = [flat(assemble(a)) for a in outs]
        lses = [mixing(0)]
        keep, give = step(lambda a: out_project(ids, a, *wo, image_len), lses[0][0])
        sync(expand[0], pairs[6], x_own)
        half = half_start(keep, give)
        expand.append(gather_one(pairs[6]))
        pairs[7] = turned(pieces[7])
        more_x = [pair_start(x_own[s]) for s in range(1, slots)]
        mine = half()
        sync(expand[1], pairs[7], [a[1] for a in more_x])
        expand = [corner(a, e) for e, a in enumerate(expand)]
        pairs[3] = turned(pieces[3])
        xs += [with_core(a[0]()) for a in more_x]
        sums = [(mine, over_z(mine))]
        atts, mids, mlps, c_own = [], [], [], []
        for s in range(1, slots):
            firsts.append(first_part(s))
            if s == 1:
                sync(expand, pairs[3])
                reduce = [None, gather_one(pairs[7])]
                c_own.append(turned(c_in[0]))
                w1 = [flat(assemble(a)) for a in expand]
            lses.append(mixing(s))
            if s == 1:
                sync(reduce[1], c_own[0], sums[0])
                reduce[0] = gather_one(pairs[3])
                cots = [pair_start(c_own[0])]
                c_own += [turned(a) for a in c_in[1:]]
            keep, give = step(lambda a: out_project(ids, a, *wo, image_len), lses[s][0])
            half = half_start(keep, give)
            atts.append(full_sum(*sums[s - 1]))
            mine = half()
            if s == 1:
                sync(reduce[0], cots[0][1])
                reduce = [corner(a, e) for e, a in enumerate(reduce)]
                cs = [with_core(cots[0][0]())]
            sums.append((mine, over_z(mine)))
        mids.append(middle(0))
        sync(reduce, c_own)
        cots += [pair_start(c_own[s]) for s in range(1, slots)]
        w2 = [flat(assemble(a)) for a in reduce]

        lefts_text, rights_text = {}, {}

        def text_left(k):
            def halves(a):
                part = a.shape[1] // 2
                return (
                    lax.dynamic_slice_in_dim(a, d * part, part, 1),
                    lax.dynamic_slice_in_dim(a, (1 - d) * part, part, 1),
                )

            mine, away = step(halves, lefts_text[k])
            return mine, over_y(away)

        def text_right(k):
            return rights_text[k], over_y(rights_text[k])

        def text_grad(k):
            def product(left, left_got, right, right_got):
                return weight_grad(ids, None, [left, left_got], [right, right_got], slots * text_rows)

            return owned(step(product, *text_lefts[k], *text_rights[k]))

        def give_later(k, right=None, stream=0):
            left, rights_now, height = ((lefts, rights, image_len), (lefts_text, rights_text, slots * text_rows))[stream]
            right = rights_now[k] if right is None else right
            left, right = (a if isinstance(a, list) else [a] for a in (left[k], right))
            return step(lambda a: weight_grad(ids, 4, a, right, height), left)

        def keep_half(k, got, stream=0, need=()):
            left, right, height = ((lefts, rights, image_len), (lefts_text, rights_text, slots * text_rows))[stream]
            left, right = (a[k] if isinstance(a[k], list) else [a[k]] for a in (left, right))
            return owned(step(lambda a: weight_grad(ids, 3, a, right, height, got), left, need=need))

        def whole_grads(k):
            def one(left, right):
                if right.ndim == 3:
                    return jnp.einsum("td,ctf->cdf", left, right, preferred_element_type=F32)
                return mm(left, right, TN)[None]

            image = sum(one(a[:image_len], b[..., :image_len, :]) for a, b in zip(lefts[k], rights[k]))
            text = one(lefts_text[k], rights_text[k])
            return [
                owned(lax.psum_scatter(a.astype(BF), "dp", scatter_dimension=1, tiled=True)) for a in (image, text)
            ]

        two_way = n_dp == 2
        sent, text_lefts, text_rights, grads = {}, {}, {}, {}
        lefts, rights, backs, gqkvs, gh1_mine, branch_mine = {}, {}, [], [], [], []

        def backward(s, need=()):
            backs.append(
                step(
                    lambda a, b: back_prepare(
                        ids, lives[s].reshape(1), a, b, *atts[s], *cs[s], *gh2s[s], mod_full, *wo, *places[s]
                    ),
                    *xs[s],
                    need=need,
                )
            )

        def unmix(s, need=()):
            gqkvs.append(
                step(
                    lambda a, b: attend_back(a, b, lses[s][1], length, image_len),
                    firsts[s][1], backs[s][1],
                    need=need,
                )
            )

        def to_input(s, need=()):
            out = step(lambda a: input_partial(ids, a, *wq, image_len), gqkvs[s], need=need)
            gh1_mine.append(own_part(half_sum(*out)))

        def to_branch(s):
            branch_mine.append(own_part(half_sum(mlps[s][2], mlps[s][3])))

        results, grads_x, modgrads, gates = [], [], [], []

        def row_results(s):
            def first(here, got):
                branch = own_sum(here, got)
                res = (mids[s][2] + per_row(5, s) * branch).astype(BF)
                return res, column_sums(c_own[s].astype(F32) * lives[s] * branch)

            res, gate = step(first, *branch_mine[s])
            gates.append(gate)
            return res

        def row_sums(s):
            _, _, n1o, _ = firsts[s]

            def first(here, got):
                gh1 = own_sum(here, got)
                q = gh1 * (1.0 + per_row(1, s))
                total = jnp.stack([jnp.sum(q, 1), jnp.sum(q * n1o, 1)])
                sums = jnp.sum(backs[s][3].reshape(2, 3, 8, local), 2)
                mods = jnp.stack(
                    [column_sums(gh1), column_sums(gh1 * n1o), sums[:, 2], sums[:, 0], sums[:, 1], gates[s]]
                )
                return total, mods

            total, mods = step(first, *gh1_mine[s])
            modgrads.append(mods)
            return total, over_z(total)

        def row_total(total, got):
            total = step(jnp.add, total, got)
            return total, send(core_swap, total)

        def row_grads(s, total, got):
            _, _, n1o, inv1 = firsts[s]

            def second(total, got, here, away):
                total = (total + got) / width
                q = own_sum(here, away) * (1.0 + per_row(1, s))
                gx = backs[s][2] + inv1[:, :1] * (q - total[0][:, None] - n1o * total[1][:, None])
                return gx.astype(BF)

            grads_x.append(owned(step(second, total, got, *gh1_mine[s])))

        fresh, outer, waiting = [None] * 8, [None] * 8, {}
        inv_count = (1.0 / group_counts[0].astype(F32)).reshape(1)

        updates = {}

        def optimize(idx):
            moment = lead_form(moments[idx][0])
            lead, rows, cols = moment.shape[1:]
            piece = rows // n_group
            new, keep, give = step(
                lambda near, far: adam(ids, inv_count, moment.reshape(2, lead, n_group, piece, cols), near, far),
                *(a.reshape(lead, n_group, piece, cols) for a in grads[idx]),
            )
            updates[idx] = keep, give
            new = new.reshape(2, lead, rows, cols)
            fresh[idx] = new.transpose(0, 2, 1, 3)[None] if moments[idx].ndim == 5 else new[:, 0][None]

        def send_update(idx):
            updates[idx] = updates[idx][0], send(core_swap, updates[idx][1])

        def finish(idx):
            keep, got = updates[idx]
            out = step(
                lambda a: outer_step(ids, lead_form(states[idx]), keep, got, a, n_group), waiting[idx]
            )
            outer[idx] = out.transpose(0, 2, 1, 3) if moments[idx].ndim == 5 else out[:, 0]

        def fill_dense():
            lefts.update({3: [a[0] for a in mlps], 2: [a[0] for a in mids], 1: [a[0] for a in lses], 0: [a[0] for a in firsts]})
            rights.update({3: [a[1] for a in mids], 2: [a[1] for a in mlps]})

        def fill_mixing():
            rights[1] = [a[0] for a in backs]
            rights[0] = gqkvs
            rights_text[0] = step(text_of, gqkvs)
            lefts_text[1] = step(text_of, [a[0] for a in lses])
            rights_text[1] = step(text_of, rights[1])

        def fill_text(k):
            lefts_text[k] = step(text_of, lefts[k])
            rights_text[k] = step(text_of, rights[k])

        mlps.append(dense(0))
        sync(sums[-1], [a[1] for a in cots])
        gh_sums = []

        def gh_half(s):
            mine = half_sum(mlps[s][4], mlps[s][5])
            gh_sums.append((mine, over_z(mine)))

        def small_sum(idx):
            keep, got = updates[idx]
            pick = lambda a: lax.dynamic_index_in_dim(a, 1 - xc, 0, False)
            far = over_x(
                step(lambda a, b: (pick(a).astype(F32) + pick(b).astype(F32)).astype(BF), keep, got)
            )
            waiting[idx] = far

        if two_way and slots == 2:
            gh = half_start(mlps[0][4], mlps[0][5])
            atts.append(full_sum(*sums[1]))
            cs.append(with_core(cots[1][0]()))
            mine = gh()
            gh_sums.append((mine, over_z(mine)))
            mids.append(middle(1))
            lefts_text[0] = step(text_of, [a[0] for a in firsts])
            text_lefts[0] = text_left(0)
            mlps.append(dense(1))
            sync(gh_sums[0], text_lefts[0])
            gh = half_start(mlps[1][4], mlps[1][5])
            gh2s = [full_sum(*gh_sums[0])]
            fill_dense()
            fill_text(3)
            text_lefts[3] = text_left(3)
            text_rights[3] = text_right(3)
            mine = gh()
            gh_sums.append((mine, over_z(mine)))
            backward(0)
            sent_three = give_later(3)
            sent_two = give_later(2)
            fill_text(2)
            sync(text_lefts[3], text_rights[3], gh_sums[1])
            gh2s.append(full_sum(*gh_sums[1]))
            br = [half_start(mlps[s][2], mlps[s][3]) for s in range(2)]
            grads[7] = text_grad(3)
            text_rights[2] = text_right(2)
            text_lefts[2] = text_left(2)
            br = [a() for a in br]
            branch_mine.append(own_part(br[0]))
            unmix(0)
            sync(grads[7], text_rights[2], text_lefts[2], branch_mine[0])
            sent[3] = over_y(sent_three)
            grads[6] = text_grad(2)
            branch_mine.append(own_part(br[1]))
            res = [row_results(0)]
            backward(1)
            out = step(lambda a: input_partial(ids, a, *wq, image_len), gqkvs[0])
            optimize(7)
            sync(sent[3], branch_mine[1])
            grads[3] = keep_half(3, sent[3])
            sync(grads[6])
            half = half_start(*out)
            send_update(7)
            gh1_mine.append(own_part(half()))
            small_sum(7)
            sent[2] = over_y(sent_two)
            unmix(1)
            sync(grads[3], gh1_mine[0], waiting[7], sent[2])
            grads[2] = keep_half(2, sent[2])
            results.append(owned(res[0]))
            totals = [row_sums(0)]
            sent_zero = give_later(0, gqkvs)
            out = step(lambda a: input_partial(ids, a, *wq, image_len), gqkvs[1])
            finish(7)
            res.append(row_results(1))
            fill_mixing()
            text_rights[0] = text_right(0)
            optimize(6)
            sync(grads[2], totals[0], text_rights[0])
            half = half_start(*out)
            send_update(6)
            totals[0] = row_total(*totals[0])
            grads[4] = text_grad(0)
            sent[0] = over_y(sent_zero)
            gh1_mine.append(own_part(half()))
            small_sum(6)
            row_grads(0, *totals[0])
            optimize(3)
            sent_text, sent_one = give_later(1, None, 1), give_later(1)
            sync(grads[4], gh1_mine[1], waiting[6], sent[0], results[0])
            send_update(3)
            grads[0] = keep_half(0, sent[0])
            totals.append(row_sums(1))
            sent[5], sent[1] = over_y(sent_text), over_y(sent_one)
            small_sum(3)
            finish(6)
            optimize(2)
            sync(totals[1], sent[5], sent[1], grads_x[0])
            grads[5] = keep_half(1, sent[5], 1)
            grads[1] = keep_half(1, sent[1])
            optimize(4)
            sync(grads[0], waiting[3], grads[5], grads[1])
            totals[1] = row_total(*totals[1])
            send_update(2)
            send_update(4)
            finish(3)
            small_sum(2)
            small_sum(4)
            results.append(owned(res[1]))
            row_grads(1, *totals[1])
            optimize(0)
            optimize(5)
            optimize(1)
            sync(waiting[2], waiting[4], results[1])
            send_update(0)
            send_update(5)
            send_update(1)
            small_sum(0)
            small_sum(5)
            small_sum(1)
            finish(2)
            finish(4)
            sync(waiting[0], waiting[5], waiting[1])
            for i in (0, 5, 1):
                finish(i)
        else:
            for s in range(1, slots):
                if len(atts) == s:
                    atts.append(full_sum(*sums[s]))
                cs.append(with_core(cots[s][0]()))
                mids.append(middle(s))
                mlps.append(dense(s))
            fill_dense()
            for s in range(slots):
                gh_half(s)
            gh2s = [full_sum(*a) for a in gh_sums]
            for s in range(slots):
                backward(s)
                unmix(s)
                to_input(s)
                to_branch(s)
                results.append(owned(row_results(s)))
                row_grads(s, *row_total(*row_sums(s)))
            fill_mixing()
            lefts_text[0] = step(text_of, lefts[0])
            fill_text(2)
            fill_text(3)
            for k in (3, 2, 1, 0):
                grads[k], grads[k + 4] = whole_grads(k)
            for i in range(8):
                optimize(i)
                send_update(i)
                small_sum(i)
                finish(i)
        mod_back = turn(jnp.stack(modgrads).reshape(slots * 12, local)).reshape(slots, 6, 2, local)

        res, gx = (jnp.stack([jnp.where(stays, a, b) for a, b in pairs]) for pairs in (results, grads_x))
        return (
            res[None, :, :image_len],
            res[None, :, image_len:length],
            gx[None, :, :image_len],
            gx[None, :, image_len:length],
            mod_back[None, :, :, 0],
            mod_back[None, :, :, 1],
            *fresh,
            *outer,
        )

    tokens = P("group", "dp", None, "mp")
    weight_specs = (
        P(None, ("dp", "group"), None, "mp"),
        P(None, ("mp", "dp", "group"), None),
        P(None, ("dp", "group"), "mp"),
        P(None, ("mp", "dp", "group"), None),
    ) * 2
    moment_specs = (
        P("group", None, "dp", None, "mp"),
        P("group", None, ("mp", "dp"), None),
        P("group", None, "dp", "mp"),
        P("group", None, ("mp", "dp"), None),
    ) * 2
    return jax.shard_map(
        body,
        mesh=mesh,
        in_specs=(tokens,) * 6 + (P("group"),) + weight_specs + moment_specs,
        out_specs=(tokens,) * 6 + moment_specs + weight_specs,
        check_vma=False,
    )
```
